256 devices in a mesh: vol: 16 (over y_hi, x, core), surf: 16 (over z, y_lo).
Axes of the slice: x: 4, y: 4 (y_hi: 2, y_lo: 2; y = y_hi * 2 + y_lo), z: 8, core: 2. Of those that a mesh axis runs over, the one named last changes fastest.
Arguments:
- surface_points: float32 [3, 131072], P(None, ('vol', 'surf')), may hold values from -3 to 11
- surface_shift: float32 [3, 131072], P(None, ('vol', 'surf')), may hold values from -1.25 to 1.25
- facet_nodes: int32 [512, 3, 512], P(('vol', 'surf')), may hold values from 0 to 255, as said below
- volume_points: float32 [3, 131072], P(None, 'vol'), may hold values from -5 to 13
- near_wall: int32 [131072], P('vol'), may hold values from 0 to 1
- candidates: int32 [1024, 16], P('vol'), may hold values from -1 to 511, as said below
Outputs:
- displacement: float32 [3, 131072], P(None, ('vol', 'surf'))
- wall_distance: float32 [131072], P(('vol', 'surf'))
The draws below stay inside these ranges and needn't reach their ends.
Inputs may be any that keep to these rules, and one draw needn't show every extreme that they name: Corner k of facet f of leaf l is surface node l * 256 + facet_nodes[l, k, f]; the three corners of a facet are distinct nodes of that leaf. `candidates`: in each row the real leaf ids come first, are distinct, and -1 fills the rest; every row holds at least one real id.
All inputs are finite; a program needn't handle non-finite values.
Results may differ from the reference program's by a relative error of at most 0.0003.
Values sent between devices are 32-bit elements; how exact they have to be, the bound alone decides.
A program may use at most 64 MiB of HBM per device.

```python
import math
import jax
import jax.numpy as jnp
import numpy as np
from jax import lax

LEAF = 256
FL = 512
VB = 128
CAND = 16
LEAF_DEV = 2
V_DEV = 8192
LEAVES = 512
VNODES = 131072
VBLOCKS = 1024


spacing = 0.1


def leaf_slots(key):
    perm_key = jax.random.fold_in(key, 101)
    leaf_keys = jax.random.split(perm_key, LEAVES)
    return jax.vmap(lambda leaf_key: jax.random.permutation(leaf_key, LEAF))(leaf_keys)


def grid_triangles():
    grid_side = math.isqrt(LEAF)
    columns = []
    for row_pos in range(grid_side - 1):
        for col_pos in range(grid_side - 1):
            corner_one = row_pos * grid_side + col_pos
            corner_two = corner_one + grid_side
            corner_three = corner_two + 1
            corner_four = corner_one + 1
            columns.append([corner_one, corner_two, corner_three])
            columns.append([corner_one, corner_three, corner_four])
    return np.array(columns, dtype=np.int32).T


def draw_facet_nodes(key, part):
    slot_of = leaf_slots(key)
    triangles = jnp.asarray(grid_triangles())
    tri_count = triangles.shape[1]
    padding = jax.random.randint(jax.random.fold_in(key, 202), (LEAVES, FL - tri_count), 0, tri_count)
    grid_ids = jnp.concatenate([jnp.broadcast_to(triangles[None], (LEAVES, 3, tri_count)), jnp.transpose(triangles[:, padding], (1, 0, 2))], axis=2)
    slot_table = jnp.broadcast_to(slot_of[:, None, :], (LEAVES, 3, LEAF))
    return jnp.take_along_axis(slot_table, grid_ids, axis=2).astype(jnp.int32)


def leaf_frames(key):
    geo_key = jax.random.fold_in(key, 303)
    key_root, key_frame, key_jitter = jax.random.split(geo_key, 3)
    root = jax.random.uniform(key_root, (LEAVES, 3), jnp.float32, 0.0, 8.0)
    raw_frame = jax.random.normal(key_frame, (LEAVES, 2, 3), jnp.float32)
    tangent_one = raw_frame[:, 0] / jnp.sqrt(jnp.sum(raw_frame[:, 0] ** 2, axis=1, keepdims=True))
    second_raw = raw_frame[:, 1] - jnp.sum(raw_frame[:, 1] * tangent_one, axis=1, keepdims=True) * tangent_one
    tangent_two = second_raw / jnp.sqrt(jnp.sum(second_raw ** 2, axis=1, keepdims=True))
    normal = jnp.cross(tangent_one, tangent_two)
    return (root, tangent_one, tangent_two, normal, key_jitter)


def candidate_table(key):
    cand_key = jax.random.fold_in(key, 606)
    key_count, key_start, key_coin, key_noise, key_anchor = jax.random.split(cand_key, 5)
    real_count = jax.random.randint(key_count, (VBLOCKS,), 1, CAND + 1)
    popular_start = jax.random.randint(key_start, (), 0, LEAVES)
    leaf_ids = jnp.arange(LEAVES, dtype=jnp.int32)
    in_window = (leaf_ids - popular_start) % LEAVES < 2 * LEAF_DEV
    popular_coin = jax.random.randint(key_coin, (VBLOCKS, LEAVES), 0, 10) < 5
    noise_draw = jax.random.randint(key_noise, (VBLOCKS, LEAVES), 0, 262144)
    boost_add = jnp.where(in_window[None, :] & popular_coin, 262144, 0)
    scores = (noise_draw + boost_add) * LEAVES + leaf_ids[None, :]
    top_values, top_ids = lax.top_k(scores, CAND)
    slot_ids = jnp.arange(CAND)[None, :]
    cand_table = jnp.where(slot_ids < real_count[:, None], top_ids, -1).astype(jnp.int32)
    anchor_slot = jax.random.randint(key_anchor, (VBLOCKS,), 0, 1048576) % real_count
    anchor_leaf = jnp.take_along_axis(top_ids, anchor_slot[:, None], axis=1)[:, 0].astype(jnp.int32)
    return (cand_table, anchor_leaf)


def draw_surface_points(key, part):
    slot_of = leaf_slots(key)
    root, tangent_one, tangent_two, normal, key_jitter = leaf_frames(key)
    grid_side = math.isqrt(LEAF)
    node_ids = jnp.arange(LEAF)
    along_one = (node_ids // grid_side).astype(jnp.float32) * spacing
    along_two = (node_ids % grid_side).astype(jnp.float32) * spacing
    jitter = jax.random.uniform(key_jitter, (LEAVES, LEAF, 3), jnp.float32, -0.05 * spacing, 0.05 * spacing)
    grid_pos = root[:, None, :] + along_one[None, :, None] * tangent_one[:, None, :] + along_two[None, :, None] * tangent_two[:, None, :] + jitter
    inverse = jnp.argsort(slot_of, axis=1)
    slot_pos = jnp.take_along_axis(grid_pos, jnp.broadcast_to(inverse[:, :, None], (LEAVES, LEAF, 3)), axis=1)
    return jnp.transpose(slot_pos.reshape(LEAVES * LEAF, 3)).astype(jnp.float32)


def draw_surface_shift(key, part):
    slot_of = leaf_slots(key)
    shift_key = jax.random.fold_in(key, 404)
    key_move, key_jitter, key_bend = jax.random.split(shift_key, 3)
    leaf_move = jnp.clip(0.4 * jax.random.normal(key_move, (LEAVES, 3), jnp.float32), -0.7, 0.7)
    bend = jax.random.uniform(key_bend, (LEAVES, 2, 3), jnp.float32, -1.0, 1.0)
    grid_side = math.isqrt(LEAF)
    node_ids = jnp.arange(LEAF)
    frac_one = (node_ids // grid_side).astype(jnp.float32) / (grid_side - 1) - 0.5
    frac_two = (node_ids % grid_side).astype(jnp.float32) / (grid_side - 1) - 0.5
    linear = 0.3 * (frac_one[None, :, None] * bend[:, 0][:, None, :] + frac_two[None, :, None] * bend[:, 1][:, None, :])
    rough = jax.random.uniform(key_jitter, (LEAVES, LEAF, 3), jnp.float32, -0.1, 0.1)
    grid_move = leaf_move[:, None, :] + linear + rough
    inverse = jnp.argsort(slot_of, axis=1)
    slot_move = jnp.take_along_axis(grid_move, jnp.broadcast_to(inverse[:, :, None], (LEAVES, LEAF, 3)), axis=1)
    return jnp.transpose(slot_move.reshape(LEAVES * LEAF, 3)).astype(jnp.float32)


def draw_volume_points(key, part):
    root, tangent_one, tangent_two, normal, key_jitter = leaf_frames(key)
    cand_table, anchor_leaf = candidate_table(key)
    place_key = jax.random.fold_in(key, 707)
    key_one, key_two, key_three = jax.random.split(place_key, 3)
    extent = (math.isqrt(LEAF) - 1) * spacing
    along_one = jax.random.uniform(key_one, (VBLOCKS, VB, 1), jnp.float32, 0.0, extent)
    along_two = jax.random.uniform(key_two, (VBLOCKS, VB, 1), jnp.float32, 0.0, extent)
    height = jax.random.uniform(key_three, (VBLOCKS, VB, 1), jnp.float32, 0.05, 4.0)
    anchor_base = root[anchor_leaf][:, None, :]
    node_pos = anchor_base + along_one * tangent_one[anchor_leaf][:, None, :] + along_two * tangent_two[anchor_leaf][:, None, :] + height * normal[anchor_leaf][:, None, :]
    return jnp.transpose(node_pos.reshape(VNODES, 3)).astype(jnp.float32)


def draw_near_wall(key, part):
    flag_key = jax.random.fold_in(key, 505)
    key_level, key_block, key_node = jax.random.split(flag_key, 3)
    vol_count = VNODES // V_DEV
    blocks_dev = V_DEV // VB
    near_level = jax.random.randint(key_level, (vol_count,), 2, 7)
    block_draw = jax.random.randint(key_block, (VBLOCKS,), 0, 20)
    block_ids = jnp.arange(VBLOCKS)
    owner_dev = block_ids // blocks_dev
    first_half = block_ids % blocks_dev < blocks_dev // 2
    threshold = jnp.where(first_half, 3 * near_level[owner_dev], near_level[owner_dev])
    block_near = block_draw < threshold
    node_pick = jax.random.randint(key_node, (VNODES,), 0, 4) < 3
    return (jnp.repeat(block_near, VB) & node_pick).astype(jnp.int32)


def draw_candidates(key, part):
    cand_table, anchor_leaf = candidate_table(key)
    return cand_table


def setup_inputs(seed: int = 0) -> dict:
    streams_of = jax.random.split(jax.random.key(seed), 7)
    surface_points = draw_surface_points(jax.random.fold_in(streams_of[6], 71), 0)
    surface_shift = draw_surface_shift(jax.random.fold_in(streams_of[6], 71), 0)
    facet_nodes = draw_facet_nodes(jax.random.fold_in(streams_of[6], 71), 0)
    volume_points = draw_volume_points(jax.random.fold_in(streams_of[6], 71), 0)
    near_wall = draw_near_wall(jax.random.fold_in(streams_of[6], 71), 0)
    candidates = draw_candidates(jax.random.fold_in(streams_of[6], 71), 0)
    return dict(surface_points=surface_points, surface_shift=surface_shift, facet_nodes=facet_nodes, volume_points=volume_points, near_wall=near_wall, candidates=candidates)


smoothing = 0.01
big_value = 1e+30

def minus3(first_vec, second_vec):
    return [first_vec[0] - second_vec[0], first_vec[1] - second_vec[1], first_vec[2] - second_vec[2]]

def dot3(first_vec, second_vec):
    return first_vec[0] * second_vec[0] + first_vec[1] * second_vec[1] + first_vec[2] * second_vec[2]

def cross3(first_vec, second_vec):
    return [first_vec[1] * second_vec[2] - first_vec[2] * second_vec[1], first_vec[2] * second_vec[0] - first_vec[0] * second_vec[2], first_vec[0] * second_vec[1] - first_vec[1] * second_vec[0]]

def segment_squares(offset_vec, edge_vec, inverse_length):
    fraction = jnp.clip(dot3(offset_vec, edge_vec) * inverse_length, 0.0, 1.0)
    remain = [offset_vec[0] - fraction * edge_vec[0], offset_vec[1] - fraction * edge_vec[1], offset_vec[2] - fraction * edge_vec[2]]
    return dot3(remain, remain)

def facet_squares(points, corners):
    probe_point = [points[..., 0, :, None], points[..., 1, :, None], points[..., 2, :, None]]
    vert_a = [corners[..., 0, None, :], corners[..., 1, None, :], corners[..., 2, None, :]]
    vert_b = [corners[..., 3, None, :], corners[..., 4, None, :], corners[..., 5, None, :]]
    vert_c = [corners[..., 6, None, :], corners[..., 7, None, :], corners[..., 8, None, :]]
    edge_ab = minus3(vert_b, vert_a)
    edge_bc = minus3(vert_c, vert_b)
    edge_ca = minus3(vert_a, vert_c)
    normal = cross3(edge_ab, minus3(vert_c, vert_a))
    inverse_normal = 1.0 / dot3(normal, normal)
    side_ab = cross3(normal, edge_ab)
    side_bc = cross3(normal, edge_bc)
    side_ca = cross3(normal, edge_ca)
    from_a = minus3(probe_point, vert_a)
    from_b = minus3(probe_point, vert_b)
    from_c = minus3(probe_point, vert_c)
    inside = (dot3(from_a, side_ab) >= 0.0) & (dot3(from_b, side_bc) >= 0.0) & (dot3(from_c, side_ca) >= 0.0)
    height = dot3(from_a, normal)
    plane_sq = height * height * inverse_normal
    edge_sq = jnp.minimum(segment_squares(from_a, edge_ab, 1.0 / dot3(edge_ab, edge_ab)), segment_squares(from_b, edge_bc, 1.0 / dot3(edge_bc, edge_bc)))
    edge_sq = jnp.minimum(edge_sq, segment_squares(from_c, edge_ca, 1.0 / dot3(edge_ca, edge_ca)))
    return jnp.where(inside, plane_sq, edge_sq)

def inverse_square(points, others):
    distance_sq = (others[..., 0, :, None] - points[..., 0, None, :]) ** 2
    distance_sq = distance_sq + (others[..., 1, :, None] - points[..., 1, None, :]) ** 2
    distance_sq = distance_sq + (others[..., 2, :, None] - points[..., 2, None, :]) ** 2
    inverse = 1.0 / (distance_sq + smoothing)
    return inverse * inverse

def weigh_sums(weight, shift):
    return jnp.stack([lax.optimization_barrier(jnp.sum(weight * shift[..., 0, :, None], axis=-2)), lax.optimization_barrier(jnp.sum(weight * shift[..., 1, :, None], axis=-2)), lax.optimization_barrier(jnp.sum(weight * shift[..., 2, :, None], axis=-2)), lax.optimization_barrier(jnp.sum(weight, axis=-2))], axis=-2)

def corner_table(moved_nodes, facet_nodes):
    leaves = facet_nodes.shape[0]
    per_leaf = jnp.moveaxis(moved_nodes.reshape(3, leaves, -1), 1, 0)
    pieces = []
    for corner in range(3):
        gather_index = jnp.broadcast_to(facet_nodes[:, corner:corner + 1, :], (leaves, 3, facet_nodes.shape[2]))
        pieces.append(jnp.take_along_axis(per_leaf, gather_index, axis=2))
    return jnp.concatenate(pieces, axis=1)

def reference(surface_points, surface_shift, facet_nodes, volume_points, near_wall, candidates):
    leaves = facet_nodes.shape[0]
    leaf_len = surface_points.shape[1] // leaves
    total_vol = volume_points.shape[1]
    block_len = total_vol // candidates.shape[0]
    leaf_points = jnp.moveaxis(surface_points.reshape(3, leaves, leaf_len), 1, 0)
    leaf_shift = jnp.moveaxis(surface_shift.reshape(3, leaves, leaf_len), 1, 0)
    centers = jnp.transpose(lax.optimization_barrier(jnp.mean(leaf_points, axis=2)))
    center_shift = jnp.transpose(lax.optimization_barrier(jnp.mean(leaf_shift, axis=2)))
    leaf_ids = jnp.arange(leaves, dtype=jnp.int32)
    block_points = jnp.moveaxis(volume_points.reshape(3, -1, block_len), 1, 0)

    def weigh(packed):
        points_here, cands_here = packed
        safe_rows = jnp.maximum(cands_here, 0).astype(jnp.int32)
        near_weight = inverse_square(points_here[None], leaf_points[safe_rows])
        near_terms = weigh_sums(near_weight, leaf_shift[safe_rows])
        near_part = lax.optimization_barrier(jnp.sum(jnp.where((cands_here >= 0)[:, None, None], near_terms, 0.0), axis=0))
        listed = jnp.any(cands_here[:, None] == leaf_ids[None, :], axis=0)
        far_weight = inverse_square(points_here, centers) * leaf_len
        far_weight = jnp.where(listed[:, None], 0.0, far_weight)
        far_part = weigh_sums(far_weight, center_shift)
        return near_part + far_part
    weighted = lax.map(weigh, (block_points, candidates))
    weighted = jnp.moveaxis(weighted, 0, 1).reshape(4, total_vol)
    displacement = weighted[:3] / weighted[3:4]
    moved_volume = volume_points + displacement
    moved_surface = surface_points + surface_shift
    leaf_table = corner_table(moved_surface, facet_nodes)
    moved_blocks = jnp.moveaxis(moved_volume.reshape(3, -1, block_len), 1, 0)
    flag_blocks = near_wall.reshape(-1, block_len)

    def one_block(packed):
        points_here, flags_here, cands_here = packed

        def compute(unused_arg):
            corners = leaf_table[jnp.maximum(cands_here, 0)]
            squared = facet_squares(points_here[None], corners)
            squared = jnp.where(cands_here[:, None, None] >= 0, squared, big_value)
            return lax.optimization_barrier(jnp.min(squared, axis=(0, 2)))

        def skipped(unused_arg):
            return jnp.full((block_len,), big_value, jnp.float32)
        return lax.cond(jnp.max(flags_here) > 0, compute, skipped, 0)
    nearest = lax.map(one_block, (moved_blocks, flag_blocks, candidates)).reshape(-1)
    wall_distance = jnp.where(near_wall == 1, jnp.sqrt(nearest), 0.0)
    return (displacement, wall_distance)
```

```python
import functools

import jax
import jax.numpy as jnp
from jax import lax
from jax.experimental import pallas as pl
from jax.experimental.pallas import tpu as pltpu
from jax.sharding import PartitionSpec as P

MESH = pl.DeviceIdType.MESH
smoothing = 0.01
big_value = 1e30

NX, NY, NZ = 4, 4, 8
SIZES = {"x": NX, "y": NY, "z": NZ}
ORDERS = (("z", "y", "x"), ("x", "z", "y"), ("y", "x", "z"))
LEAF = 256
CHIPS = NX * NY * NZ
LEAVES = 4 * CHIPS
LANES = 128


def coords_of(vol, surf):
    return {
        "x": (vol // 2) % NX,
        "y": (vol // (2 * NX)) * 2 + surf % 2,
        "z": surf // 2,
        "c": vol % 2,
    }


def mesh_id(c):
    return ((c["y"] // 2) * NX + c["x"]) * 2 + c["c"], c["z"] * 2 + c["y"] % 2


def shifted(c, axis, k):
    n = SIZES[axis]
    return {**c, axis: lax.rem(c[axis] + (k % n), n)}


def place(c, order):
    a, b, d = order
    return ((c["c"] * SIZES[d] + c[d]) * SIZES[b] + c[b]) * SIZES[a] + c[a]


def chunk_of(c, order, phase):
    a, b, _ = order
    length = (1, SIZES[a], SIZES[a] * SIZES[b])[phase]
    start = place(c, order)
    return (start // length) * length, length


def gather_kernel(points_ref, shift_ref, facets_ref, table, moments, mom_own, mom_z, mom_y, mom_c,
                  send_sem, recv_sem, core_send, core_recv, mom_send, mom_recv):
    me = coords_of(lax.axis_index("vol"), lax.axis_index("surf"))
    sibling = {**me, "c": 1 - me["c"]}
    partners = [sibling]
    for axis, n in SIZES.items():
        partners += [shifted(me, axis, k) for k in range(1, n)]
    barrier = pltpu.get_barrier_semaphore()
    for other in partners:
        pl.semaphore_signal(barrier, inc=1, device_id=mesh_id(other), device_id_type=MESH)

    own = [place(me, order) * 2 for order in ORDERS]
    for leaf in range(2):
        for half in range(2):
            lanes = pl.ds(leaf * LEAF + half * LANES, LANES)
            for c in range(3):
                table[0, own[0] + leaf, pl.ds(2 * c + half, 1), :] = points_ref[pl.ds(c, 1), lanes]
            table[0, own[0] + leaf, pl.ds(6 + half, 1), :] = shift_ref[pl.ds(0, 1), lanes]
            table[1, own[1] + leaf, pl.ds(0 + half, 1), :] = shift_ref[pl.ds(1, 1), lanes]
            table[1, own[1] + leaf, pl.ds(2 + half, 1), :] = shift_ref[pl.ds(2, 1), lanes]
        for quarter in range(4):
            lanes = pl.ds(quarter * LANES, LANES)
            for k, (part, row) in enumerate(((1, 4), (2, 0), (2, 4))):
                table[part, own[part] + leaf, pl.ds(row + quarter, 1), :] = (
                    facets_ref[leaf, pl.ds(k, 1), lanes].astype(jnp.float32)
                )
    lane = lax.broadcasted_iota(jnp.int32, (3, LANES), 1)
    my_lane = ((me["c"] * NY + me["y"]) * NZ + me["z"]) * 2
    for row, ref in ((0, points_ref), (3, shift_ref)):
        tile = jnp.zeros((3, LANES), jnp.float32)
        for leaf in range(2):
            mean = jnp.sum(ref[:, pl.ds(leaf * LEAF, LEAF)], axis=1, keepdims=True) * (1.0 / LEAF)
            tile = jnp.where(lane == my_lane + leaf, mean, tile)
        mom_own[pl.ds(row, 3), :] = tile
    mom_own[pl.ds(6, 2), :] = jnp.zeros((2, LANES), jnp.float32)
    pl.semaphore_wait(barrier, len(partners))

    sent = []

    def push(part, start, length, to, s_sem, r_sem):
        where = table.at[part, pl.ds(start * 2, length * 2)]
        copy = pltpu.make_async_remote_copy(
            src_ref=where, dst_ref=where, send_sem=s_sem, recv_sem=r_sem,
            device_id=mesh_id(to), device_id_type=MESH,
        )
        copy.start()
        sent.append(copy)

    def arrived(part, start, length, frm, s_sem, r_sem):
        where = table.at[part, pl.ds(start * 2, length * 2)]
        pltpu.make_async_remote_copy(
            src_ref=where, dst_ref=where, send_sem=s_sem, recv_sem=r_sem,
            device_id=mesh_id(frm), device_id_type=MESH,
        ).wait_recv()

    steps = []
    for order in ORDERS:
        steps.append([(ph, s) for ph in range(3) for s in range(1, SIZES[order[ph]] // 2 + 1)])
    core_slot = [0, 0, 0]
    core_in = []

    def to_sibling(part, c, phase, first=0, count=None):
        start, length = chunk_of(c, ORDERS[part], phase)
        theirs, _ = chunk_of({**c, "c": 1 - me["c"]}, ORDERS[part], phase)
        count = length if count is None else count
        slot = core_slot[part]
        core_slot[part] += 1
        push(part, start + first, count, sibling, core_send.at[part, slot], core_recv.at[part, slot])
        core_in.append((part, theirs + first, count, slot))

    def pieces(part, phase, s):
        axis = ORDERS[part][phase]
        n = SIZES[axis]
        _, length = chunk_of(me, ORDERS[part], phase)
        if s < n // 2:
            return [(1, first_, 0, length) for first_ in (s - 1,)] + [(-1, s - 1, 0, length)]
        if length == 1:
            return [(1, s - 1, 0, 1)]
        return [(1, s - 1, 0, length // 2), (-1, s - 1, length // 2, length // 2)]

    def issue(part, index):
        phase, s = steps[part][index]
        axis = ORDERS[part][phase]
        for way, back, first, count in pieces(part, phase, s):
            origin = shifted(me, axis, -way * back)
            start, _ = chunk_of(origin, ORDERS[part], phase)
            d = 0 if way > 0 else 1
            push(part, start + first, count, shifted(me, axis, way),
                 send_sem.at[part, index, d], recv_sem.at[part, index, d])

    def collect(part, index):
        phase, s = steps[part][index]
        axis = ORDERS[part][phase]
        for way, back, first, count in pieces(part, phase, s):
            origin = shifted(me, axis, -way * (back + 1))
            start, _ = chunk_of(origin, ORDERS[part], phase)
            d = 0 if way > 0 else 1
            arrived(part, start + first, count, shifted(me, axis, -way),
                    send_sem.at[part, index, d], recv_sem.at[part, index, d])

    def hand_on(part, index):
        phase, s = steps[part][index]
        axis = ORDERS[part][phase]
        if phase == 0:
            if s == SIZES[axis] // 2:
                to_sibling(part, me, 1)
            return
        for way, back, first, count in pieces(part, phase, s):
            to_sibling(part, shifted(me, axis, -way * (back + 1)), phase, first, count)

    def mom_copies(src, dst, others, slot0):
        out = []
        for k, (other, row) in enumerate(others):
            out.append(pltpu.make_async_remote_copy(
                src_ref=src, dst_ref=dst.at[row], send_sem=mom_send.at[slot0 + k],
                recv_sem=mom_recv.at[slot0 + k], device_id=mesh_id(other), device_id_type=MESH,
            ))
        return out

    z_copies = mom_copies(mom_own, mom_z, [(shifted(me, "z", k), k - 1) for k in range(1, NZ)], 0)
    for part in range(3):
        issue(part, 0)
    for copy in z_copies:
        copy.start()
    n_steps = len(steps[0])
    later = []
    for index in range(n_steps):
        for part in range(3):
            collect(part, index)
            if index + 1 < n_steps:
                issue(part, index + 1)
            hand_on(part, index)
        if index == 0:
            total = mom_own[...]
            for k, copy in enumerate(z_copies):
                copy.wait()
                total = total + mom_z[k]
            mom_own[...] = total
            later = mom_copies(mom_own, mom_y, [(shifted(me, "y", k), k - 1) for k in range(1, NY)], 7)
            for copy in later:
                copy.start()
        elif index == 2:
            total = mom_own[...]
            for k, copy in enumerate(later):
                copy.wait()
                total = total + mom_y[k]
            mom_own[...] = total
            later = mom_copies(mom_own, mom_c, [(sibling, 0)], 10)
            later[0].start()
        elif index == 3:
            later[0].wait()
            mom_own[...] = mom_own[...] + mom_c[0]
            moments[pl.ds(me["x"], 1)] = mom_own[...][None]
            later = []
            for k in range(1, NX):
                copy = pltpu.make_async_remote_copy(
                    src_ref=mom_own, dst_ref=moments.at[me["x"]], send_sem=mom_send.at[10 + k],
                    recv_sem=mom_recv.at[10 + k], device_id=mesh_id(shifted(me, "x", k)),
                    device_id_type=MESH,
                )
                copy.start()
                later.append(copy)
        elif index == 5:
            for k in range(1, NX):
                frm = shifted(me, "x", -k)
                pltpu.make_async_remote_copy(
                    src_ref=mom_own, dst_ref=moments.at[frm["x"]], send_sem=mom_send.at[10 + k],
                    recv_sem=mom_recv.at[10 + k], device_id=mesh_id(frm), device_id_type=MESH,
                ).wait_recv()
            for copy in later:
                copy.wait_send()
    for part, start, count, slot in core_in:
        arrived(part, start, count, sibling, core_send.at[part, slot], core_recv.at[part, slot])
    for copy in sent:
        copy.wait_send()


def gather(points, shift, facets):
    f32 = jnp.float32
    vmem = pl.BlockSpec(memory_space=pltpu.VMEM)
    return pl.pallas_call(
        gather_kernel,
        out_shape=(
            jax.ShapeDtypeStruct((3, LEAVES, 8, LANES), f32),
            jax.ShapeDtypeStruct((NX, 8, LANES), f32),
        ),
        in_specs=[vmem] * 3,
        out_specs=(vmem, vmem),
        scratch_shapes=[
            pltpu.VMEM((8, LANES), f32),
            pltpu.VMEM((7, 8, LANES), f32),
            pltpu.VMEM((3, 8, LANES), f32),
            pltpu.VMEM((1, 8, LANES), f32),
            pltpu.SemaphoreType.DMA((3, 8, 2)),
            pltpu.SemaphoreType.DMA((3, 8, 2)),
            pltpu.SemaphoreType.DMA((3, 24)),
            pltpu.SemaphoreType.DMA((3, 24)),
            pltpu.SemaphoreType.DMA((14,)),
            pltpu.SemaphoreType.DMA((14,)),
        ],
        compiler_params=pltpu.CompilerParams(
            collective_id=0, has_side_effects=True, vmem_limit_bytes=40 * 2**20
        ),
    )(points, shift, facets)


def dot3(a, b):
    return a[0] * b[0] + a[1] * b[1] + a[2] * b[2]


def minus3(a, b):
    return [a[0] - b[0], a[1] - b[1], a[2] - b[2]]


def cross3(a, b):
    return [a[1] * b[2] - a[2] * b[1], a[2] * b[0] - a[0] * b[2], a[0] * b[1] - a[1] * b[0]]


def leaf_places(leaf):
    device, within = leaf // 2, leaf % 2
    c = coords_of(device // 16, device % 16)
    return [place(c, order) * 2 + within for order in ORDERS]


def leaf_ids(x):
    lane = lax.broadcasted_iota(jnp.int32, (1, LANES), 1)
    z = (lane // 2) % NZ
    y = (lane // (2 * NZ)) % NY
    core = lane // (2 * NZ * NY)
    vol = ((y // 2) * NX + x) * 2 + core
    return (vol * 16 + z * 2 + y % 2) * 2 + lane % 2


PG = 32
CONST = 20


def facet_constants(a, b, c):
    ab, ac = minus3(b, a), minus3(c, a)
    normal = cross3(ab, ac)
    ab_len = jnp.sqrt(dot3(ab, ab))
    inv_ab = 1.0 / ab_len
    inv_n = lax.rsqrt(dot3(normal, normal))
    e1 = [q * inv_ab for q in ab]
    n = [q * inv_n for q in normal]
    e2 = cross3(n, e1)
    cx, cy = dot3(ac, e1), dot3(ac, e2)
    bc_x = cx - ab_len
    bc_len = jnp.sqrt(bc_x * bc_x + cy * cy)
    ac_len = jnp.sqrt(cx * cx + cy * cy)
    inv_bc, inv_ac = 1.0 / bc_len, 1.0 / ac_len
    bx, by = bc_x * inv_bc, cy * inv_bc
    ax, ay = cx * inv_ac, cy * inv_ac
    return [*e1, -dot3(e1, a), *e2, -dot3(e2, a), *n, -dot3(n, a),
            ab_len, bx, by, bx * ab_len, by * ab_len, bc_len, ax, ay, ac_len]


def facet_square(p, k):
    px, py, pz = p
    u = px * k[0] + py * k[1] + (pz * k[2] + k[3])
    v = px * k[4] + py * k[5] + (pz * k[6] + k[7])
    h = px * k[8] + py * k[9] + (pz * k[10] + k[11])
    ab, bx, by, bxl, byl, bc, ax, ay, ac = k[12:21]
    r1 = u - jnp.clip(u, 0.0, ab)
    t2 = bx * u + by * v - bxl
    s2 = bx * v - by * u + byl
    r2 = t2 - jnp.clip(t2, 0.0, bc)
    t3 = ax * u + ay * v
    s3 = ay * u - ax * v
    r3 = t3 - jnp.clip(t3, 0.0, ac)
    edge = jnp.minimum(jnp.minimum(r1 * r1 + v * v, r2 * r2 + s2 * s2), r3 * r3 + s3 * s3)
    inside = jnp.minimum(jnp.minimum(v, s2), s3) >= 0.0
    return h * h + jnp.where(inside, 0.0, edge)


def as_columns(row):
    return jnp.transpose(jnp.broadcast_to(row, (LANES, LANES)))


def compute_kernel(cand_ref, table, moments, vol_ref, flag_ref, disp_ref, wall_ref,
                   cols, acc, moved, index, const, best):
    surf = lax.axis_index("surf")

    def one_block(block, carry):
        row = surf * 4 + block
        lanes = pl.ds(pl.multiple_of(row * LANES, LANES), LANES)
        rows = [vol_ref[pl.ds(c, 1), lanes] for c in range(3)]
        for c in range(3):
            cols[c] = as_columns(rows[c])
        count = jnp.int32(0)
        for j in range(16):
            count += (cand_ref[row, j] >= 0).astype(jnp.int32)

        def add_terms(carry, d, s):
            q = d[0] * d[0] + d[1] * d[1] + d[2] * d[2] + smoothing
            inv = 1.0 / q
            return inv * inv

        center = []
        for x in range(NX):
            ids = leaf_ids(x)
            listed = ids == cand_ref[row, 0]
            for j in range(1, 16):
                listed = listed | (ids == cand_ref[row, j])
            center.append(jnp.where(listed, 0.0, float(LEAF)))
        for g in range(LANES // PG):
            part = pl.ds(g * PG, PG)
            p = [cols[c, part, :] for c in range(3)]
            sums = [jnp.zeros((PG, LANES), jnp.float32) for _ in range(4)]
            for x in range(NX):
                m = moments[x]
                d = [m[c:c + 1] - p[c] for c in range(3)]
                w = add_terms(None, d, None) * center[x]
                for c in range(3):
                    sums[c] = sums[c] + w * m[3 + c:4 + c]
                sums[3] = sums[3] + w

            def near(j, sums):
                p0, p1, _ = leaf_places(cand_ref[row, j])
                sums = list(sums)
                for half in range(2):
                    def at(part_, place_, r):
                        return table[part_, place_, pl.ds(r + half, 1), :]
                    d = [at(0, p0, 2 * c) - p[c] for c in range(3)]
                    w = add_terms(None, d, None)
                    shift = [at(0, p0, 6), at(1, p1, 0), at(1, p1, 2)]
                    for c in range(3):
                        sums[c] = sums[c] + w * shift[c]
                    sums[3] = sums[3] + w
                return tuple(sums)

            sums = lax.fori_loop(0, count, near, tuple(sums))
            for c in range(4):
                acc[c, part, :] = sums[c]
        total = [jnp.sum(jnp.transpose(acc[c]), axis=0, keepdims=True) for c in range(4)]
        inv = 1.0 / total[3]
        out_lanes = pl.ds(pl.multiple_of(block * LANES, LANES), LANES)
        for c in range(3):
            disp = total[c] * inv
            disp_ref[pl.ds(c, 1), out_lanes] = disp
            cols[c] = as_columns(rows[c] + disp)
        flags = flag_ref[pl.ds(row, 1), :]
        flagged = jnp.max(flags) > 0
        wall_ref[pl.ds(block, 1), :] = jnp.zeros((1, LANES), jnp.float32)

        @pl.when(flagged)
        def _():
            def fetch(j, carry):
                p0, p1, p2 = leaf_places(jnp.maximum(cand_ref[row, j], 0))
                here = pl.ds(j, 1)
                for half in range(2):
                    s = [table[0, p0, pl.ds(6 + half, 1), :], table[1, p1, pl.ds(half, 1), :],
                         table[1, p1, pl.ds(2 + half, 1), :]]
                    for c in range(3):
                        moved[c, half, here, :] = table[0, p0, pl.ds(2 * c + half, 1), :] + s[c]
                for quarter in range(4):
                    index[0, quarter, here, :] = table[1, p1, pl.ds(4 + quarter, 1), :].astype(jnp.int32)
                    index[1, quarter, here, :] = table[2, p2, pl.ds(quarter, 1), :].astype(jnp.int32)
                    index[2, quarter, here, :] = table[2, p2, pl.ds(4 + quarter, 1), :].astype(jnp.int32)
                return carry

            lax.fori_loop(0, 16, fetch, 0)
            for quarter in range(4):
                corners = []
                for k in range(3):
                    where = index[k, quarter]
                    low = where % LANES
                    corner = []
                    for c in range(3):
                        lo = jnp.take_along_axis(moved[c, 0], low, axis=1, mode="promise_in_bounds")
                        hi = jnp.take_along_axis(moved[c, 1], low, axis=1, mode="promise_in_bounds")
                        corner.append(jnp.where(where < LANES, lo, hi))
                    corners.append(corner)
                for i, value in enumerate(facet_constants(*corners)):
                    const[i, quarter] = value
            best[...] = jnp.full((LANES, LANES), big_value, jnp.float32)

            def one_leaf(j, carry):
                for quarter in range(4):
                    k = [jnp.broadcast_to(const[i, quarter, pl.ds(j, 1), :], (8, LANES)) for i in range(21)]
                    for g in range(16):
                        part = pl.ds(g * 8, 8)
                        p = [cols[c, part, :] for c in range(3)]
                        best[part, :] = jnp.minimum(best[part, :], facet_square(p, k))
                return carry

            lax.fori_loop(0, count, one_leaf, 0)
            nearest = jnp.min(jnp.transpose(best[...]), axis=0, keepdims=True)
            wall_ref[pl.ds(block, 1), :] = jnp.where(flags == 1, jnp.sqrt(nearest), 0.0)

        return carry

    lax.fori_loop(0, 4, one_block, 0)


def compute(candidates, table, moments, points, flags):
    f32 = jnp.float32
    vmem = pl.BlockSpec(memory_space=pltpu.VMEM)
    return pl.pallas_call(
        compute_kernel,
        out_shape=(
            jax.ShapeDtypeStruct((3, 4 * LANES), f32),
            jax.ShapeDtypeStruct((4, LANES), f32),
        ),
        in_specs=[pl.BlockSpec(memory_space=pltpu.SMEM), vmem, vmem, vmem, vmem],
        out_specs=(vmem, vmem),
        scratch_shapes=[
            pltpu.VMEM((3, LANES, LANES), f32),
            pltpu.VMEM((4, LANES, LANES), f32),
            pltpu.VMEM((3, 2, 16, LANES), f32),
            pltpu.VMEM((3, 4, 16, LANES), jnp.int32),
            pltpu.VMEM((21, 4, 16, LANES), f32),
            pltpu.VMEM((LANES, LANES), f32),
        ],
        compiler_params=pltpu.CompilerParams(vmem_limit_bytes=40 * 2**20),
    )(candidates, table, moments, points, flags)


def body(surface_points, surface_shift, facet_nodes, volume_points, near_wall, candidates):
    table, moments = gather(surface_points, surface_shift, facet_nodes)
    flags = near_wall.reshape(-1, LANES)
    displacement, wall = compute(candidates, table, moments, volume_points, flags)
    return displacement, wall.reshape(-1)


def solution(mesh):
    placed = (
        P(None, ("vol", "surf")),
        P(None, ("vol", "surf")),
        P(("vol", "surf"), None, None),
        P(None, "vol"),
        P("vol"),
        P("vol", None),
    )
    return jax.shard_map(
        body,
        mesh=mesh,
        in_specs=placed,
        out_specs=(P(None, ("vol", "surf")), P(("vol", "surf"))),
        check_vma=False,
    )
```

```python
import functools

import jax
import jax.numpy as jnp
from jax import lax
from jax.experimental import pallas as pl
from jax.experimental.pallas import tpu as pltpu
from jax.sharding import PartitionSpec as P

MESH = pl.DeviceIdType.MESH
smoothing = 0.01
big_value = 1e30

NX, NY, NZ = 4, 4, 8
SIZES = {"x": NX, "y": NY, "z": NZ}
ORDERS = (("z", "y", "x"), ("x", "z", "y"), ("y", "x", "z"))
LEAF = 256
CHIPS = NX * NY * NZ
LEAVES = 4 * CHIPS
LANES = 128


def coords_of(vol, surf):
    return {
        "x": (vol // 2) % NX,
        "y": (vol // (2 * NX)) * 2 + surf % 2,
        "z": surf // 2,
        "c": vol % 2,
    }


def mesh_id(c):
    return ((c["y"] // 2) * NX + c["x"]) * 2 + c["c"], c["z"] * 2 + c["y"] % 2


def shifted(c, axis, k):
    n = SIZES[axis]
    return {**c, axis: lax.rem(c[axis] + (k % n), n)}


def place(c, order):
    a, b, d = order
    return ((c["c"] * SIZES[d] + c[d]) * SIZES[b] + c[b]) * SIZES[a] + c[a]


def chunk_of(c, order, phase):
    a, b, _ = order
    length = (1, SIZES[a], SIZES[a] * SIZES[b])[phase]
    start = place(c, order)
    return (start // length) * length, length


def gather_kernel(points_ref, shift_ref, facets_ref, table, moments, mom_own, mom_z, mom_y, mom_c,
                  send_sem, recv_sem, core_send, core_recv, mom_send, mom_recv):
    me = coords_of(lax.axis_index("vol"), lax.axis_index("surf"))
    sibling = {**me, "c": 1 - me["c"]}
    partners = [sibling]
    for axis, n in SIZES.items():
        partners += [shifted(me, axis, k) for k in range(1, n)]
    barrier = pltpu.get_barrier_semaphore()
    for other in partners:
        pl.semaphore_signal(barrier, inc=1, device_id=mesh_id(other), device_id_type=MESH)

    own = [place(me, order) * 2 for order in ORDERS]
    for leaf in range(2):
        for half in range(2):
            lanes = pl.ds(leaf * LEAF + half * LANES, LANES)
            for c in range(3):
                table[0, own[0] + leaf, pl.ds(2 * c + half, 1), :] = points_ref[pl.ds(c, 1), lanes]
            table[0, own[0] + leaf, pl.ds(6 + half, 1), :] = shift_ref[pl.ds(0, 1), lanes]
            table[1, own[1] + leaf, pl.ds(0 + half, 1), :] = shift_ref[pl.ds(1, 1), lanes]
            table[1, own[1] + leaf, pl.ds(2 + half, 1), :] = shift_ref[pl.ds(2, 1), lanes]
        for quarter in range(4):
            lanes = pl.ds(quarter * LANES, LANES)
            for k, (part, row) in enumerate(((1, 4), (2, 0), (2, 4))):
                table[part, own[part] + leaf, pl.ds(row + quarter, 1), :] = (
                    facets_ref[leaf, pl.ds(k, 1), lanes].astype(jnp.float32)
                )
    lane = lax.broadcasted_iota(jnp.int32, (3, LANES), 1)
    my_lane = ((me["c"] * NY + me["y"]) * NZ + me["z"]) * 2
    for row, ref in ((0, points_ref), (3, shift_ref)):
        tile = jnp.zeros((3, LANES), jnp.float32)
        for leaf in range(2):
            mean = jnp.sum(ref[:, pl.ds(leaf * LEAF, LEAF)], axis=1, keepdims=True) * (1.0 / LEAF)
            tile = jnp.where(lane == my_lane + leaf, mean, tile)
        mom_own[pl.ds(row, 3), :] = tile
    mom_own[pl.ds(6, 2), :] = jnp.zeros((2, LANES), jnp.float32)
    pl.semaphore_wait(barrier, len(partners))

    sent = []

    def push(part, start, length, to, s_sem, r_sem):
        where = table.at[part, pl.ds(start * 2, length * 2)]
        copy = pltpu.make_async_remote_copy(
            src_ref=where, dst_ref=where, send_sem=s_sem, recv_sem=r_sem,
            device_id=mesh_id(to), device_id_type=MESH,
        )
        copy.start()
        sent.append(copy)

    def arrived(part, start, length, frm, s_sem, r_sem):
        where = table.at[part, pl.ds(start * 2, length * 2)]
        pltpu.make_async_remote_copy(
            src_ref=where, dst_ref=where, send_sem=s_sem, recv_sem=r_sem,
            device_id=mesh_id(frm), device_id_type=MESH,
        ).wait_recv()

    steps = []
    for order in ORDERS:
        steps.append([(ph, s) for ph in range(3) for s in range(1, SIZES[order[ph]] // 2 + 1)])
    core_slot = [0, 0, 0]
    core_in = []

    def to_sibling(part, c, phase, first=0, count=None):
        start, length = chunk_of(c, ORDERS[part], phase)
        theirs, _ = chunk_of({**c, "c": 1 - me["c"]}, ORDERS[part], phase)
        count = length if count is None else count
        slot = core_slot[part]
        core_slot[part] += 1
        push(part, start + first, count, sibling, core_send.at[part, slot], core_recv.at[part, slot])
        core_in.append((part, theirs + first, count, slot))

    def pieces(part, phase, s):
        axis = ORDERS[part][phase]
        n = SIZES[axis]
        _, length = chunk_of(me, ORDERS[part], phase)
        if s < n // 2:
            return [(1, first_, 0, length) for first_ in (s - 1,)] + [(-1, s - 1, 0, length)]
        if length == 1:
            return [(1, s - 1, 0, 1)]
        return [(1, s - 1, 0, length // 2), (-1, s - 1, length // 2, length // 2)]

    def issue(part, index):
        phase, s = steps[part][index]
        axis = ORDERS[part][phase]
        for way, back, first, count in pieces(part, phase, s):
            origin = shifted(me, axis, -way * back)
            start, _ = chunk_of(origin, ORDERS[part], phase)
            d = 0 if way > 0 else 1
            push(part, start + first, count, shifted(me, axis, way),
                 send_sem.at[part, index, d], recv_sem.at[part, index, d])

    def collect(part, index):
        phase, s = steps[part][index]
        axis = ORDERS[part][phase]
        for way, back, first, count in pieces(part, phase, s):
            origin = shifted(me, axis, -way * (back + 1))
            start, _ = chunk_of(origin, ORDERS[part], phase)
            d = 0 if way > 0 else 1
            arrived(part, start + first, count, shifted(me, axis, -way),
                    send_sem.at[part, index, d], recv_sem.at[part, index, d])

    def hand_on(part, index):
        phase, s = steps[part][index]
        axis = ORDERS[part][phase]
        if phase == 0:
            if s == SIZES[axis] // 2:
                to_sibling(part, me, 1)
            return
        for way, back, first, count in pieces(part, phase, s):
            to_sibling(part, shifted(me, axis, -way * (back + 1)), phase, first, count)

    def mom_copies(src, dst, others, slot0):
        out = []
        for k, (other, row) in enumerate(others):
            out.append(pltpu.make_async_remote_copy(
                src_ref=src, dst_ref=dst.at[row], send_sem=mom_send.at[slot0 + k],
                recv_sem=mom_recv.at[slot0 + k], device_id=mesh_id(other), device_id_type=MESH,
            ))
        return out

    z_copies = mom_copies(mom_own, mom_z, [(shifted(me, "z", k), k - 1) for k in range(1, NZ)], 0)
    for part in range(3):
        issue(part, 0)
    for copy in z_copies:
        copy.start()
    n_steps = len(steps[0])
    later = []
    for index in range(n_steps):
        for part in range(3):
            collect(part, index)
            if index + 1 < n_steps:
                issue(part, index + 1)
            hand_on(part, index)
        if index == 0:
            total = mom_own[...]
            for k, copy in enumerate(z_copies):
                copy.wait()
                total = total + mom_z[k]
            mom_own[...] = total
            later = mom_copies(mom_own, mom_y, [(shifted(me, "y", k), k - 1) for k in range(1, NY)], 7)
            for copy in later:
                copy.start()
        elif index == 2:
            total = mom_own[...]
            for k, copy in enumerate(later):
                copy.wait()
                total = total + mom_y[k]
            mom_own[...] = total
            later = mom_copies(mom_own, mom_c, [(sibling, 0)], 10)
            later[0].start()
        elif index == 3:
            later[0].wait()
            mom_own[...] = mom_own[...] + mom_c[0]
            moments[pl.ds(me["x"], 1)] = mom_own[...][None]
            later = []
            for k in range(1, NX):
                copy = pltpu.make_async_remote_copy(
                    src_ref=mom_own, dst_ref=moments.at[me["x"]], send_sem=mom_send.at[10 + k],
                    recv_sem=mom_recv.at[10 + k], device_id=mesh_id(shifted(me, "x", k)),
                    device_id_type=MESH,
                )
                copy.start()
                later.append(copy)
        elif index == 5:
            for k in range(1, NX):
                frm = shifted(me, "x", -k)
                pltpu.make_async_remote_copy(
                    src_ref=mom_own, dst_ref=moments.at[frm["x"]], send_sem=mom_send.at[10 + k],
                    recv_sem=mom_recv.at[10 + k], device_id=mesh_id(frm), device_id_type=MESH,
                ).wait_recv()
            for copy in later:
                copy.wait_send()
    for part, start, count, slot in core_in:
        arrived(part, start, count, sibling, core_send.at[part, slot], core_recv.at[part, slot])
    for copy in sent:
        copy.wait_send()


def gather(points, shift, facets):
    f32 = jnp.float32
    vmem = pl.BlockSpec(memory_space=pltpu.VMEM)
    return pl.pallas_call(
        gather_kernel,
        out_shape=(
            jax.ShapeDtypeStruct((3, LEAVES, 8, LANES), f32),
            jax.ShapeDtypeStruct((NX, 8, LANES), f32),
        ),
        in_specs=[vmem] * 3,
        out_specs=(vmem, vmem),
        scratch_shapes=[
            pltpu.VMEM((8, LANES), f32),
            pltpu.VMEM((7, 8, LANES), f32),
            pltpu.VMEM((3, 8, LANES), f32),
            pltpu.VMEM((1, 8, LANES), f32),
            pltpu.SemaphoreType.DMA((3, 8, 2)),
            pltpu.SemaphoreType.DMA((3, 8, 2)),
            pltpu.SemaphoreType.DMA((3, 24)),
            pltpu.SemaphoreType.DMA((3, 24)),
            pltpu.SemaphoreType.DMA((14,)),
            pltpu.SemaphoreType.DMA((14,)),
        ],
        compiler_params=pltpu.CompilerParams(
            collective_id=0, has_side_effects=True, vmem_limit_bytes=40 * 2**20
        ),
    )(points, shift, facets)


def dot3(a, b):
    return a[0] * b[0] + a[1] * b[1] + a[2] * b[2]


def minus3(a, b):
    return [a[0] - b[0], a[1] - b[1], a[2] - b[2]]


def cross3(a, b):
    return [a[1] * b[2] - a[2] * b[1], a[2] * b[0] - a[0] * b[2], a[0] * b[1] - a[1] * b[0]]


def leaf_places(leaf):
    device, within = leaf // 2, leaf % 2
    c = coords_of(device // 16, device % 16)
    return [place(c, order) * 2 + within for order in ORDERS]


def leaf_ids(x):
    lane = lax.broadcasted_iota(jnp.int32, (1, LANES), 1)
    z = (lane // 2) % NZ
    y = (lane // (2 * NZ)) % NY
    core = lane // (2 * NZ * NY)
    vol = ((y // 2) * NX + x) * 2 + core
    return (vol * 16 + z * 2 + y % 2) * 2 + lane % 2


margin = 1e-4
PG = 32
CONST = 20


def facet_constants(a, b, c):
    ab, ac = minus3(b, a), minus3(c, a)
    normal = cross3(ab, ac)
    ab_len = jnp.sqrt(dot3(ab, ab))
    inv_ab = 1.0 / ab_len
    inv_n = lax.rsqrt(dot3(normal, normal))
    e1 = [q * inv_ab for q in ab]
    n = [q * inv_n for q in normal]
    e2 = cross3(n, e1)
    cx, cy = dot3(ac, e1), dot3(ac, e2)
    bc_x = cx - ab_len
    bc_len = jnp.sqrt(bc_x * bc_x + cy * cy)
    ac_len = jnp.sqrt(cx * cx + cy * cy)
    inv_bc, inv_ac = 1.0 / bc_len, 1.0 / ac_len
    bx, by = bc_x * inv_bc, cy * inv_bc
    ax, ay = cx * inv_ac, cy * inv_ac
    return [*e1, -dot3(e1, a), *e2, -dot3(e2, a), *n, -dot3(n, a),
            ab_len, bx, by, bx * ab_len, by * ab_len, bc_len, ax, ay, ac_len]


def facet_square(p, k):
    px, py, pz = p
    u = px * k[0] + py * k[1] + (pz * k[2] + k[3])
    v = px * k[4] + py * k[5] + (pz * k[6] + k[7])
    h = px * k[8] + py * k[9] + (pz * k[10] + k[11])
    ab, bx, by, bxl, byl, bc, ax, ay, ac = k[12:21]
    r1 = u - jnp.clip(u, 0.0, ab)
    t2 = bx * u + by * v - bxl
    s2 = bx * v - by * u + byl
    r2 = t2 - jnp.clip(t2, 0.0, bc)
    t3 = ax * u + ay * v
    s3 = ay * u - ax * v
    r3 = t3 - jnp.clip(t3, 0.0, ac)
    edge = jnp.minimum(jnp.minimum(r1 * r1 + v * v, r2 * r2 + s2 * s2), r3 * r3 + s3 * s3)
    inside = jnp.minimum(jnp.minimum(v, s2), s3) >= 0.0
    return h * h + jnp.where(inside, 0.0, edge)


def as_columns(row):
    return jnp.transpose(jnp.broadcast_to(row, (LANES, LANES)))


def compute_kernel(cand_ref, table, moments, vol_ref, flag_ref, disp_ref, wall_ref,
                   cols, acc, moved, index, const, best):
    surf = lax.axis_index("surf")

    def one_block(block, carry):
        row = surf * 4 + block
        lanes = pl.ds(pl.multiple_of(row * LANES, LANES), LANES)
        rows = [vol_ref[pl.ds(c, 1), lanes] for c in range(3)]
        for c in range(3):
            cols[c] = as_columns(rows[c])
        count = jnp.int32(0)
        for j in range(16):
            count += (cand_ref[row, j] >= 0).astype(jnp.int32)

        def add_terms(carry, d, s):
            q = d[0] * d[0] + d[1] * d[1] + d[2] * d[2] + smoothing
            inv = 1.0 / q
            return inv * inv

        center = []
        for x in range(NX):
            ids = leaf_ids(x)
            listed = ids == cand_ref[row, 0]
            for j in range(1, 16):
                listed = listed | (ids == cand_ref[row, j])
            center.append(jnp.where(listed, 0.0, float(LEAF)))
        for g in range(LANES // PG):
            part = pl.ds(g * PG, PG)
            p = [cols[c, part, :] for c in range(3)]
            sums = [jnp.zeros((PG, LANES), jnp.float32) for _ in range(4)]
            for x in range(NX):
                m = moments[x]
                d = [m[c:c + 1] - p[c] for c in range(3)]
                w = add_terms(None, d, None) * center[x]
                for c in range(3):
                    sums[c] = sums[c] + w * m[3 + c:4 + c]
                sums[3] = sums[3] + w

            def near(j, sums):
                p0, p1, _ = leaf_places(cand_ref[row, j])
                sums = list(sums)
                for half in range(2):
                    def at(part_, place_, r):
                        return table[part_, place_, pl.ds(r + half, 1), :]
                    d = [at(0, p0, 2 * c) - p[c] for c in range(3)]
                    w = add_terms(None, d, None)
                    shift = [at(0, p0, 6), at(1, p1, 0), at(1, p1, 2)]
                    for c in range(3):
                        sums[c] = sums[c] + w * shift[c]
                    sums[3] = sums[3] + w
                return tuple(sums)

            sums = lax.fori_loop(0, count, near, tuple(sums))
            for c in range(4):
                acc[c, part, :] = sums[c]
        total = [jnp.sum(jnp.transpose(acc[c]), axis=0, keepdims=True) for c in range(4)]
        inv = 1.0 / total[3]
        out_lanes = pl.ds(pl.multiple_of(block * LANES, LANES), LANES)
        targets = []
        for c in range(3):
            disp = total[c] * inv
            disp_ref[pl.ds(c, 1), out_lanes] = disp
            targets.append(rows[c] + disp)
            cols[c] = as_columns(targets[c])
        flags = flag_ref[pl.ds(row, 1), :]
        flagged = jnp.max(flags) > 0
        wall_ref[pl.ds(block, 1), :] = jnp.zeros((1, LANES), jnp.float32)

        @pl.when(flagged)
        def _():
            def fetch(j, carry):
                p0, p1, p2 = leaf_places(jnp.maximum(cand_ref[row, j], 0))
                here = pl.ds(j, 1)
                for half in range(2):
                    s = [table[0, p0, pl.ds(6 + half, 1), :], table[1, p1, pl.ds(half, 1), :],
                         table[1, p1, pl.ds(2 + half, 1), :]]
                    for c in range(3):
                        moved[c, half, here, :] = table[0, p0, pl.ds(2 * c + half, 1), :] + s[c]
                for quarter in range(4):
                    index[0, quarter, here, :] = table[1, p1, pl.ds(4 + quarter, 1), :].astype(jnp.int32)
                    index[1, quarter, here, :] = table[2, p2, pl.ds(quarter, 1), :].astype(jnp.int32)
                    index[2, quarter, here, :] = table[2, p2, pl.ds(4 + quarter, 1), :].astype(jnp.int32)
                return carry

            lax.fori_loop(0, 16, fetch, 0)
            for quarter in range(4):
                corners = []
                for k in range(3):
                    where = index[k, quarter]
                    low = where % LANES
                    corner = []
                    for c in range(3):
                        lo = jnp.take_along_axis(moved[c, 0], low, axis=1, mode="promise_in_bounds")
                        hi = jnp.take_along_axis(moved[c, 1], low, axis=1, mode="promise_in_bounds")
                        corner.append(jnp.where(where < LANES, lo, hi))
                    corners.append(corner)
                for i, value in enumerate(facet_constants(*corners)):
                    const[i, quarter] = value
            best[...] = jnp.full((LANES, LANES), big_value, jnp.float32)

            def one_leaf(j):
                for quarter in range(4):
                    k = [jnp.broadcast_to(const[i, quarter, pl.ds(j, 1), :], (8, LANES)) for i in range(21)]
                    for g in range(16):
                        part = pl.ds(g * 8, 8)
                        p = [cols[c, part, :] for c in range(3)]
                        best[part, :] = jnp.minimum(best[part, :], facet_square(p, k))

            slot = lax.broadcasted_iota(jnp.int32, (16, 1), 0)
            middle = [
                jnp.sum(moved[c, 0] + moved[c, 1], axis=1, keepdims=True) * (1.0 / LEAF) for c in range(3)
            ]
            spread = [
                sum((moved[c, half] - middle[c]) * (moved[c, half] - middle[c]) for c in range(3))
                for half in range(2)
            ]
            radius = jnp.sqrt(jnp.max(jnp.maximum(*spread), axis=1, keepdims=True)) + margin
            away = [middle[c] - targets[c] for c in range(3)]
            away = jnp.sqrt(dot3(away, away))
            valid = slot < count
            lower = jnp.maximum(away - radius, 0.0)
            lower = jnp.where(valid & (flags == 1), lower * lower, big_value)
            upper = jnp.where(valid, away + radius, 1e15)
            upper = jnp.min(upper * upper, axis=0, keepdims=True)
            rank = jnp.sum(jnp.where(flags == 1, away, 0.0), axis=1, keepdims=True)
            rank = jnp.where(valid, rank, big_value)

            def nearest_slot(rank):
                low = jnp.min(rank, axis=0, keepdims=True)
                return jnp.min(jnp.where(rank == low, slot, 15))

            def so_far():
                return jnp.min(jnp.transpose(best[...]), axis=0, keepdims=True)

            def wanted(open_):
                below = lower < jnp.minimum(so_far(), upper)
                hit = jnp.max(jnp.where(below, 1.0, 0.0), axis=1, keepdims=True)
                return jnp.where(open_, hit, 0.0)

            first = nearest_slot(rank)
            one_leaf(first)
            open_ = slot != first
            hit = wanted(open_)

            @pl.when(jnp.max(hit) > 0.0)
            def _():
                second = nearest_slot(jnp.where(hit > 0.0, rank, big_value))
                one_leaf(second)
                rest = wanted(open_ & (slot != second))
                bits = jnp.sum(jnp.where(rest > 0.0, lax.shift_left(jnp.ones_like(slot), slot), 0))

                def perhaps(j, carry):
                    @pl.when(lax.shift_right_logical(bits, j) % 2 == 1)
                    def _():
                        one_leaf(j)

                    return carry

                lax.fori_loop(0, count, perhaps, 0)

            wall_ref[pl.ds(block, 1), :] = jnp.where(flags == 1, jnp.sqrt(so_far()), 0.0)

        return carry

    lax.fori_loop(0, 4, one_block, 0)


def compute(candidates, table, moments, points, flags):
    f32 = jnp.float32
    vmem = pl.BlockSpec(memory_space=pltpu.VMEM)
    return pl.pallas_call(
        compute_kernel,
        out_shape=(
            jax.ShapeDtypeStruct((3, 4 * LANES), f32),
            jax.ShapeDtypeStruct((4, LANES), f32),
        ),
        in_specs=[pl.BlockSpec(memory_space=pltpu.SMEM), vmem, vmem, vmem, vmem],
        out_specs=(vmem, vmem),
        scratch_shapes=[
            pltpu.VMEM((3, LANES, LANES), f32),
            pltpu.VMEM((4, LANES, LANES), f32),
            pltpu.VMEM((3, 2, 16, LANES), f32),
            pltpu.VMEM((3, 4, 16, LANES), jnp.int32),
            pltpu.VMEM((21, 4, 16, LANES), f32),
            pltpu.VMEM((LANES, LANES), f32),
        ],
        compiler_params=pltpu.CompilerParams(vmem_limit_bytes=40 * 2**20),
    )(candidates, table, moments, points, flags)


def body(surface_points, surface_shift, facet_nodes, volume_points, near_wall, candidates):
    table, moments = gather(surface_points, surface_shift, facet_nodes)
    flags = near_wall.reshape(-1, LANES)
    displacement, wall = compute(candidates, table, moments, volume_points, flags)
    return displacement, wall.reshape(-1)


def solution(mesh):
    placed = (
        P(None, ("vol", "surf")),
        P(None, ("vol", "surf")),
        P(("vol", "surf"), None, None),
        P(None, "vol"),
        P("vol"),
        P("vol", None),
    )
    return jax.shard_map(
        body,
        mesh=mesh,
        in_specs=placed,
        out_specs=(P(None, ("vol", "surf")), P(("vol", "surf"))),
        check_vma=False,
    )
```

```python
import jax
import jax.numpy as jnp
from jax import lax
from jax.experimental import pallas as pl
from jax.experimental.pallas import tpu as pltpu
from jax.sharding import PartitionSpec as P

MESH = pl.DeviceIdType.MESH
smoothing = 0.01
big_value = 1e30

NX, NY, NZ = 4, 4, 8
SIZES = {"x": NX, "y": NY, "z": NZ}
LEAF = 256
CHIPS = NX * NY * NZ
LANES = 128
ROWS = 4


def coords_of(vol, surf):
    return {
        "x": (vol // 2) % NX,
        "y": (vol // (2 * NX)) * 2 + surf % 2,
        "z": surf // 2,
        "c": vol % 2,
    }


def mesh_id(c):
    return ((c["y"] // 2) * NX + c["x"]) * 2 + c["c"], c["z"] * 2 + c["y"] % 2


def shifted(c, axis, k):
    n = SIZES[axis]
    return {**c, axis: lax.rem(c[axis] + (k % n), n)}


WAYS = (("z", "y", "x"), ("z", "x", "y"))
NEAR_FIRST = {4: (1, 3, 2), 8: (1, 7, 2, 6, 3, 5, 4)}


def span(table, part, phase, c):
    if phase == 0:
        return table.at[:, c["c"], c["x"], c["y"], pl.ds(c["z"] * 3, 3)]
    if phase == 1:
        return table.at[part, c["c"], c["x"], c["y"]]
    if part == 0:
        return table.at[0, c["c"], c["x"]]
    return table.at[1, c["c"], :, c["y"]]


def leaf_index(leaf):
    device = leaf // 2
    c = coords_of(device // 16, device % 16)
    return leaf % 2, c["c"], c["x"], c["y"], c["z"] * 3


def gather_kernel(cand_hbm, points_hbm, shift_hbm, facets_hbm, vol_hbm, listed_ref, disp_ref, target_ref,
                  nodes, facets, mom_own, mom_z, mom_y, mom_c, moments, cols, acc,
                  cand_ref, points_ref, shift_ref, facets_ref, vol_ref,
                  in_sem, send_sem, recv_sem, core_send, core_recv, mom_send, mom_recv):
    surf = lax.axis_index("surf")
    me = coords_of(lax.axis_index("vol"), surf)
    sibling = {**me, "c": 1 - me["c"]}
    partners = [sibling]
    for axis, n in SIZES.items():
        partners += [shifted(me, axis, k) for k in range(1, n)]
    barrier = pltpu.get_barrier_semaphore()
    for other in partners:
        pl.semaphore_signal(barrier, inc=1, device_id=mesh_id(other), device_id_type=MESH)
    share = pl.ds(pl.multiple_of(surf * 4 * LANES, 4 * LANES), 4 * LANES)
    inputs = [
        pltpu.make_async_copy(points_hbm, points_ref, in_sem.at[0]),
        pltpu.make_async_copy(shift_hbm, shift_ref, in_sem.at[1]),
        pltpu.make_async_copy(facets_hbm, facets_ref, in_sem.at[2]),
        pltpu.make_async_copy(vol_hbm.at[:, share], vol_ref, in_sem.at[3]),
        pltpu.make_async_copy(cand_hbm, cand_ref, in_sem.at[4]),
    ]
    for copy in inputs:
        copy.start()
    for copy in inputs:
        copy.wait()

    for leaf in range(2):
        own = (leaf, me["c"], me["x"], me["y"])
        for half in range(2):
            lanes = pl.ds(leaf * LEAF + half * LANES, LANES)
            for c in range(3):
                nodes[(*own, me["z"] * 3 + (2 * c) // 4, pl.ds((2 * c) % 4 + half, 1), slice(None))] = (
                    points_ref[pl.ds(c, 1), lanes]
                )
                nodes[(*own, me["z"] * 3 + (6 + 2 * c) // 4, pl.ds((6 + 2 * c) % 4 + half, 1), slice(None))] = (
                    shift_ref[pl.ds(c, 1), lanes]
                )
        for quarter in range(4):
            lanes = pl.ds(quarter * LANES, LANES)
            for k in range(3):
                facets[(*own, me["z"] * 3 + k, pl.ds(quarter, 1), slice(None))] = (
                    facets_ref[k, pl.ds(leaf, 1), lanes].astype(jnp.float32)
                )
    lane = lax.broadcasted_iota(jnp.int32, (3, LANES), 1)
    my_lane = ((me["c"] * NY + me["y"]) * NZ + me["z"]) * 2
    for row, ref in ((0, points_ref), (3, shift_ref)):
        tile = jnp.zeros((3, LANES), jnp.float32)
        for leaf in range(2):
            mean = jnp.sum(ref[:, pl.ds(leaf * LEAF, LEAF)], axis=1, keepdims=True) * (1.0 / LEAF)
            tile = jnp.where(lane == my_lane + leaf, mean, tile)
        mom_own[pl.ds(row, 3), :] = tile
    mom_own[pl.ds(6, 2), :] = jnp.zeros((2, LANES), jnp.float32)
    pl.semaphore_wait(barrier, len(partners))

    sent = []

    def remote(src, dst, to, s_sem, r_sem):
        return pltpu.make_async_remote_copy(
            src_ref=src, dst_ref=dst, send_sem=s_sem, recv_sem=r_sem,
            device_id=mesh_id(to), device_id_type=MESH,
        )

    def start(copy):
        copy.start()
        sent.append(copy)

    tables = (nodes, facets)

    def sems(which, part, phase, k):
        slot = (part, phase, k)
        return send_sem.at[(which, *slot)], recv_sem.at[(which, *slot)]

    def issue(which, part, phase):
        axis = WAYS[part][phase]
        mine = span(tables[which], part, phase, me)
        for k in NEAR_FIRST[SIZES[axis]]:
            start(remote(mine, mine, shifted(me, axis, k), *sems(which, part, phase, k)))

    def collect(which, part, phase, steps=None):
        axis = WAYS[part][phase]
        for k in steps or NEAR_FIRST[SIZES[axis]]:
            frm = shifted(me, axis, -k)
            theirs = span(tables[which], part, phase, frm)
            remote(theirs, theirs, frm, *sems(which, part, phase, k)).wait_recv()

    def to_sibling(which, part, k):
        mine = span(tables[which], part, 2, shifted(me, WAYS[part][2], -k))
        start(remote(mine, mine, sibling, core_send.at[which, part, k], core_recv.at[which, part, k]))

    def from_sibling(which, part, k):
        theirs = span(tables[which], part, 2, shifted(sibling, WAYS[part][2], -k))
        remote(theirs, theirs, sibling, core_send.at[which, part, k], core_recv.at[which, part, k]).wait_recv()

    def mom_copies(dst, others, slot0):
        return [
            remote(mom_own, dst.at[k], other, mom_send.at[slot0 + k], mom_recv.at[slot0 + k])
            for k, other in enumerate(others)
        ]

    def mom_sum(copies, arrived):
        total = mom_own[...]
        for k, copy in enumerate(copies):
            copy.wait()
            total = total + arrived[k]
        mom_own[...] = total

    issue(0, 0, 0)
    mom = mom_copies(mom_z, [shifted(me, "z", k) for k in range(1, NZ)], 0)
    for copy in mom:
        copy.start()
    issue(1, 0, 0)
    collect(0, 0, 0)
    issue(0, 0, 1)
    issue(0, 1, 1)
    mom_sum(mom, mom_z)
    mom = mom_copies(mom_y, [shifted(me, "y", k) for k in range(1, NY)], 7)
    for copy in mom:
        copy.start()
    collect(1, 0, 0)
    issue(1, 0, 1)
    issue(1, 1, 1)
    for part in range(2):
        collect(0, part, 1)
        issue(0, part, 2)
    for part in range(2):
        to_sibling(0, part, 0)
    mom_sum(mom, mom_y)
    mom = mom_copies(mom_c, [sibling], 10)
    mom[0].start()
    for part in range(2):
        collect(1, part, 1)
    mom_sum(mom, mom_c)
    moments[pl.ds(me["x"], 1)] = mom_own[...][None]
    for k in range(1, NX):
        start(remote(mom_own, moments.at[me["x"]], shifted(me, "x", k), mom_send.at[10 + k], mom_recv.at[10 + k]))
    for k in (1, 3, 2):
        for part in range(2):
            collect(0, part, 2, (k,))
            to_sibling(0, part, k)
    for part in range(2):
        issue(1, part, 2)
        to_sibling(1, part, 0)
    for k in range(1, NX):
        frm = shifted(me, "x", -k)
        remote(mom_own, moments.at[frm["x"]], frm, mom_send.at[10 + k], mom_recv.at[10 + k]).wait_recv()
    for part in range(2):
        for k in range(4):
            from_sibling(0, part, k)

    def displace(block):
        row = surf * 4 + block
        out_lanes = pl.ds(block * LANES, LANES)
        rows = [vol_ref[pl.ds(c, 1), out_lanes] for c in range(3)]
        for c in range(3):
            cols[c] = as_columns(rows[c])
        centers = []
        for x in range(NX):
            ids = leaf_ids(x)
            listed = ids == cand_ref[0, row]
            for j in range(1, 16):
                listed = listed | (ids == cand_ref[j, row])
            centers.append(jnp.where(listed, 0.0, float(LEAF)))

        def point_group(g, carry):
            part = pl.ds(pl.multiple_of(g * PG, PG), PG)
            p = [cols[c, part, :] for c in range(3)]
            sums = [jnp.zeros((PG, LANES), jnp.float32) for _ in range(4)]
            for x in range(NX):
                m = moments[x]
                w = weight([m[c:c + 1] - p[c] for c in range(3)]) * centers[x]
                for c in range(3):
                    sums[c] = sums[c] + w * m[3 + c:4 + c]
                sums[3] = sums[3] + w

            def near(j, sums):
                leaf = cand_ref[j, row]
                real = jnp.where(leaf >= 0, 1.0, 0.0)
                i0, i1, i2, i3, quad = leaf_index(jnp.maximum(leaf, 0))
                sums = list(sums)
                for half in range(2):
                    at = [nodes[i0, i1, i2, i3, quad + (2 * c) // 4, pl.ds((2 * c) % 4 + half, 1), :] for c in range(6)]
                    w = weight([at[c] - p[c] for c in range(3)]) * real
                    for c in range(3):
                        sums[c] = sums[c] + w * at[3 + c]
                    sums[3] = sums[3] + w
                return tuple(sums)

            sums = lax.fori_loop(0, 16, near, tuple(sums))
            for c in range(4):
                acc[c, part, :] = sums[c]
            return carry

        lax.fori_loop(0, LANES // PG, point_group, 0)
        total = [jnp.sum(jnp.transpose(acc[c]), axis=0, keepdims=True) for c in range(4)]
        inv = 1.0 / total[3]
        for c in range(3):
            disp = total[c] * inv
            disp_ref[pl.ds(c, 1), out_lanes] = disp
            target_ref[pl.ds(c, 1), out_lanes] = rows[c] + disp

    displace(0)
    displace(1)
    for k in (1, 3):
        for part in range(2):
            collect(1, part, 2, (k,))
            to_sibling(1, part, k)
    displace(2)
    for part in range(2):
        collect(1, part, 2, (2,))
        to_sibling(1, part, 2)
    displace(3)
    for part in range(2):
        for k in range(4):
            from_sibling(1, part, k)

    def hand_out(n, carry):
        leaf = jnp.maximum(cand_ref[n % 16, surf * 4 + n // 16], 0)
        i0, i1, i2, i3, quad = leaf_index(leaf)
        for q in range(3):
            listed_ref[n, q] = nodes[i0, i1, i2, i3, quad + q]
            listed_ref[n, 3 + q] = facets[i0, i1, i2, i3, quad + q]
        return carry

    lax.fori_loop(0, 64, hand_out, 0)
    for copy in sent:
        copy.wait_send()


def displace_and_list(candidates, points, shift, facets, vol):
    f32 = jnp.float32
    vmem = pl.BlockSpec(memory_space=pltpu.VMEM)
    table = pltpu.VMEM((2, 2, NX, NY, NZ * 3, ROWS, LANES), f32)
    dma = pltpu.SemaphoreType.DMA
    return pl.pallas_call(
        gather_kernel,
        name="displace",
        out_shape=(
            jax.ShapeDtypeStruct((64, 6, ROWS, LANES), f32),
            jax.ShapeDtypeStruct((3, 4 * LANES), f32),
            jax.ShapeDtypeStruct((3, 4 * LANES), f32),
        ),
        in_specs=[pl.BlockSpec(memory_space=pltpu.HBM)] * 5,
        out_specs=(vmem, vmem, vmem),
        scratch_shapes=[
            table,
            table,
            pltpu.VMEM((8, LANES), f32),
            pltpu.VMEM((7, 8, LANES), f32),
            pltpu.VMEM((3, 8, LANES), f32),
            pltpu.VMEM((1, 8, LANES), f32),
            pltpu.VMEM((NX, 8, LANES), f32),
            pltpu.VMEM((3, LANES, LANES), f32),
            pltpu.VMEM((4, LANES, LANES), f32),
            pltpu.SMEM((16, 64), jnp.int32),
            pltpu.VMEM((3, 4 * LANES), f32),
            pltpu.VMEM((3, 4 * LANES), f32),
            pltpu.VMEM((3, 2, 4 * LANES), jnp.int32),
            pltpu.VMEM((3, 4 * LANES), f32),
            dma((5,)),
            dma((2, 2, 3, 8)),
            dma((2, 2, 3, 8)),
            dma((2, 2, 4)),
            dma((2, 2, 4)),
            dma((14,)),
            dma((14,)),
        ],
        compiler_params=pltpu.CompilerParams(
            collective_id=0, has_side_effects=True, vmem_limit_bytes=24 * 2**20
        ),
    )(candidates, points, shift, facets, vol)


def dot3(a, b):
    return a[0] * b[0] + a[1] * b[1] + a[2] * b[2]


def minus3(a, b):
    return [a[0] - b[0], a[1] - b[1], a[2] - b[2]]


def cross3(a, b):
    return [a[1] * b[2] - a[2] * b[1], a[2] * b[0] - a[0] * b[2], a[0] * b[1] - a[1] * b[0]]


def leaf_ids(x):
    lane = lax.broadcasted_iota(jnp.int32, (1, LANES), 1)
    z = (lane // 2) % NZ
    y = (lane // (2 * NZ)) % NY
    core = lane // (2 * NZ * NY)
    vol = ((y // 2) * NX + x) * 2 + core
    return (vol * 16 + z * 2 + y % 2) * 2 + lane % 2


margin = 1e-4
PG = 32


def facet_constants(a, b, c):
    ab, ac = minus3(b, a), minus3(c, a)
    normal = cross3(ab, ac)
    ab_len = jnp.sqrt(dot3(ab, ab))
    inv_ab = 1.0 / ab_len
    inv_n = lax.rsqrt(dot3(normal, normal))
    e1 = [q * inv_ab for q in ab]
    n = [q * inv_n for q in normal]
    e2 = cross3(n, e1)
    cx, cy = dot3(ac, e1), dot3(ac, e2)
    bc_x = cx - ab_len
    bc_len = jnp.sqrt(bc_x * bc_x + cy * cy)
    ac_len = jnp.sqrt(cx * cx + cy * cy)
    inv_bc, inv_ac = 1.0 / bc_len, 1.0 / ac_len
    bx, by = bc_x * inv_bc, cy * inv_bc
    ax, ay = cx * inv_ac, cy * inv_ac
    return [*e1, -dot3(e1, a), *e2, -dot3(e2, a), *n, -dot3(n, a),
            ab_len, bx, by, bx * ab_len, by * ab_len, bc_len, ax, ay, ac_len]


def facet_square(p, k):
    px, py, pz = p
    u = px * k[0] + py * k[1] + (pz * k[2] + k[3])
    v = px * k[4] + py * k[5] + (pz * k[6] + k[7])
    h = px * k[8] + py * k[9] + (pz * k[10] + k[11])
    ab, bx, by, bxl, byl, bc, ax, ay, ac = k[12:21]
    r1 = u - jnp.clip(u, 0.0, ab)
    t2 = bx * u + by * v - bxl
    s2 = bx * v - by * u + byl
    r2 = t2 - jnp.clip(t2, 0.0, bc)
    t3 = ax * u + ay * v
    s3 = ay * u - ax * v
    r3 = t3 - jnp.clip(t3, 0.0, ac)
    edge = jnp.minimum(jnp.minimum(r1 * r1 + v * v, r2 * r2 + s2 * s2), r3 * r3 + s3 * s3)
    inside = jnp.minimum(jnp.minimum(v, s2), s3) >= 0.0
    return h * h + jnp.where(inside, 0.0, edge)


def weight(d):
    inv = 1.0 / (dot3(d, d) + smoothing)
    return inv * inv


def as_columns(row):
    return jnp.transpose(jnp.broadcast_to(row, (LANES, LANES)))


def wall_kernel(cand_hbm, listed_ref, disp_in, target_ref, flag_ref, disp_ref, wall_ref,
                cols, moved, index, const, best, cand_ref, in_sem):
    surf = lax.axis_index("surf")
    copy = pltpu.make_async_copy(cand_hbm, cand_ref, in_sem)
    copy.start()
    disp_ref[...] = disp_in[...]
    copy.wait()

    def one_block(block, carry):
        row = surf * 4 + block
        lanes = pl.ds(pl.multiple_of(block * LANES, LANES), LANES)
        count = jnp.int32(0)
        for j in range(16):
            count += (cand_ref[j, row] >= 0).astype(jnp.int32)
        flags = flag_ref[pl.ds(row, 1), :]
        flagged = jnp.max(flags) > 0
        wall_ref[pl.ds(block, 1), :] = jnp.zeros((1, LANES), jnp.float32)

        @pl.when(flagged)
        def _():
            targets = [target_ref[pl.ds(c, 1), lanes] for c in range(3)]
            for c in range(3):
                cols[c] = as_columns(targets[c])

            def fetch(j, carry):
                here = pl.ds(j, 1)
                rows = block * 16 + j
                for half in range(2):
                    at = [listed_ref[rows, (2 * c) // 4, pl.ds((2 * c) % 4 + half, 1), :] for c in range(6)]
                    for c in range(3):
                        moved[c, half, here, :] = at[c] + at[3 + c]
                for k in range(3):
                    for quarter in range(4):
                        index[k, quarter, here, :] = listed_ref[rows, 3 + k, pl.ds(quarter, 1), :].astype(jnp.int32)
                return carry

            lax.fori_loop(0, 16, fetch, 0)
            for quarter in range(4):
                corners = []
                for k in range(3):
                    where = index[k, quarter]
                    low = where % LANES
                    corner = []
                    for c in range(3):
                        lo = jnp.take_along_axis(moved[c, 0], low, axis=1, mode="promise_in_bounds")
                        hi = jnp.take_along_axis(moved[c, 1], low, axis=1, mode="promise_in_bounds")
                        corner.append(jnp.where(where < LANES, lo, hi))
                    corners.append(corner)
                for i, value in enumerate(facet_constants(*corners)):
                    const[i, quarter] = value
            best[...] = jnp.full((LANES, LANES), big_value, jnp.float32)

            def one_leaf(j):
                for quarter in range(4):
                    k = [jnp.broadcast_to(const[i, quarter, pl.ds(j, 1), :], (8, LANES)) for i in range(21)]
                    for g in range(16):
                        part = pl.ds(g * 8, 8)
                        p = [cols[c, part, :] for c in range(3)]
                        best[part, :] = jnp.minimum(best[part, :], facet_square(p, k))

            slot = lax.broadcasted_iota(jnp.int32, (16, 1), 0)
            middle = [
                jnp.sum(moved[c, 0] + moved[c, 1], axis=1, keepdims=True) * (1.0 / LEAF) for c in range(3)
            ]
            spread = [
                sum((moved[c, half] - middle[c]) * (moved[c, half] - middle[c]) for c in range(3))
                for half in range(2)
            ]
            radius = jnp.sqrt(jnp.max(jnp.maximum(*spread), axis=1, keepdims=True)) + margin
            away = [middle[c] - targets[c] for c in range(3)]
            away = jnp.sqrt(dot3(away, away))
            valid = slot < count
            lower = jnp.maximum(away - radius, 0.0)
            lower = jnp.where(valid & (flags == 1), lower * lower, big_value)
            upper = jnp.where(valid, away + radius, 1e15)
            upper = jnp.min(upper * upper, axis=0, keepdims=True)
            rank = jnp.sum(jnp.where(flags == 1, away, 0.0), axis=1, keepdims=True)
            rank = jnp.where(valid, rank, big_value)

            def nearest_slot(rank):
                low = jnp.min(rank, axis=0, keepdims=True)
                return jnp.min(jnp.where(rank == low, slot, 15))

            def so_far():
                return jnp.min(jnp.transpose(best[...]), axis=0, keepdims=True)

            def wanted(open_):
                below = lower < jnp.minimum(so_far(), upper)
                hit = jnp.max(jnp.where(below, 1.0, 0.0), axis=1, keepdims=True)
                return jnp.where(open_, hit, 0.0)

            first = nearest_slot(rank)
            one_leaf(first)
            open_ = slot != first
            hit = wanted(open_)

            @pl.when(jnp.max(hit) > 0.0)
            def _():
                second = nearest_slot(jnp.where(hit > 0.0, rank, big_value))
                one_leaf(second)
                rest = wanted(open_ & (slot != second))
                bits = jnp.sum(jnp.where(rest > 0.0, lax.shift_left(jnp.ones_like(slot), slot), 0))

                def perhaps(j, carry):
                    @pl.when(lax.shift_right_logical(bits, j) % 2 == 1)
                    def _():
                        one_leaf(j)

                    return carry

                lax.fori_loop(0, count, perhaps, 0)

            wall_ref[pl.ds(block, 1), :] = jnp.where(flags == 1, jnp.sqrt(so_far()), 0.0)

        return carry

    lax.fori_loop(0, 4, one_block, 0)


def wall(candidates, listed, disp, target, flags):
    f32 = jnp.float32
    vmem = pl.BlockSpec(memory_space=pltpu.VMEM)
    return pl.pallas_call(
        wall_kernel,
        name="wall",
        out_shape=(
            jax.ShapeDtypeStruct((3, 4 * LANES), f32),
            jax.ShapeDtypeStruct((4, LANES), f32),
        ),
        in_specs=[pl.BlockSpec(memory_space=pltpu.HBM), vmem, vmem, vmem, vmem],
        out_specs=(vmem, vmem),
        scratch_shapes=[
            pltpu.VMEM((3, LANES, LANES), f32),
            pltpu.VMEM((3, 2, 16, LANES), f32),
            pltpu.VMEM((3, 4, 16, LANES), jnp.int32),
            pltpu.VMEM((21, 4, 16, LANES), f32),
            pltpu.VMEM((LANES, LANES), f32),
            pltpu.SMEM((16, 64), jnp.int32),
            pltpu.SemaphoreType.DMA,
        ],
        compiler_params=pltpu.CompilerParams(vmem_limit_bytes=24 * 2**20),
    )(candidates, listed, disp, target, flags)


def body(surface_points, surface_shift, facet_nodes, volume_points, near_wall, candidates):
    candidates = candidates.T
    listed, disp, target = displace_and_list(
        candidates, surface_points, surface_shift, jnp.transpose(facet_nodes, (1, 0, 2)), volume_points
    )
    flags = near_wall.reshape(-1, LANES)
    displacement, distance = wall(candidates, listed, disp, target, flags)
    return displacement, distance.reshape(-1)


def solution(mesh):
    placed = (
        P(None, ("vol", "surf")),
        P(None, ("vol", "surf")),
        P(("vol", "surf"), None, None),
        P(None, "vol"),
        P("vol"),
        P("vol", None),
    )
    return jax.shard_map(
        body,
        mesh=mesh,
        in_specs=placed,
        out_specs=(P(None, ("vol", "surf")), P(("vol", "surf"))),
        check_vma=False,
    )
```

```python
import jax
import jax.numpy as jnp
from jax import lax
from jax.experimental import pallas as pl
from jax.experimental.pallas import tpu as pltpu
from jax.sharding import PartitionSpec as P

MESH = pl.DeviceIdType.MESH
smoothing = 0.01
big_value = 1e30

NX, NY, NZ = 4, 4, 8
SIZES = {"x": NX, "y": NY, "z": NZ}
LEAF = 256
CHIPS = NX * NY * NZ
LANES = 128
ROWS = 4


def coords_of(vol, surf):
    return {
        "x": (vol // 2) % NX,
        "y": (vol // (2 * NX)) * 2 + surf % 2,
        "z": surf // 2,
        "c": vol % 2,
    }


def mesh_id(c):
    return ((c["y"] // 2) * NX + c["x"]) * 2 + c["c"], c["z"] * 2 + c["y"] % 2


def shifted(c, axis, k):
    n = SIZES[axis]
    return {**c, axis: lax.rem(c[axis] + (k % n), n)}


WAYS = (("z", "y", "x"), ("z", "x", "y"))
NEAR_FIRST = {4: (1, 3, 2), 8: (1, 7, 2, 6, 3, 5, 4)}


def span(table, part, phase, c):
    if phase == 0:
        return table.at[:, c["c"] * NX + c["x"], c["y"], pl.ds(c["z"] * 3, 3)]
    if phase == 1:
        return table.at[part, c["c"] * NX + c["x"], c["y"]]
    if part == 0:
        return table.at[0, c["c"] * NX + c["x"]]
    return table.at[1, pl.ds(c["c"] * NX, NX), c["y"]]


def half_span(table, part, c, half):
    if part == 0:
        return table.at[0, c["c"] * NX + c["x"], pl.ds(half * 2, 2)]
    return table.at[1, pl.ds(c["c"] * NX + half * 2, 2), c["y"]]


def leaf_index(leaf):
    right = lax.shift_right_logical
    surf, vol = right(leaf, 1) & 15, right(leaf, 5)
    y = (right(vol, 3) << 1) | (surf & 1)
    return leaf & 1, ((vol & 1) << 2) | (right(vol, 1) & 3), y, right(surf, 1) * 3


def gather_kernel(cand_hbm, points_hbm, shift_hbm, facets_hbm, vol_hbm, listed_ref, disp_ref, target_ref,
                  nodes, facets, mom_own, mom_z, mom_y, mom_c, moments, cols, acc, where,
                  cand_ref, points_ref, shift_ref, facets_ref, vol_ref,
                  in_sem, send_sem, recv_sem, core_send, core_recv, mom_send, mom_recv):
    surf = lax.axis_index("surf")
    me = coords_of(lax.axis_index("vol"), surf)
    sibling = {**me, "c": 1 - me["c"]}
    partners = [sibling]
    for axis, n in SIZES.items():
        partners += [shifted(me, axis, k) for k in range(1, n)]
    barrier = pltpu.get_barrier_semaphore()
    for other in partners:
        pl.semaphore_signal(barrier, inc=1, device_id=mesh_id(other), device_id_type=MESH)
    share = pl.ds(pl.multiple_of(surf * 4 * LANES, 4 * LANES), 4 * LANES)
    inputs = [
        pltpu.make_async_copy(points_hbm, points_ref, in_sem.at[0]),
        pltpu.make_async_copy(shift_hbm, shift_ref, in_sem.at[1]),
        pltpu.make_async_copy(facets_hbm, facets_ref, in_sem.at[2]),
        pltpu.make_async_copy(vol_hbm.at[:, share], vol_ref, in_sem.at[3]),
        pltpu.make_async_copy(cand_hbm, cand_ref, in_sem.at[4]),
    ]
    for copy in inputs:
        copy.start()
    for copy in inputs:
        copy.wait()

    for leaf in range(2):
        own = (leaf, me["c"] * NX + me["x"], me["y"])
        for half in range(2):
            lanes = pl.ds(leaf * LEAF + half * LANES, LANES)
            for c in range(3):
                nodes[(*own, me["z"] * 3 + (2 * c) // 4, pl.ds((2 * c) % 4 + half, 1), slice(None))] = (
                    points_ref[pl.ds(c, 1), lanes]
                )
                nodes[(*own, me["z"] * 3 + (6 + 2 * c) // 4, pl.ds((6 + 2 * c) % 4 + half, 1), slice(None))] = (
                    shift_ref[pl.ds(c, 1), lanes]
                )
        for quarter in range(4):
            lanes = pl.ds(quarter * LANES, LANES)
            for k in range(3):
                facets[(*own, me["z"] * 3 + k, pl.ds(quarter, 1), slice(None))] = (
                    facets_ref[k, pl.ds(leaf, 1), lanes].astype(jnp.float32)
                )
    lane = lax.broadcasted_iota(jnp.int32, (3, LANES), 1)
    my_lane = ((me["c"] * NY + me["y"]) * NZ + me["z"]) * 2
    for row, ref in ((0, points_ref), (3, shift_ref)):
        tile = jnp.zeros((3, LANES), jnp.float32)
        for leaf in range(2):
            mean = jnp.sum(ref[:, pl.ds(leaf * LEAF, LEAF)], axis=1, keepdims=True) * (1.0 / LEAF)
            tile = jnp.where(lane == my_lane + leaf, mean, tile)
        mom_own[pl.ds(row, 3), :] = tile
    mom_own[pl.ds(6, 2), :] = jnp.zeros((2, LANES), jnp.float32)
    pl.semaphore_wait(barrier, len(partners))

    sent = []

    def remote(src, dst, to, s_sem, r_sem):
        return pltpu.make_async_remote_copy(
            src_ref=src, dst_ref=dst, send_sem=s_sem, recv_sem=r_sem,
            device_id=mesh_id(to), device_id_type=MESH,
        )

    def start(copy):
        copy.start()
        sent.append(copy)

    tables = (nodes, facets)

    def sems(which, part, phase, k):
        slot = (part, phase, k)
        return send_sem.at[(which, *slot)], recv_sem.at[(which, *slot)]

    def issue(which, part, phase):
        axis = WAYS[part][phase]
        mine = span(tables[which], part, phase, me)
        for k in (1, 3) if phase == 2 else NEAR_FIRST[SIZES[axis]]:
            start(remote(mine, mine, shifted(me, axis, k), *sems(which, part, phase, k)))

    def collect(which, part, phase, steps=None):
        axis = WAYS[part][phase]
        for k in steps or NEAR_FIRST[SIZES[axis]]:
            frm = shifted(me, axis, -k)
            theirs = span(tables[which], part, phase, frm)
            remote(theirs, theirs, frm, *sems(which, part, phase, k)).wait_recv()

    def forward(which, part, k):
        axis = WAYS[part][2]
        piece = half_span(tables[which], part, shifted(me, axis, -k), k // 2)
        start(remote(piece, piece, shifted(me, axis, k), *sems(which, part, 2, k - 1)))

    def collect_halves(which, part):
        axis = WAYS[part][2]
        for k in (1, 3):
            piece = half_span(tables[which], part, shifted(me, axis, 2), k // 2)
            remote(piece, piece, shifted(me, axis, -k), *sems(which, part, 2, k - 1)).wait_recv()

    def to_sibling(which, part, k):
        mine = span(tables[which], part, 2, shifted(me, WAYS[part][2], -k))
        start(remote(mine, mine, sibling, core_send.at[which, part, k], core_recv.at[which, part, k]))

    def from_sibling(which, part, k):
        theirs = span(tables[which], part, 2, shifted(sibling, WAYS[part][2], -k))
        remote(theirs, theirs, sibling, core_send.at[which, part, k], core_recv.at[which, part, k]).wait_recv()

    def mom_copies(dst, others, slot0):
        return [
            remote(mom_own, dst.at[k], other, mom_send.at[slot0 + k], mom_recv.at[slot0 + k])
            for k, other in enumerate(others)
        ]

    def mom_sum(copies, arrived):
        total = mom_own[...]
        for k, copy in enumerate(copies):
            copy.wait()
            total = total + arrived[k]
        mom_own[...] = total

    issue(0, 0, 0)
    mom = mom_copies(mom_z, [shifted(me, "z", k) for k in range(1, NZ)], 0)
    for copy in mom:
        copy.start()
    issue(1, 0, 0)
    collect(0, 0, 0)
    issue(0, 0, 1)
    issue(0, 1, 1)
    mom_sum(mom, mom_z)
    mom = mom_copies(mom_y, [shifted(me, "y", k) for k in range(1, NY)], 7)
    for copy in mom:
        copy.start()
    collect(1, 0, 0)
    issue(1, 0, 1)
    issue(1, 1, 1)
    for part in range(2):
        collect(0, part, 1)
        issue(0, part, 2)
    for part in range(2):
        to_sibling(0, part, 0)
    mom_sum(mom, mom_y)
    mom = mom_copies(mom_c, [sibling], 10)
    mom[0].start()
    for part in range(2):
        collect(1, part, 1)
    mom_sum(mom, mom_c)
    moments[pl.ds(me["x"], 1)] = mom_own[...][None]
    for k in range(1, NX):
        start(remote(mom_own, moments.at[me["x"]], shifted(me, "x", k), mom_send.at[10 + k], mom_recv.at[10 + k]))
    def locate(n, carry):
        at = leaf_index(jnp.maximum(cand_ref[n % 16, surf * 4 + n // 16], 0))
        for i in range(4):
            where[i, n] = at[i]
        return carry

    lax.fori_loop(0, 64, locate, 0)
    for block in range(4):
        for c in range(3):
            cols[block, c] = as_columns(vol_ref[pl.ds(c, 1), pl.ds(block * LANES, LANES)])
    for k in range(1, NX):
        frm = shifted(me, "x", -k)
        remote(mom_own, moments.at[frm["x"]], frm, mom_send.at[10 + k], mom_recv.at[10 + k]).wait_recv()

    def far(block, carry):
        row = surf * 4 + block
        centers = []
        for x in range(NX):
            ids = leaf_ids(x)
            listed = ids == cand_ref[0, row]
            for j in range(1, 16):
                listed = listed | (ids == cand_ref[j, row])
            centers.append(jnp.where(listed, 0.0, float(LEAF)))
        for g in range(LANES // PG):
            part = pl.ds(g * PG, PG)
            p = [cols[block, c, part, :] for c in range(3)]
            sums = [None] * 4
            for x in range(NX):
                m = moments[x]
                w = weight([m[c:c + 1] - p[c] for c in range(3)]) * centers[x]
                terms = [w * m[3 + c:4 + c] for c in range(3)] + [w]
                sums = terms if x == 0 else [a + b for a, b in zip(sums, terms)]
            for c in range(4):
                acc[block, c, part, :] = sums[c]
        return carry

    lax.fori_loop(0, 4, far, 0)
    for k in (1, 3):
        for part in range(2):
            collect(0, part, 2, (k,))
            forward(0, part, k)
            to_sibling(0, part, k)
    for part in range(2):
        issue(1, part, 2)
    for part in range(2):
        collect_halves(0, part)
        to_sibling(0, part, 2)
    for part in range(2):
        to_sibling(1, part, 0)
        for k in range(4):
            from_sibling(0, part, k)

    def displace(block):
        def near(j, carry):
            n = block * 16 + j
            i0, i1, i2, quad = (where[i, n] for i in range(4))
            push_off = jnp.where(cand_ref[j, surf * 4 + block] >= 0, 0.0, 1e15)
            at = [
                [nodes[i0, i1, i2, quad + (2 * c) // 4, pl.ds((2 * c) % 4 + half, 1), :] for c in range(6)]
                for half in range(2)
            ]
            for half in range(2):
                at[half][0] = at[half][0] + push_off
            for g in range(LANES // PG):
                part = pl.ds(g * PG, PG)
                p = [cols[block, c, part, :] for c in range(3)]
                w = [weight([at[half][c] - p[c] for c in range(3)]) for half in range(2)]
                for c in range(3):
                    acc[block, c, part, :] += w[0] * at[0][3 + c] + w[1] * at[1][3 + c]
                acc[block, 3, part, :] += w[0] + w[1]
            for q in range(3):
                listed_ref[n, q] = nodes[i0, i1, i2, quad + q]
            return carry

        lax.fori_loop(0, 16, near, 0)
        out_lanes = pl.ds(block * LANES, LANES)
        total = [jnp.sum(jnp.transpose(acc[block, c]), axis=0, keepdims=True) for c in range(4)]
        inv = 1.0 / total[3]
        for c in range(3):
            disp = total[c] * inv
            disp_ref[pl.ds(c, 1), out_lanes] = disp
            target_ref[pl.ds(c, 1), out_lanes] = vol_ref[pl.ds(c, 1), out_lanes] + disp

    displace(0)
    for k in (1, 3):
        for part in range(2):
            collect(1, part, 2, (k,))
            forward(1, part, k)
            to_sibling(1, part, k)
    displace(1)
    displace(2)
    for part in range(2):
        collect_halves(1, part)
        to_sibling(1, part, 2)
    displace(3)
    for part in range(2):
        for k in range(4):
            from_sibling(1, part, k)

    def hand_out(n, carry):
        i0, i1, i2, quad = (where[i, n] for i in range(4))
        for q in range(3):
            listed_ref[n, 3 + q] = facets[i0, i1, i2, quad + q]
        return carry

    lax.fori_loop(0, 64, hand_out, 0)
    for copy in sent:
        copy.wait_send()


def displace_and_list(candidates, points, shift, facets, vol):
    f32 = jnp.float32
    vmem = pl.BlockSpec(memory_space=pltpu.VMEM)
    table = pltpu.VMEM((2, 2 * NX, NY, NZ * 3, ROWS, LANES), f32)
    dma = pltpu.SemaphoreType.DMA
    return pl.pallas_call(
        gather_kernel,
        name="displace",
        out_shape=(
            jax.ShapeDtypeStruct((64, 6, ROWS, LANES), f32),
            jax.ShapeDtypeStruct((3, 4 * LANES), f32),
            jax.ShapeDtypeStruct((3, 4 * LANES), f32),
        ),
        in_specs=[pl.BlockSpec(memory_space=pltpu.HBM)] * 5,
        out_specs=(vmem, vmem, vmem),
        scratch_shapes=[
            table,
            table,
            pltpu.VMEM((8, LANES), f32),
            pltpu.VMEM((7, 8, LANES), f32),
            pltpu.VMEM((3, 8, LANES), f32),
            pltpu.VMEM((1, 8, LANES), f32),
            pltpu.VMEM((NX, 8, LANES), f32),
            pltpu.VMEM((4, 3, LANES, LANES), f32),
            pltpu.VMEM((4, 4, LANES, LANES), f32),
            pltpu.SMEM((4, 64), jnp.int32),
            pltpu.SMEM((16, 64), jnp.int32),
            pltpu.VMEM((3, 4 * LANES), f32),
            pltpu.VMEM((3, 4 * LANES), f32),
            pltpu.VMEM((3, 2, 4 * LANES), jnp.int32),
            pltpu.VMEM((3, 4 * LANES), f32),
            dma((5,)),
            dma((2, 2, 3, 8)),
            dma((2, 2, 3, 8)),
            dma((2, 2, 4)),
            dma((2, 2, 4)),
            dma((14,)),
            dma((14,)),
        ],
        compiler_params=pltpu.CompilerParams(
            collective_id=0, has_side_effects=True, vmem_limit_bytes=24 * 2**20
        ),
    )(candidates, points, shift, facets, vol)


def dot3(a, b):
    return a[0] * b[0] + a[1] * b[1] + a[2] * b[2]


def minus3(a, b):
    return [a[0] - b[0], a[1] - b[1], a[2] - b[2]]


def cross3(a, b):
    return [a[1] * b[2] - a[2] * b[1], a[2] * b[0] - a[0] * b[2], a[0] * b[1] - a[1] * b[0]]


def leaf_ids(x):
    lane = lax.broadcasted_iota(jnp.int32, (1, LANES), 1)
    z = (lane // 2) % NZ
    y = (lane // (2 * NZ)) % NY
    core = lane // (2 * NZ * NY)
    vol = ((y // 2) * NX + x) * 2 + core
    return (vol * 16 + z * 2 + y % 2) * 2 + lane % 2


margin = 1e-4
PG = 32


def facet_constants(a, b, c):
    ab, ac = minus3(b, a), minus3(c, a)
    normal = cross3(ab, ac)
    ab_len = jnp.sqrt(dot3(ab, ab))
    inv_ab = 1.0 / ab_len
    inv_n = lax.rsqrt(dot3(normal, normal))
    e1 = [q * inv_ab for q in ab]
    n = [q * inv_n for q in normal]
    e2 = cross3(n, e1)
    cx, cy = dot3(ac, e1), dot3(ac, e2)
    bc_x = cx - ab_len
    bc_len = jnp.sqrt(bc_x * bc_x + cy * cy)
    ac_len = jnp.sqrt(cx * cx + cy * cy)
    inv_bc, inv_ac = 1.0 / bc_len, 1.0 / ac_len
    bx, by = bc_x * inv_bc, cy * inv_bc
    ax, ay = cx * inv_ac, cy * inv_ac
    return [*e1, -dot3(e1, a), *e2, -dot3(e2, a), *n, -dot3(n, a),
            ab_len, bx, by, bx * ab_len, by * ab_len, bc_len, ax, ay, ac_len]


def facet_square(p, k):
    px, py, pz = p
    u = px * k[0] + py * k[1] + (pz * k[2] + k[3])
    v = px * k[4] + py * k[5] + (pz * k[6] + k[7])
    h = px * k[8] + py * k[9] + (pz * k[10] + k[11])
    ab, bx, by, bxl, byl, bc, ax, ay, ac = k[12:21]
    r1 = u - jnp.clip(u, 0.0, ab)
    t2 = bx * u + by * v - bxl
    s2 = bx * v - by * u + byl
    r2 = t2 - jnp.clip(t2, 0.0, bc)
    t3 = ax * u + ay * v
    s3 = ay * u - ax * v
    r3 = t3 - jnp.clip(t3, 0.0, ac)
    edge = jnp.minimum(jnp.minimum(r1 * r1 + v * v, r2 * r2 + s2 * s2), r3 * r3 + s3 * s3)
    inside = jnp.minimum(jnp.minimum(v, s2), s3) >= 0.0
    return h * h + jnp.where(inside, 0.0, edge)


def weight(d):
    q = dot3(d, d) + smoothing
    inv = pl.reciprocal(q, approx=True)
    inv = inv * (2.0 - q * inv)
    return inv * inv


def as_columns(row):
    return jnp.transpose(jnp.broadcast_to(row, (LANES, LANES)))


def wall_kernel(cand_hbm, listed_ref, disp_in, target_ref, flag_ref, disp_ref, wall_ref,
                cols, moved, index, const, best, cand_ref, in_sem):
    surf = lax.axis_index("surf")
    copy = pltpu.make_async_copy(cand_hbm, cand_ref, in_sem)
    copy.start()
    disp_ref[...] = disp_in[...]
    copy.wait()

    def one_block(block, carry):
        row = surf * 4 + block
        lanes = pl.ds(pl.multiple_of(block * LANES, LANES), LANES)
        count = jnp.int32(0)
        for j in range(16):
            count += (cand_ref[j, row] >= 0).astype(jnp.int32)
        flags = flag_ref[pl.ds(row, 1), :]
        flagged = jnp.max(flags) > 0
        wall_ref[pl.ds(block, 1), :] = jnp.zeros((1, LANES), jnp.float32)

        @pl.when(flagged)
        def _():
            targets = [target_ref[pl.ds(c, 1), lanes] for c in range(3)]
            for c in range(3):
                cols[c] = as_columns(targets[c])

            def fetch(j, carry):
                here = pl.ds(j, 1)
                rows = block * 16 + j
                for half in range(2):
                    at = [listed_ref[rows, (2 * c) // 4, pl.ds((2 * c) % 4 + half, 1), :] for c in range(6)]
                    for c in range(3):
                        moved[c, half, here, :] = at[c] + at[3 + c]
                for k in range(3):
                    for quarter in range(4):
                        index[k, quarter, here, :] = listed_ref[rows, 3 + k, pl.ds(quarter, 1), :].astype(jnp.int32)
                return carry

            lax.fori_loop(0, 16, fetch, 0)
            for quarter in range(4):
                corners = []
                for k in range(3):
                    where = index[k, quarter]
                    low = where % LANES
                    corner = []
                    for c in range(3):
                        lo = jnp.take_along_axis(moved[c, 0], low, axis=1, mode="promise_in_bounds")
                        hi = jnp.take_along_axis(moved[c, 1], low, axis=1, mode="promise_in_bounds")
                        corner.append(jnp.where(where < LANES, lo, hi))
                    corners.append(corner)
                for i, value in enumerate(facet_constants(*corners)):
                    const[i, quarter] = value
            best[...] = jnp.full((LANES, LANES), big_value, jnp.float32)

            def one_leaf(j):
                for quarter in range(4):
                    k = [jnp.broadcast_to(const[i, quarter, pl.ds(j, 1), :], (8, LANES)) for i in range(21)]
                    for g in range(16):
                        part = pl.ds(g * 8, 8)
                        p = [cols[c, part, :] for c in range(3)]
                        best[part, :] = jnp.minimum(best[part, :], facet_square(p, k))

            slot = lax.broadcasted_iota(jnp.int32, (16, 1), 0)
            middle = [
                jnp.sum(moved[c, 0] + moved[c, 1], axis=1, keepdims=True) * (1.0 / LEAF) for c in range(3)
            ]
            spread = [
                sum((moved[c, half] - middle[c]) * (moved[c, half] - middle[c]) for c in range(3))
                for half in range(2)
            ]
            radius = jnp.sqrt(jnp.max(jnp.maximum(*spread), axis=1, keepdims=True)) + margin
            away = [middle[c] - targets[c] for c in range(3)]
            away = jnp.sqrt(dot3(away, away))
            valid = slot < count
            lower = jnp.maximum(away - radius, 0.0)
            lower = jnp.where(valid & (flags == 1), lower * lower, big_value)
            upper = jnp.where(valid, away + radius, 1e15)
            upper = jnp.min(upper * upper, axis=0, keepdims=True)
            rank = jnp.sum(jnp.where(flags == 1, away, 0.0), axis=1, keepdims=True)
            rank = jnp.where(valid, rank, big_value)

            def nearest_slot(rank):
                low = jnp.min(rank, axis=0, keepdims=True)
                return jnp.min(jnp.where(rank == low, slot, 15))

            def so_far():
                return jnp.min(jnp.transpose(best[...]), axis=0, keepdims=True)

            def wanted(open_):
                below = lower < jnp.minimum(so_far(), upper)
                hit = jnp.max(jnp.where(below, 1.0, 0.0), axis=1, keepdims=True)
                return jnp.where(open_, hit, 0.0)

            first = nearest_slot(rank)
            one_leaf(first)
            open_ = slot != first
            hit = wanted(open_)

            @pl.when(jnp.max(hit) > 0.0)
            def _():
                second = nearest_slot(jnp.where(hit > 0.0, rank, big_value))
                one_leaf(second)
                rest = wanted(open_ & (slot != second))
                bits = jnp.sum(jnp.where(rest > 0.0, lax.shift_left(jnp.ones_like(slot), slot), 0))

                def perhaps(j, carry):
                    @pl.when(lax.shift_right_logical(bits, j) % 2 == 1)
                    def _():
                        one_leaf(j)

                    return carry

                lax.fori_loop(0, count, perhaps, 0)

            wall_ref[pl.ds(block, 1), :] = jnp.where(flags == 1, jnp.sqrt(so_far()), 0.0)

        return carry

    lax.fori_loop(0, 4, one_block, 0)


def wall(candidates, listed, disp, target, flags):
    f32 = jnp.float32
    vmem = pl.BlockSpec(memory_space=pltpu.VMEM)
    return pl.pallas_call(
        wall_kernel,
        name="wall",
        out_shape=(
            jax.ShapeDtypeStruct((3, 4 * LANES), f32),
            jax.ShapeDtypeStruct((4, LANES), f32),
        ),
        in_specs=[pl.BlockSpec(memory_space=pltpu.HBM), vmem, vmem, vmem, vmem],
        out_specs=(vmem, vmem),
        scratch_shapes=[
            pltpu.VMEM((3, LANES, LANES), f32),
            pltpu.VMEM((3, 2, 16, LANES), f32),
            pltpu.VMEM((3, 4, 16, LANES), jnp.int32),
            pltpu.VMEM((21, 4, 16, LANES), f32),
            pltpu.VMEM((LANES, LANES), f32),
            pltpu.SMEM((16, 64), jnp.int32),
            pltpu.SemaphoreType.DMA,
        ],
        compiler_params=pltpu.CompilerParams(vmem_limit_bytes=24 * 2**20),
    )(candidates, listed, disp, target, flags)


def body(surface_points, surface_shift, facet_nodes, volume_points, near_wall, candidates):
    candidates = candidates.T
    listed, disp, target = displace_and_list(
        candidates, surface_points, surface_shift, jnp.transpose(facet_nodes, (1, 0, 2)), volume_points
    )
    flags = near_wall.reshape(-1, LANES)
    displacement, distance = wall(candidates, listed, disp, target, flags)
    return displacement, distance.reshape(-1)


def solution(mesh):
    placed = (
        P(None, ("vol", "surf")),
        P(None, ("vol", "surf")),
        P(("vol", "surf"), None, None),
        P(None, "vol"),
        P("vol"),
        P("vol", None),
    )
    return jax.shard_map(
        body,
        mesh=mesh,
        in_specs=placed,
        out_specs=(P(None, ("vol", "surf")), P(("vol", "surf"))),
        check_vma=False,
    )
```

```python
import jax
import jax.numpy as jnp
from jax import lax
from jax.experimental import pallas as pl
from jax.experimental.pallas import tpu as pltpu
from jax.sharding import PartitionSpec as P

MESH = pl.DeviceIdType.MESH
smoothing = 0.01
big_value = 1e30

NX, NY, NZ = 4, 4, 8
SIZES = {"x": NX, "y": NY, "z": NZ}
LEAF = 256
CHIPS = NX * NY * NZ
LANES = 128
ROWS = 4


def coords_of(vol, surf):
    return {
        "x": (vol // 2) % NX,
        "y": (vol // (2 * NX)) * 2 + surf % 2,
        "z": surf // 2,
        "c": vol % 2,
    }


def mesh_id(c):
    return ((c["y"] // 2) * NX + c["x"]) * 2 + c["c"], c["z"] * 2 + c["y"] % 2


def shifted(c, axis, k):
    n = SIZES[axis]
    return {**c, axis: lax.rem(c[axis] + (k % n), n)}


WAYS = (("z", "y", "x"), ("z", "x", "y"))
NEAR_FIRST = {4: (1, 3, 2), 8: (1, 7, 2, 6, 3, 5, 4)}


def span(table, part, phase, c):
    if phase == 0:
        return table.at[:, c["c"] * NX + c["x"], c["y"], pl.ds(c["z"] * 3, 3)]
    if phase == 1:
        return table.at[part, c["c"] * NX + c["x"], c["y"]]
    if part == 0:
        return table.at[0, c["c"] * NX + c["x"]]
    return table.at[1, pl.ds(c["c"] * NX, NX), c["y"]]


def half_span(table, part, c, half):
    if part == 0:
        return table.at[0, c["c"] * NX + c["x"], pl.ds(half * 2, 2)]
    return table.at[1, pl.ds(c["c"] * NX + half * 2, 2), c["y"]]


def leaf_index(leaf):
    right = lax.shift_right_logical
    surf, vol = right(leaf, 1) & 15, right(leaf, 5)
    y = (right(vol, 3) << 1) | (surf & 1)
    return leaf & 1, ((vol & 1) << 2) | (right(vol, 1) & 3), y, right(surf, 1) * 3


def gather_kernel(cand_hbm, points_hbm, shift_hbm, facets_hbm, vol_hbm, listed_ref, disp_ref, target_ref,
                  nodes, facets, mom_own, mom_z, mom_y, mom_c, moments, cols, acc, where,
                  cand_ref, points_ref, shift_ref, facets_ref, vol_ref,
                  in_sem, send_sem, recv_sem, core_send, core_recv, mom_send, mom_recv):
    surf = lax.axis_index("surf")
    me = coords_of(lax.axis_index("vol"), surf)
    sibling = {**me, "c": 1 - me["c"]}
    partners = [sibling]
    for axis, n in SIZES.items():
        partners += [shifted(me, axis, k) for k in range(1, n)]
    barrier = pltpu.get_barrier_semaphore()
    for other in partners:
        pl.semaphore_signal(barrier, inc=1, device_id=mesh_id(other), device_id_type=MESH)
    share = pl.ds(pl.multiple_of(surf * 4 * LANES, 4 * LANES), 4 * LANES)
    inputs = [
        pltpu.make_async_copy(points_hbm, points_ref, in_sem.at[0]),
        pltpu.make_async_copy(shift_hbm, shift_ref, in_sem.at[1]),
        pltpu.make_async_copy(facets_hbm, facets_ref, in_sem.at[2]),
        pltpu.make_async_copy(vol_hbm.at[:, share], vol_ref, in_sem.at[3]),
        pltpu.make_async_copy(cand_hbm, cand_ref, in_sem.at[4]),
    ]
    for copy in inputs:
        copy.start()
    for copy in inputs:
        copy.wait()

    for leaf in range(2):
        own = (leaf, me["c"] * NX + me["x"], me["y"])
        for half in range(2):
            lanes = pl.ds(leaf * LEAF + half * LANES, LANES)
            for c in range(3):
                nodes[(*own, me["z"] * 3 + (2 * c) // 4, pl.ds((2 * c) % 4 + half, 1), slice(None))] = (
                    points_ref[pl.ds(c, 1), lanes]
                )
                nodes[(*own, me["z"] * 3 + (6 + 2 * c) // 4, pl.ds((6 + 2 * c) % 4 + half, 1), slice(None))] = (
                    shift_ref[pl.ds(c, 1), lanes]
                )
        for quarter in range(4):
            lanes = pl.ds(quarter * LANES, LANES)
            for k in range(3):
                facets[(*own, me["z"] * 3 + k, pl.ds(quarter, 1), slice(None))] = (
                    facets_ref[k, pl.ds(leaf, 1), lanes].astype(jnp.float32)
                )
    lane = lax.broadcasted_iota(jnp.int32, (3, LANES), 1)
    my_lane = ((me["c"] * NY + me["y"]) * NZ + me["z"]) * 2
    for row, ref in ((0, points_ref), (3, shift_ref)):
        tile = jnp.zeros((3, LANES), jnp.float32)
        for leaf in range(2):
            mean = jnp.sum(ref[:, pl.ds(leaf * LEAF, LEAF)], axis=1, keepdims=True) * (1.0 / LEAF)
            tile = jnp.where(lane == my_lane + leaf, mean, tile)
        mom_own[pl.ds(row, 3), :] = tile
    mom_own[pl.ds(6, 2), :] = jnp.zeros((2, LANES), jnp.float32)
    pl.semaphore_wait(barrier, len(partners))

    sent = []

    def remote(src, dst, to, s_sem, r_sem):
        return pltpu.make_async_remote_copy(
            src_ref=src, dst_ref=dst, send_sem=s_sem, recv_sem=r_sem,
            device_id=mesh_id(to), device_id_type=MESH,
        )

    def start(copy):
        copy.start()
        sent.append(copy)

    tables = (nodes, facets)

    def sems(which, part, phase, k):
        slot = (part, phase, k)
        return send_sem.at[(which, *slot)], recv_sem.at[(which, *slot)]

    def issue(which, part, phase):
        axis = WAYS[part][phase]
        mine = span(tables[which], part, phase, me)
        if phase == 2:
            for turn in range(2):
                for k in (1, 3):
                    piece = half_span(tables[which], part, me, (k // 2) ^ turn)
                    start(remote(piece, piece, shifted(me, axis, k), *sems(which, part, 2, k + 4 * turn - 1)))
            return
        for k in NEAR_FIRST[SIZES[axis]]:
            start(remote(mine, mine, shifted(me, axis, k), *sems(which, part, phase, k)))

    def collect(which, part, phase):
        axis = WAYS[part][phase]
        for k in NEAR_FIRST[SIZES[axis]]:
            frm = shifted(me, axis, -k)
            theirs = span(tables[which], part, phase, frm)
            remote(theirs, theirs, frm, *sems(which, part, phase, k)).wait_recv()

    def collect_turn(which, part, k, turn):
        axis = WAYS[part][2]
        frm = shifted(me, axis, -k)
        piece = half_span(tables[which], part, frm, (k // 2) ^ turn)
        remote(piece, piece, frm, *sems(which, part, 2, k + 4 * turn - 1)).wait_recv()

    def forward(which, part, k):
        axis = WAYS[part][2]
        piece = half_span(tables[which], part, shifted(me, axis, -k), k // 2)
        start(remote(piece, piece, shifted(me, axis, k), *sems(which, part, 2, k)))

    def pass_on(which):
        for k in (1, 3):
            for part in range(2):
                collect_turn(which, part, k, 0)
                forward(which, part, k)

    def take_rest(which):
        for k in (1, 3):
            for part in range(2):
                collect_turn(which, part, k, 1)
                to_sibling(which, part, k)

    def collect_halves(which, part):
        axis = WAYS[part][2]
        for k in (1, 3):
            piece = half_span(tables[which], part, shifted(me, axis, 2), k // 2)
            remote(piece, piece, shifted(me, axis, -k), *sems(which, part, 2, k)).wait_recv()

    def to_sibling(which, part, k):
        mine = span(tables[which], part, 2, shifted(me, WAYS[part][2], -k))
        start(remote(mine, mine, sibling, core_send.at[which, part, k], core_recv.at[which, part, k]))

    def from_sibling(which, part, k):
        theirs = span(tables[which], part, 2, shifted(sibling, WAYS[part][2], -k))
        remote(theirs, theirs, sibling, core_send.at[which, part, k], core_recv.at[which, part, k]).wait_recv()

    def mom_copies(dst, others, slot0):
        return [
            remote(mom_own, dst.at[k], other, mom_send.at[slot0 + k], mom_recv.at[slot0 + k])
            for k, other in enumerate(others)
        ]

    def mom_sum(copies, arrived):
        total = mom_own[...]
        for k, copy in enumerate(copies):
            copy.wait()
            total = total + arrived[k]
        mom_own[...] = total

    issue(0, 0, 0)
    mom = mom_copies(mom_z, [shifted(me, "z", k) for k in range(1, NZ)], 0)
    for copy in mom:
        copy.start()
    issue(1, 0, 0)
    collect(0, 0, 0)
    issue(0, 0, 1)
    issue(0, 1, 1)
    mom_sum(mom, mom_z)
    mom = mom_copies(mom_y, [shifted(me, "y", k) for k in range(1, NY)], 7)
    for copy in mom:
        copy.start()
    collect(1, 0, 0)
    issue(1, 0, 1)
    issue(1, 1, 1)
    for part in range(2):
        collect(0, part, 1)
        issue(0, part, 2)
    for part in range(2):
        to_sibling(0, part, 0)
    mom_sum(mom, mom_y)
    mom = mom_copies(mom_c, [sibling], 10)
    mom[0].start()
    for part in range(2):
        collect(1, part, 1)
    mom_sum(mom, mom_c)
    moments[pl.ds(me["x"], 1)] = mom_own[...][None]
    for k in range(1, NX):
        start(remote(mom_own, moments.at[me["x"]], shifted(me, "x", k), mom_send.at[10 + k], mom_recv.at[10 + k]))
    def locate(n, carry):
        at = leaf_index(jnp.maximum(cand_ref[n % 16, surf * 4 + n // 16], 0))
        for i in range(4):
            where[i, n] = at[i]
        return carry

    lax.fori_loop(0, 64, locate, 0)
    for block in range(4):
        for c in range(3):
            cols[block, c] = as_columns(vol_ref[pl.ds(c, 1), pl.ds(block * LANES, LANES)])
    for k in range(1, NX):
        frm = shifted(me, "x", -k)
        remote(mom_own, moments.at[frm["x"]], frm, mom_send.at[10 + k], mom_recv.at[10 + k]).wait_recv()

    def far(block, carry):
        row = surf * 4 + block
        centers = []
        for x in range(NX):
            ids = leaf_ids(x)
            listed = ids == cand_ref[0, row]
            for j in range(1, 16):
                listed = listed | (ids == cand_ref[j, row])
            centers.append(jnp.where(listed, 0.0, float(LEAF)))
        for g in range(LANES // PG):
            part = pl.ds(g * PG, PG)
            p = [cols[block, c, part, :] for c in range(3)]
            sums = [None] * 4
            for x in range(NX):
                m = moments[x]
                w = weight([m[c:c + 1] - p[c] for c in range(3)]) * centers[x]
                terms = [w * m[3 + c:4 + c] for c in range(3)] + [w]
                sums = terms if x == 0 else [a + b for a, b in zip(sums, terms)]
            for c in range(4):
                acc[block, c, part, :] = sums[c]
        return carry

    lax.fori_loop(0, 4, far, 0)
    pass_on(0)
    take_rest(0)
    for part in range(2):
        issue(1, part, 2)
    for part in range(2):
        collect_halves(0, part)
        to_sibling(0, part, 2)
    for part in range(2):
        to_sibling(1, part, 0)
        for k in range(4):
            from_sibling(0, part, k)

    def displace(block):
        def near(j, carry):
            n = block * 16 + j
            i0, i1, i2, quad = (where[i, n] for i in range(4))
            push_off = jnp.where(cand_ref[j, surf * 4 + block] >= 0, 0.0, 1e15)
            at = [
                [nodes[i0, i1, i2, quad + (2 * c) // 4, pl.ds((2 * c) % 4 + half, 1), :] for c in range(6)]
                for half in range(2)
            ]
            for half in range(2):
                at[half][0] = at[half][0] + push_off
            for g in range(LANES // PG):
                part = pl.ds(g * PG, PG)
                p = [cols[block, c, part, :] for c in range(3)]
                w = [weight([at[half][c] - p[c] for c in range(3)]) for half in range(2)]
                for c in range(3):
                    acc[block, c, part, :] += w[0] * at[0][3 + c] + w[1] * at[1][3 + c]
                acc[block, 3, part, :] += w[0] + w[1]
            for q in range(3):
                listed_ref[n, q] = nodes[i0, i1, i2, quad + q]
            return carry

        lax.fori_loop(0, 16, near, 0)
        out_lanes = pl.ds(block * LANES, LANES)
        total = [jnp.sum(jnp.transpose(acc[block, c]), axis=0, keepdims=True) for c in range(4)]
        inv = 1.0 / total[3]
        for c in range(3):
            disp = total[c] * inv
            disp_ref[pl.ds(c, 1), out_lanes] = disp
            target_ref[pl.ds(c, 1), out_lanes] = vol_ref[pl.ds(c, 1), out_lanes] + disp

    displace(0)
    pass_on(1)
    take_rest(1)
    displace(1)
    displace(2)
    for part in range(2):
        collect_halves(1, part)
        to_sibling(1, part, 2)
    displace(3)
    for part in range(2):
        for k in range(4):
            from_sibling(1, part, k)

    def hand_out(n, carry):
        i0, i1, i2, quad = (where[i, n] for i in range(4))
        for q in range(3):
            listed_ref[n, 3 + q] = facets[i0, i1, i2, quad + q]
        return carry

    lax.fori_loop(0, 64, hand_out, 0)
    for copy in sent:
        copy.wait_send()


def displace_and_list(candidates, points, shift, facets, vol):
    f32 = jnp.float32
    vmem = pl.BlockSpec(memory_space=pltpu.VMEM)
    table = pltpu.VMEM((2, 2 * NX, NY, NZ * 3, ROWS, LANES), f32)
    dma = pltpu.SemaphoreType.DMA
    return pl.pallas_call(
        gather_kernel,
        name="displace",
        out_shape=(
            jax.ShapeDtypeStruct((64, 6, ROWS, LANES), f32),
            jax.ShapeDtypeStruct((3, 4 * LANES), f32),
            jax.ShapeDtypeStruct((3, 4 * LANES), f32),
        ),
        in_specs=[pl.BlockSpec(memory_space=pltpu.HBM)] * 5,
        out_specs=(vmem, vmem, vmem),
        scratch_shapes=[
            table,
            table,
            pltpu.VMEM((8, LANES), f32),
            pltpu.VMEM((7, 8, LANES), f32),
            pltpu.VMEM((3, 8, LANES), f32),
            pltpu.VMEM((1, 8, LANES), f32),
            pltpu.VMEM((NX, 8, LANES), f32),
            pltpu.VMEM((4, 3, LANES, LANES), f32),
            pltpu.VMEM((4, 4, LANES, LANES), f32),
            pltpu.SMEM((4, 64), jnp.int32),
            pltpu.SMEM((16, 64), jnp.int32),
            pltpu.VMEM((3, 4 * LANES), f32),
            pltpu.VMEM((3, 4 * LANES), f32),
            pltpu.VMEM((3, 2, 4 * LANES), jnp.int32),
            pltpu.VMEM((3, 4 * LANES), f32),
            dma((5,)),
            dma((2, 2, 3, 8)),
            dma((2, 2, 3, 8)),
            dma((2, 2, 4)),
            dma((2, 2, 4)),
            dma((14,)),
            dma((14,)),
        ],
        compiler_params=pltpu.CompilerParams(
            collective_id=0, has_side_effects=True, vmem_limit_bytes=60 * 2**20
        ),
    )(candidates, points, shift, facets, vol)


def dot3(a, b):
    return a[0] * b[0] + a[1] * b[1] + a[2] * b[2]


def minus3(a, b):
    return [a[0] - b[0], a[1] - b[1], a[2] - b[2]]


def cross3(a, b):
    return [a[1] * b[2] - a[2] * b[1], a[2] * b[0] - a[0] * b[2], a[0] * b[1] - a[1] * b[0]]


def leaf_ids(x):
    lane = lax.broadcasted_iota(jnp.int32, (1, LANES), 1)
    z = (lane // 2) % NZ
    y = (lane // (2 * NZ)) % NY
    core = lane // (2 * NZ * NY)
    vol = ((y // 2) * NX + x) * 2 + core
    return (vol * 16 + z * 2 + y % 2) * 2 + lane % 2


margin = 1e-4
PG = 32


def facet_constants(a, b, c):
    ab, ac = minus3(b, a), minus3(c, a)
    normal = cross3(ab, ac)
    ab_len = jnp.sqrt(dot3(ab, ab))
    inv_ab = 1.0 / ab_len
    inv_n = lax.rsqrt(dot3(normal, normal))
    e1 = [q * inv_ab for q in ab]
    n = [q * inv_n for q in normal]
    e2 = cross3(n, e1)
    cx, cy = dot3(ac, e1), dot3(ac, e2)
    bc_x = cx - ab_len
    bc_len = jnp.sqrt(bc_x * bc_x + cy * cy)
    ac_len = jnp.sqrt(cx * cx + cy * cy)
    inv_bc, inv_ac = 1.0 / bc_len, 1.0 / ac_len
    bx, by = bc_x * inv_bc, cy * inv_bc
    ax, ay = cx * inv_ac, cy * inv_ac
    return [*e1, -dot3(e1, a), *e2, -dot3(e2, a), *n, -dot3(n, a),
            ab_len, bx, by, bc_len, ax, ay, ac_len]


def facet_square(p, k):
    px, py, pz = p
    u = px * k[0] + py * k[1] + (pz * k[2] + k[3])
    v = px * k[4] + py * k[5] + (pz * k[6] + k[7])
    h = px * k[8] + py * k[9] + (pz * k[10] + k[11])
    ab, bx, by, bc, ax, ay, ac = k[12:]
    past = u - ab
    r1 = jnp.maximum(jnp.maximum(past, -u), 0.0)
    t2 = bx * past + by * v
    s2 = bx * v - by * past
    r2 = t2 - jnp.clip(t2, 0.0, bc)
    t3 = ax * u + ay * v
    s3 = ay * u - ax * v
    r3 = t3 - jnp.clip(t3, 0.0, ac)
    edge = jnp.minimum(jnp.minimum(r1 * r1 + v * v, r2 * r2 + s2 * s2), r3 * r3 + s3 * s3)
    inside = jnp.minimum(jnp.minimum(v, s2), s3) >= 0.0
    return h * h + jnp.where(inside, 0.0, edge)


def weight(d):
    q = dot3(d, d) + smoothing
    inv = pl.reciprocal(q, approx=True)
    inv = inv * (2.0 - q * inv)
    return inv * inv


def as_columns(row):
    return jnp.transpose(jnp.broadcast_to(row, (LANES, LANES)))


def wall_kernel(cand_hbm, listed_hbm, target_hbm, flag_hbm, wall_ref,
                cols, moved, index, const, best, cand_ref, listed_ref, target_ref, flag_ref, in_sem):
    surf = lax.axis_index("surf")
    inputs = [
        pltpu.make_async_copy(cand_hbm, cand_ref, in_sem.at[0]),
        pltpu.make_async_copy(listed_hbm, listed_ref, in_sem.at[1]),
        pltpu.make_async_copy(target_hbm, target_ref, in_sem.at[2]),
        pltpu.make_async_copy(flag_hbm, flag_ref, in_sem.at[3]),
    ]
    for copy in inputs:
        copy.start()
    for copy in inputs:
        copy.wait()

    def one_block(block, carry):
        row = surf * 4 + block
        lanes = pl.ds(pl.multiple_of(block * LANES, LANES), LANES)
        count = jnp.int32(0)
        for j in range(16):
            count += (cand_ref[j, row] >= 0).astype(jnp.int32)
        flags = flag_ref[pl.ds(row, 1), :]
        flagged = jnp.max(flags) > 0
        wall_ref[pl.ds(block, 1), :] = jnp.zeros((1, LANES), jnp.float32)

        @pl.when(flagged)
        def _():
            targets = [target_ref[pl.ds(c, 1), lanes] for c in range(3)]
            for c in range(3):
                cols[c] = as_columns(targets[c])

            def fetch(j, carry):
                here = pl.ds(j, 1)
                rows = block * 16 + j
                for half in range(2):
                    at = [listed_ref[rows, (2 * c) // 4, pl.ds((2 * c) % 4 + half, 1), :] for c in range(6)]
                    for c in range(3):
                        moved[c, half, here, :] = at[c] + at[3 + c]
                for k in range(3):
                    for quarter in range(4):
                        index[k, quarter, here, :] = listed_ref[rows, 3 + k, pl.ds(quarter, 1), :].astype(jnp.int32)
                return carry

            lax.fori_loop(0, 16, fetch, 0)
            for quarter in range(4):
                corners = []
                for k in range(3):
                    where = index[k, quarter]
                    low = where % LANES
                    corner = []
                    for c in range(3):
                        lo = jnp.take_along_axis(moved[c, 0], low, axis=1, mode="promise_in_bounds")
                        hi = jnp.take_along_axis(moved[c, 1], low, axis=1, mode="promise_in_bounds")
                        corner.append(jnp.where(where < LANES, lo, hi))
                    corners.append(corner)
                for i, value in enumerate(facet_constants(*corners)):
                    const[i, quarter] = value
            best[...] = jnp.full((LANES, LANES), big_value, jnp.float32)

            def one_leaf(j):
                for quarter in range(4):
                    k = [jnp.broadcast_to(const[i, quarter, pl.ds(j, 1), :], (8, LANES)) for i in range(19)]
                    for g in range(16):
                        part = pl.ds(g * 8, 8)
                        p = [cols[c, part, :] for c in range(3)]
                        best[part, :] = jnp.minimum(best[part, :], facet_square(p, k))

            slot = lax.broadcasted_iota(jnp.int32, (16, 1), 0)
            middle = [
                jnp.sum(moved[c, 0] + moved[c, 1], axis=1, keepdims=True) * (1.0 / LEAF) for c in range(3)
            ]
            spread = [
                sum((moved[c, half] - middle[c]) * (moved[c, half] - middle[c]) for c in range(3))
                for half in range(2)
            ]
            radius = jnp.sqrt(jnp.max(jnp.maximum(*spread), axis=1, keepdims=True)) + margin
            away = [middle[c] - targets[c] for c in range(3)]
            away = jnp.sqrt(dot3(away, away))
            valid = slot < count
            lower = jnp.maximum(away - radius, 0.0)
            lower = jnp.where(valid & (flags == 1), lower * lower, big_value)
            upper = jnp.where(valid, away + radius, 1e15)
            upper = jnp.min(upper * upper, axis=0, keepdims=True)
            rank = jnp.sum(jnp.where(flags == 1, away, 0.0), axis=1, keepdims=True)
            rank = jnp.where(valid, rank, big_value)

            def nearest_slot(rank):
                low = jnp.min(rank, axis=0, keepdims=True)
                return jnp.min(jnp.where(rank == low, slot, 15))

            def so_far():
                return jnp.min(jnp.transpose(best[...]), axis=0, keepdims=True)

            def wanted(open_):
                below = lower < jnp.minimum(so_far(), upper)
                hit = jnp.max(jnp.where(below, 1.0, 0.0), axis=1, keepdims=True)
                return jnp.where(open_, hit, 0.0)

            first = nearest_slot(rank)
            one_leaf(first)
            open_ = slot != first
            hit = wanted(open_)

            @pl.when(jnp.max(hit) > 0.0)
            def _():
                second = nearest_slot(jnp.where(hit > 0.0, rank, big_value))
                one_leaf(second)
                rest = wanted(open_ & (slot != second))
                bits = jnp.sum(jnp.where(rest > 0.0, lax.shift_left(jnp.ones_like(slot), slot), 0))

                def perhaps(j, carry):
                    @pl.when(lax.shift_right_logical(bits, j) % 2 == 1)
                    def _():
                        one_leaf(j)

                    return carry

                lax.fori_loop(0, count, perhaps, 0)

            wall_ref[pl.ds(block, 1), :] = jnp.where(flags == 1, jnp.sqrt(so_far()), 0.0)

        return carry

    lax.fori_loop(0, 4, one_block, 0)


def wall(candidates, listed, target, flags):
    f32 = jnp.float32
    return pl.pallas_call(
        wall_kernel,
        name="wall",
        out_shape=jax.ShapeDtypeStruct((4, LANES), f32),
        in_specs=[pl.BlockSpec(memory_space=pltpu.HBM)] * 4,
        out_specs=pl.BlockSpec(memory_space=pltpu.VMEM),
        scratch_shapes=[
            pltpu.VMEM((3, LANES, LANES), f32),
            pltpu.VMEM((3, 2, 16, LANES), f32),
            pltpu.VMEM((3, 4, 16, LANES), jnp.int32),
            pltpu.VMEM((19, 4, 16, LANES), f32),
            pltpu.VMEM((LANES, LANES), f32),
            pltpu.SMEM((16, 64), jnp.int32),
            pltpu.VMEM((64, 6, ROWS, LANES), f32),
            pltpu.VMEM((3, 4 * LANES), f32),
            pltpu.VMEM((64, LANES), jnp.int32),
            pltpu.SemaphoreType.DMA((4,)),
        ],
        compiler_params=pltpu.CompilerParams(vmem_limit_bytes=60 * 2**20),
    )(candidates, listed, target, flags)


def body(surface_points, surface_shift, facet_nodes, volume_points, near_wall, candidates):
    candidates = candidates.T
    listed, displacement, target = displace_and_list(
        candidates, surface_points, surface_shift, jnp.transpose(facet_nodes, (1, 0, 2)), volume_points
    )
    distance = wall(candidates, listed, target, near_wall.reshape(-1, LANES))
    return displacement, distance.reshape(-1)


def solution(mesh):
    placed = (
        P(None, ("vol", "surf")),
        P(None, ("vol", "surf")),
        P(("vol", "surf"), None, None),
        P(None, "vol"),
        P("vol"),
        P("vol", None),
    )
    return jax.shard_map(
        body,
        mesh=mesh,
        in_specs=placed,
        out_specs=(P(None, ("vol", "surf")), P(("vol", "surf"))),
        check_vma=False,
    )
```

```python
import jax
import jax.numpy as jnp
from jax import lax
from jax.experimental import pallas as pl
from jax.experimental.pallas import tpu as pltpu
from jax.sharding import PartitionSpec as P

MESH = pl.DeviceIdType.MESH
smoothing = 0.01
big_value = 1e30

NX, NY, NZ = 4, 4, 8
SIZES = {"x": NX, "y": NY, "z": NZ}
LEAF = 256
CHIPS = NX * NY * NZ
LANES = 128
ROWS = 4


def coords_of(vol, surf):
    return {
        "x": (vol // 2) % NX,
        "y": (vol // (2 * NX)) * 2 + surf % 2,
        "z": surf // 2,
        "c": vol % 2,
    }


def mesh_id(c):
    return ((c["y"] // 2) * NX + c["x"]) * 2 + c["c"], c["z"] * 2 + c["y"] % 2


def shifted(c, axis, k):
    n = SIZES[axis]
    return {**c, axis: lax.rem(c[axis] + (k % n), n)}


WAYS = (("z", "y", "x"), ("z", "x", "y"))
NEAR_FIRST = {4: (1, 3, 2), 8: (1, 7, 2, 6, 3, 5, 4)}


def span(table, part, phase, c):
    if phase == 0:
        return table.at[:, c["c"] * NX + c["x"], c["y"], pl.ds(c["z"] * 3, 3)]
    if phase == 1:
        return table.at[part, c["c"] * NX + c["x"], c["y"]]
    if part == 0:
        return table.at[0, c["c"] * NX + c["x"]]
    return table.at[1, pl.ds(c["c"] * NX, NX), c["y"]]


def half_span(table, part, c, half):
    if part == 0:
        return table.at[0, c["c"] * NX + c["x"], pl.ds(half * 2, 2)]
    return table.at[1, pl.ds(c["c"] * NX + half * 2, 2), c["y"]]


def leaf_index(leaf):
    right = lax.shift_right_logical
    surf, vol = right(leaf, 1) & 15, right(leaf, 5)
    y = (right(vol, 3) << 1) | (surf & 1)
    return leaf & 1, ((vol & 1) << 2) | (right(vol, 1) & 3), y, right(surf, 1) * 3


def gather_kernel(cand_hbm, points_hbm, shift_hbm, facets_hbm, vol_hbm, listed_ref, disp_ref, target_ref,
                  nodes, facets, mom_own, mom_z, mom_y, mom_c, moments, cols, acc, where,
                  cand_ref, points_ref, shift_ref, facets_ref, vol_ref,
                  in_sem, send_sem, recv_sem, core_send, core_recv, mom_send, mom_recv):
    surf = lax.axis_index("surf")
    me = coords_of(lax.axis_index("vol"), surf)
    sibling = {**me, "c": 1 - me["c"]}
    partners = [sibling]
    for axis, n in SIZES.items():
        partners += [shifted(me, axis, k) for k in range(1, n)]
    barrier = pltpu.get_barrier_semaphore()
    for other in partners:
        pl.semaphore_signal(barrier, inc=1, device_id=mesh_id(other), device_id_type=MESH)
    share = pl.ds(pl.multiple_of(surf * 4 * LANES, 4 * LANES), 4 * LANES)
    inputs = [
        pltpu.make_async_copy(points_hbm, points_ref, in_sem.at[0]),
        pltpu.make_async_copy(shift_hbm, shift_ref, in_sem.at[1]),
        pltpu.make_async_copy(facets_hbm, facets_ref, in_sem.at[2]),
        pltpu.make_async_copy(vol_hbm.at[:, share], vol_ref, in_sem.at[3]),
        pltpu.make_async_copy(cand_hbm, cand_ref, in_sem.at[4]),
    ]
    for copy in inputs:
        copy.start()
    for copy in inputs:
        copy.wait()

    for leaf in range(2):
        own = (leaf, me["c"] * NX + me["x"], me["y"])
        for half in range(2):
            lanes = pl.ds(leaf * LEAF + half * LANES, LANES)
            for c in range(3):
                nodes[(*own, me["z"] * 3 + (2 * c) // 4, pl.ds((2 * c) % 4 + half, 1), slice(None))] = (
                    points_ref[pl.ds(c, 1), lanes]
                )
                nodes[(*own, me["z"] * 3 + (6 + 2 * c) // 4, pl.ds((6 + 2 * c) % 4 + half, 1), slice(None))] = (
                    shift_ref[pl.ds(c, 1), lanes]
                )
        for quarter in range(4):
            lanes = pl.ds(quarter * LANES, LANES)
            for k in range(3):
                facets[(*own, me["z"] * 3 + k, pl.ds(quarter, 1), slice(None))] = (
                    facets_ref[k, pl.ds(leaf, 1), lanes].astype(jnp.float32)
                )
    lane = lax.broadcasted_iota(jnp.int32, (3, LANES), 1)
    my_lane = ((me["c"] * NY + me["y"]) * NZ + me["z"]) * 2
    for row, ref in ((0, points_ref), (3, shift_ref)):
        tile = jnp.zeros((3, LANES), jnp.float32)
        for leaf in range(2):
            mean = jnp.sum(ref[:, pl.ds(leaf * LEAF, LEAF)], axis=1, keepdims=True) * (1.0 / LEAF)
            tile = jnp.where(lane == my_lane + leaf, mean, tile)
        mom_own[pl.ds(row, 3), :] = tile
    mom_own[pl.ds(6, 2), :] = jnp.zeros((2, LANES), jnp.float32)
    pl.semaphore_wait(barrier, len(partners))

    sent = []

    def remote(src, dst, to, s_sem, r_sem):
        return pltpu.make_async_remote_copy(
            src_ref=src, dst_ref=dst, send_sem=s_sem, recv_sem=r_sem,
            device_id=mesh_id(to), device_id_type=MESH,
        )

    def start(copy):
        copy.start()
        sent.append(copy)

    tables = (nodes, facets)

    def sems(which, part, phase, k):
        slot = (part, phase, k)
        return send_sem.at[(which, *slot)], recv_sem.at[(which, *slot)]

    def issue(which, part, phase):
        axis = WAYS[part][phase]
        mine = span(tables[which], part, phase, me)
        if phase == 2:
            for turn in range(2):
                for k in (1, 3):
                    piece = half_span(tables[which], part, me, (k // 2) ^ turn)
                    start(remote(piece, piece, shifted(me, axis, k), *sems(which, part, 2, k + 4 * turn - 1)))
            return
        for k in NEAR_FIRST[SIZES[axis]]:
            start(remote(mine, mine, shifted(me, axis, k), *sems(which, part, phase, k)))

    def collect(which, part, phase):
        axis = WAYS[part][phase]
        for k in NEAR_FIRST[SIZES[axis]]:
            frm = shifted(me, axis, -k)
            theirs = span(tables[which], part, phase, frm)
            remote(theirs, theirs, frm, *sems(which, part, phase, k)).wait_recv()

    def collect_turn(which, part, k, turn):
        axis = WAYS[part][2]
        frm = shifted(me, axis, -k)
        piece = half_span(tables[which], part, frm, (k // 2) ^ turn)
        remote(piece, piece, frm, *sems(which, part, 2, k + 4 * turn - 1)).wait_recv()

    def forward(which, part, k):
        axis = WAYS[part][2]
        piece = half_span(tables[which], part, shifted(me, axis, -k), k // 2)
        start(remote(piece, piece, shifted(me, axis, k), *sems(which, part, 2, k)))

    def pass_on(which):
        for k in (1, 3):
            for part in range(2):
                collect_turn(which, part, k, 0)
                forward(which, part, k)

    def take_rest(which):
        for k in (1, 3):
            for part in range(2):
                collect_turn(which, part, k, 1)
                to_sibling(which, part, k)

    def collect_halves(which, part):
        axis = WAYS[part][2]
        for k in (1, 3):
            piece = half_span(tables[which], part, shifted(me, axis, 2), k // 2)
            remote(piece, piece, shifted(me, axis, -k), *sems(which, part, 2, k)).wait_recv()

    def to_sibling(which, part, k):
        mine = span(tables[which], part, 2, shifted(me, WAYS[part][2], -k))
        start(remote(mine, mine, sibling, core_send.at[which, part, k], core_recv.at[which, part, k]))

    def from_sibling(which, part, k):
        theirs = span(tables[which], part, 2, shifted(sibling, WAYS[part][2], -k))
        remote(theirs, theirs, sibling, core_send.at[which, part, k], core_recv.at[which, part, k]).wait_recv()

    def mom_copies(dst, others, slot0):
        return [
            remote(mom_own, dst.at[k], other, mom_send.at[slot0 + k], mom_recv.at[slot0 + k])
            for k, other in enumerate(others)
        ]

    def mom_sum(copies, arrived):
        total = mom_own[...]
        for k, copy in enumerate(copies):
            copy.wait()
            total = total + arrived[k]
        mom_own[...] = total

    issue(0, 0, 0)
    mom = mom_copies(mom_z, [shifted(me, "z", k) for k in range(1, NZ)], 0)
    for copy in mom:
        copy.start()
    issue(1, 0, 0)
    collect(0, 0, 0)
    issue(0, 0, 1)
    issue(0, 1, 1)
    mom_sum(mom, mom_z)
    mom = mom_copies(mom_y, [shifted(me, "y", k) for k in range(1, NY)], 7)
    for copy in mom:
        copy.start()
    collect(1, 0, 0)
    issue(1, 0, 1)
    issue(1, 1, 1)
    for part in range(2):
        collect(0, part, 1)
        issue(0, part, 2)
    for part in range(2):
        to_sibling(0, part, 0)
    mom_sum(mom, mom_y)
    mom = mom_copies(mom_c, [sibling], 10)
    mom[0].start()
    for part in range(2):
        collect(1, part, 1)
    mom_sum(mom, mom_c)
    moments[pl.ds(me["x"], 1)] = mom_own[...][None]
    for k in range(1, NX):
        start(remote(mom_own, moments.at[me["x"]], shifted(me, "x", k), mom_send.at[10 + k], mom_recv.at[10 + k]))
    def locate(n, carry):
        at = leaf_index(jnp.maximum(cand_ref[n % 16, surf * 4 + n // 16], 0))
        for i in range(4):
            where[i, n] = at[i]
        return carry

    lax.fori_loop(0, 64, locate, 0)
    for block in range(4):
        for c in range(3):
            cols[block, c] = as_columns(vol_ref[pl.ds(c, 1), pl.ds(block * LANES, LANES)])
    for k in range(1, NX):
        frm = shifted(me, "x", -k)
        remote(mom_own, moments.at[frm["x"]], frm, mom_send.at[10 + k], mom_recv.at[10 + k]).wait_recv()

    def far(block, carry):
        row = surf * 4 + block
        centers = []
        for x in range(NX):
            ids = leaf_ids(x)
            listed = ids == cand_ref[0, row]
            for j in range(1, 16):
                listed = listed | (ids == cand_ref[j, row])
            centers.append(jnp.where(listed, 0.0, float(LEAF)))
        for g in range(LANES // PG):
            part = pl.ds(g * PG, PG)
            p = [cols[block, c, part, :] for c in range(3)]
            sums = [None] * 4
            for x in range(NX):
                m = moments[x]
                w = weight([m[c:c + 1] - p[c] for c in range(3)]) * centers[x]
                terms = [w * m[3 + c:4 + c] for c in range(3)] + [w]
                sums = terms if x == 0 else [a + b for a, b in zip(sums, terms)]
            for c in range(4):
                acc[block, c, part, :] = sums[c]
        return carry

    lax.fori_loop(0, 4, far, 0)
    pass_on(0)
    take_rest(0)
    for part in range(2):
        issue(1, part, 2)
    for part in range(2):
        collect_halves(0, part)
        to_sibling(0, part, 2)
    for part in range(2):
        to_sibling(1, part, 0)
        for k in range(4):
            from_sibling(0, part, k)

    def displace(block):
        def near(j, carry):
            n = block * 16 + j
            i0, i1, i2, quad = (where[i, n] for i in range(4))
            push_off = jnp.where(cand_ref[j, surf * 4 + block] >= 0, 0.0, 1e15)
            at = [
                [nodes[i0, i1, i2, quad + (2 * c) // 4, pl.ds((2 * c) % 4 + half, 1), :] for c in range(6)]
                for half in range(2)
            ]
            for half in range(2):
                at[half][0] = at[half][0] + push_off
            for g in range(LANES // PG):
                part = pl.ds(g * PG, PG)
                p = [cols[block, c, part, :] for c in range(3)]
                w = [weight([at[half][c] - p[c] for c in range(3)]) for half in range(2)]
                for c in range(3):
                    acc[block, c, part, :] += w[0] * at[0][3 + c] + w[1] * at[1][3 + c]
                acc[block, 3, part, :] += w[0] + w[1]
            for q in range(3):
                listed_ref[n, q] = nodes[i0, i1, i2, quad + q]
            return carry

        lax.fori_loop(0, 16, near, 0)
        out_lanes = pl.ds(block * LANES, LANES)
        total = [jnp.sum(jnp.transpose(acc[block, c]), axis=0, keepdims=True) for c in range(4)]
        inv = 1.0 / total[3]
        for c in range(3):
            disp = total[c] * inv
            disp_ref[pl.ds(c, 1), out_lanes] = disp
            target_ref[pl.ds(c, 1), out_lanes] = vol_ref[pl.ds(c, 1), out_lanes] + disp

    displace(0)
    pass_on(1)
    take_rest(1)
    displace(1)
    displace(2)
    for part in range(2):
        collect_halves(1, part)
        to_sibling(1, part, 2)
    displace(3)
    for part in range(2):
        for k in range(4):
            from_sibling(1, part, k)

    def hand_out(n, carry):
        i0, i1, i2, quad = (where[i, n] for i in range(4))
        for q in range(3):
            listed_ref[n, 3 + q] = facets[i0, i1, i2, quad + q]
        return carry

    lax.fori_loop(0, 64, hand_out, 0)
    for copy in sent:
        copy.wait_send()


def displace_and_list(candidates, points, shift, facets, vol):
    f32 = jnp.float32
    vmem = pl.BlockSpec(memory_space=pltpu.VMEM)
    table = pltpu.VMEM((2, 2 * NX, NY, NZ * 3, ROWS, LANES), f32)
    dma = pltpu.SemaphoreType.DMA
    return pl.pallas_call(
        gather_kernel,
        name="displace",
        out_shape=(
            jax.ShapeDtypeStruct((64, 6, ROWS, LANES), f32),
            jax.ShapeDtypeStruct((3, 4 * LANES), f32),
            jax.ShapeDtypeStruct((3, 4 * LANES), f32),
        ),
        in_specs=[pl.BlockSpec(memory_space=pltpu.HBM)] * 5,
        out_specs=(vmem, vmem, vmem),
        scratch_shapes=[
            table,
            table,
            pltpu.VMEM((8, LANES), f32),
            pltpu.VMEM((7, 8, LANES), f32),
            pltpu.VMEM((3, 8, LANES), f32),
            pltpu.VMEM((1, 8, LANES), f32),
            pltpu.VMEM((NX, 8, LANES), f32),
            pltpu.VMEM((4, 3, LANES, LANES), f32),
            pltpu.VMEM((4, 4, LANES, LANES), f32),
            pltpu.SMEM((4, 64), jnp.int32),
            pltpu.SMEM((16, 64), jnp.int32),
            pltpu.VMEM((3, 4 * LANES), f32),
            pltpu.VMEM((3, 4 * LANES), f32),
            pltpu.VMEM((3, 2, 4 * LANES), jnp.int32),
            pltpu.VMEM((3, 4 * LANES), f32),
            dma((5,)),
            dma((2, 2, 3, 8)),
            dma((2, 2, 3, 8)),
            dma((2, 2, 4)),
            dma((2, 2, 4)),
            dma((14,)),
            dma((14,)),
        ],
        compiler_params=pltpu.CompilerParams(
            collective_id=0, has_side_effects=True, vmem_limit_bytes=60 * 2**20
        ),
    )(candidates, points, shift, facets, vol)


def dot3(a, b):
    return a[0] * b[0] + a[1] * b[1] + a[2] * b[2]


def minus3(a, b):
    return [a[0] - b[0], a[1] - b[1], a[2] - b[2]]


def cross3(a, b):
    return [a[1] * b[2] - a[2] * b[1], a[2] * b[0] - a[0] * b[2], a[0] * b[1] - a[1] * b[0]]


def leaf_ids(x):
    lane = lax.broadcasted_iota(jnp.int32, (1, LANES), 1)
    z = (lane // 2) % NZ
    y = (lane // (2 * NZ)) % NY
    core = lane // (2 * NZ * NY)
    vol = ((y // 2) * NX + x) * 2 + core
    return (vol * 16 + z * 2 + y % 2) * 2 + lane % 2


margin = 1e-4
PG = 32


def facet_constants(a, b, c):
    sides = [dot3(d, d) for d in (minus3(b, a), minus3(c, b), minus3(a, c))]
    bc_long = (sides[1] > sides[0]) & (sides[1] >= sides[2])
    ca_long = (sides[2] > sides[0]) & (sides[2] > sides[1])

    def pick(p, q, r):
        return [jnp.where(bc_long, q[i], jnp.where(ca_long, r[i], p[i])) for i in range(3)]

    a, b, c = pick(a, b, c), pick(b, c, a), pick(c, a, b)
    ab, ac = minus3(b, a), minus3(c, a)
    normal = cross3(ab, ac)
    ab_len = jnp.sqrt(dot3(ab, ab))
    inv_ab = 1.0 / ab_len
    inv_n = lax.rsqrt(dot3(normal, normal))
    e1 = [q * inv_ab for q in ab]
    n = [q * inv_n for q in normal]
    e2 = cross3(n, e1)
    top = dot3(ac, e2)
    left = dot3(ac, e1)
    out = [*e1, -dot3(e1, a) - left, *e2, -dot3(e2, a), *n, -dot3(n, a)]
    for foot in (left, ab_len - left):
        leg = jnp.sqrt(foot * foot + top * top)
        inv_leg = 1.0 / leg
        out += [foot, top * inv_leg, foot * inv_leg, leg]
    return out


def facet_square(p, k):
    px, py, pz = p
    u = px * k[0] + py * k[1] + (pz * k[2] + k[3])
    v = px * k[4] + py * k[5] + (pz * k[6] + k[7])
    h = px * k[8] + py * k[9] + (pz * k[10] + k[11])
    on_left = u < 0.0
    foot, rise, run, leg = (jnp.where(on_left, k[12 + i], k[16 + i]) for i in range(4))
    past = jnp.abs(u) - foot
    s = past * rise + v * run
    t = v * rise - past * run
    below = v < 0.0
    across = jnp.where(below, past, s)
    across = jnp.maximum(across, 0.0)
    along = jnp.where(below, v, t - jnp.clip(t, 0.0, leg))
    return h * h + (across * across + along * along)


def weight(d):
    q = dot3(d, d) + smoothing
    inv = pl.reciprocal(q, approx=True)
    inv = inv * (2.0 - q * inv)
    return inv * inv


def as_columns(row):
    return jnp.transpose(jnp.broadcast_to(row, (LANES, LANES)))


def wall_kernel(cand_hbm, listed_hbm, target_hbm, flag_hbm, wall_ref,
                cols, moved, index, const, best, cand_ref, listed_ref, target_ref, flag_ref, in_sem):
    surf = lax.axis_index("surf")
    inputs = [
        pltpu.make_async_copy(cand_hbm, cand_ref, in_sem.at[0]),
        pltpu.make_async_copy(listed_hbm, listed_ref, in_sem.at[1]),
        pltpu.make_async_copy(target_hbm, target_ref, in_sem.at[2]),
        pltpu.make_async_copy(flag_hbm, flag_ref, in_sem.at[3]),
    ]
    for copy in inputs:
        copy.start()
    for copy in inputs:
        copy.wait()

    def one_block(block, carry):
        row = surf * 4 + block
        lanes = pl.ds(pl.multiple_of(block * LANES, LANES), LANES)
        count = jnp.int32(0)
        for j in range(16):
            count += (cand_ref[j, row] >= 0).astype(jnp.int32)
        flags = flag_ref[pl.ds(row, 1), :]
        flagged = jnp.max(flags) > 0
        wall_ref[pl.ds(block, 1), :] = jnp.zeros((1, LANES), jnp.float32)

        @pl.when(flagged)
        def _():
            targets = [target_ref[pl.ds(c, 1), lanes] for c in range(3)]
            for c in range(3):
                cols[c] = as_columns(targets[c])

            def fetch(j, carry):
                here = pl.ds(j, 1)
                rows = block * 16 + j
                for half in range(2):
                    at = [listed_ref[rows, (2 * c) // 4, pl.ds((2 * c) % 4 + half, 1), :] for c in range(6)]
                    for c in range(3):
                        moved[c, half, here, :] = at[c] + at[3 + c]
                for k in range(3):
                    for quarter in range(4):
                        index[k, quarter, here, :] = listed_ref[rows, 3 + k, pl.ds(quarter, 1), :].astype(jnp.int32)
                return carry

            lax.fori_loop(0, 16, fetch, 0)
            for quarter in range(4):
                corners = []
                for k in range(3):
                    where = index[k, quarter]
                    low = where % LANES
                    corner = []
                    for c in range(3):
                        lo = jnp.take_along_axis(moved[c, 0], low, axis=1, mode="promise_in_bounds")
                        hi = jnp.take_along_axis(moved[c, 1], low, axis=1, mode="promise_in_bounds")
                        corner.append(jnp.where(where < LANES, lo, hi))
                    corners.append(corner)
                for i, value in enumerate(facet_constants(*corners)):
                    const[i, quarter] = value
            best[...] = jnp.full((LANES, LANES), big_value, jnp.float32)

            def one_leaf(j):
                for quarter in range(4):
                    k = [jnp.broadcast_to(const[i, quarter, pl.ds(j, 1), :], (8, LANES)) for i in range(20)]
                    for g in range(16):
                        part = pl.ds(g * 8, 8)
                        p = [cols[c, part, :] for c in range(3)]
                        best[part, :] = jnp.minimum(best[part, :], facet_square(p, k))

            slot = lax.broadcasted_iota(jnp.int32, (16, 1), 0)
            middle = [
                jnp.sum(moved[c, 0] + moved[c, 1], axis=1, keepdims=True) * (1.0 / LEAF) for c in range(3)
            ]
            spread = [
                sum((moved[c, half] - middle[c]) * (moved[c, half] - middle[c]) for c in range(3))
                for half in range(2)
            ]
            radius = jnp.sqrt(jnp.max(jnp.maximum(*spread), axis=1, keepdims=True)) + margin
            away = [middle[c] - targets[c] for c in range(3)]
            away = jnp.sqrt(dot3(away, away))
            valid = slot < count
            lower = jnp.maximum(away - radius, 0.0)
            lower = jnp.where(valid & (flags == 1), lower * lower, big_value)
            upper = jnp.where(valid, away + radius, 1e15)
            upper = jnp.min(upper * upper, axis=0, keepdims=True)
            rank = jnp.sum(jnp.where(flags == 1, away, 0.0), axis=1, keepdims=True)
            rank = jnp.where(valid, rank, big_value)

            def nearest_slot(rank):
                low = jnp.min(rank, axis=0, keepdims=True)
                return jnp.min(jnp.where(rank == low, slot, 15))

            def so_far():
                return jnp.min(jnp.transpose(best[...]), axis=0, keepdims=True)

            def wanted(open_):
                below = lower < jnp.minimum(so_far(), upper)
                hit = jnp.max(jnp.where(below, 1.0, 0.0), axis=1, keepdims=True)
                return jnp.where(open_, hit, 0.0)

            first = nearest_slot(rank)
            one_leaf(first)
            open_ = slot != first
            hit = wanted(open_)

            @pl.when(jnp.max(hit) > 0.0)
            def _():
                second = nearest_slot(jnp.where(hit > 0.0, rank, big_value))
                one_leaf(second)
                rest = wanted(open_ & (slot != second))
                bits = jnp.sum(jnp.where(rest > 0.0, lax.shift_left(jnp.ones_like(slot), slot), 0))

                def perhaps(j, carry):
                    @pl.when(lax.shift_right_logical(bits, j) % 2 == 1)
                    def _():
                        one_leaf(j)

                    return carry

                lax.fori_loop(0, count, perhaps, 0)

            wall_ref[pl.ds(block, 1), :] = jnp.where(flags == 1, jnp.sqrt(so_far()), 0.0)

        return carry

    lax.fori_loop(0, 4, one_block, 0)


def wall(candidates, listed, target, flags):
    f32 = jnp.float32
    return pl.pallas_call(
        wall_kernel,
        name="wall",
        out_shape=jax.ShapeDtypeStruct((4, LANES), f32),
        in_specs=[pl.BlockSpec(memory_space=pltpu.HBM)] * 4,
        out_specs=pl.BlockSpec(memory_space=pltpu.VMEM),
        scratch_shapes=[
            pltpu.VMEM((3, LANES, LANES), f32),
            pltpu.VMEM((3, 2, 16, LANES), f32),
            pltpu.VMEM((3, 4, 16, LANES), jnp.int32),
            pltpu.VMEM((20, 4, 16, LANES), f32),
            pltpu.VMEM((LANES, LANES), f32),
            pltpu.SMEM((16, 64), jnp.int32),
            pltpu.VMEM((64, 6, ROWS, LANES), f32),
            pltpu.VMEM((3, 4 * LANES), f32),
            pltpu.VMEM((64, LANES), jnp.int32),
            pltpu.SemaphoreType.DMA((4,)),
        ],
        compiler_params=pltpu.CompilerParams(vmem_limit_bytes=60 * 2**20),
    )(candidates, listed, target, flags)


def body(surface_points, surface_shift, facet_nodes, volume_points, near_wall, candidates):
    candidates = candidates.T
    listed, displacement, target = displace_and_list(
        candidates, surface_points, surface_shift, jnp.transpose(facet_nodes, (1, 0, 2)), volume_points
    )
    distance = wall(candidates, listed, target, near_wall.reshape(-1, LANES))
    return displacement, distance.reshape(-1)


def solution(mesh):
    placed = (
        P(None, ("vol", "surf")),
        P(None, ("vol", "surf")),
        P(("vol", "surf"), None, None),
        P(None, "vol"),
        P("vol"),
        P("vol", None),
    )
    return jax.shard_map(
        body,
        mesh=mesh,
        in_specs=placed,
        out_specs=(P(None, ("vol", "surf")), P(("vol", "surf"))),
        check_vma=False,
    )
```

```python
import jax
import jax.numpy as jnp
from jax import lax
from jax.experimental import pallas as pl
from jax.experimental.pallas import tpu as pltpu
from jax.sharding import PartitionSpec as P

MESH = pl.DeviceIdType.MESH
smoothing = 0.01
big_value = 1e30

NX, NY, NZ = 4, 4, 8
SIZES = {"x": NX, "y": NY, "z": NZ}
LEAF = 256
CHIPS = NX * NY * NZ
LANES = 128
ROWS = 4


def coords_of(vol, surf):
    return {
        "x": (vol // 2) % NX,
        "y": (vol // (2 * NX)) * 2 + surf % 2,
        "z": surf // 2,
        "c": vol % 2,
    }


def mesh_id(c):
    return ((c["y"] // 2) * NX + c["x"]) * 2 + c["c"], c["z"] * 2 + c["y"] % 2


def shifted(c, axis, k):
    n = SIZES[axis]
    return {**c, axis: lax.rem(c[axis] + (k % n), n)}


WAYS = (("z", "y", "x"), ("z", "x", "y"))
NEAR_FIRST = {4: (1, 3, 2), 8: (1, 7, 2, 6, 3, 5, 4)}


def span(table, part, phase, c):
    if phase == 0:
        return table.at[:, c["c"] * NX + c["x"], c["y"], pl.ds(c["z"] * 3, 3)]
    if phase == 1:
        return table.at[part, c["c"] * NX + c["x"], c["y"]]
    if part == 0:
        return table.at[0, c["c"] * NX + c["x"]]
    return table.at[1, pl.ds(c["c"] * NX, NX), c["y"]]


def half_span(table, part, c, half):
    if part == 0:
        return table.at[0, c["c"] * NX + c["x"], pl.ds(half * 2, 2)]
    return table.at[1, pl.ds(c["c"] * NX + half * 2, 2), c["y"]]


def leaf_index(leaf):
    right = lax.shift_right_logical
    surf, vol = right(leaf, 1) & 15, right(leaf, 5)
    y = (right(vol, 3) << 1) | (surf & 1)
    return leaf & 1, ((vol & 1) << 2) | (right(vol, 1) & 3), y, right(surf, 1) * 3


def gather_kernel(cand_hbm, points_hbm, shift_hbm, facets_hbm, vol_hbm, listed_ref, disp_ref, target_ref,
                  nodes, facets, mom_own, mom_z, mom_y, mom_c, moments, cols, acc, where,
                  cand_ref, points_ref, shift_ref, facets_ref, vol_ref,
                  in_sem, send_sem, recv_sem, core_send, core_recv, mom_send, mom_recv):
    surf = lax.axis_index("surf")
    me = coords_of(lax.axis_index("vol"), surf)
    sibling = {**me, "c": 1 - me["c"]}
    partners = [sibling]
    for axis, n in SIZES.items():
        partners += [shifted(me, axis, k) for k in range(1, n)]
    barrier = pltpu.get_barrier_semaphore()
    for other in partners:
        pl.semaphore_signal(barrier, inc=1, device_id=mesh_id(other), device_id_type=MESH)
    share = pl.ds(pl.multiple_of(surf * 4 * LANES, 4 * LANES), 4 * LANES)
    inputs = [
        pltpu.make_async_copy(points_hbm, points_ref, in_sem.at[0]),
        pltpu.make_async_copy(shift_hbm, shift_ref, in_sem.at[1]),
        pltpu.make_async_copy(facets_hbm, facets_ref, in_sem.at[2]),
        pltpu.make_async_copy(vol_hbm.at[:, share], vol_ref, in_sem.at[3]),
        pltpu.make_async_copy(cand_hbm, cand_ref, in_sem.at[4]),
    ]
    for copy in inputs:
        copy.start()
    for copy in inputs:
        copy.wait()

    for leaf in range(2):
        own = (leaf, me["c"] * NX + me["x"], me["y"])
        for half in range(2):
            lanes = pl.ds(leaf * LEAF + half * LANES, LANES)
            for c in range(3):
                nodes[(*own, me["z"] * 3 + (2 * c) // 4, pl.ds((2 * c) % 4 + half, 1), slice(None))] = (
                    points_ref[pl.ds(c, 1), lanes]
                )
                nodes[(*own, me["z"] * 3 + (6 + 2 * c) // 4, pl.ds((6 + 2 * c) % 4 + half, 1), slice(None))] = (
                    shift_ref[pl.ds(c, 1), lanes]
                )
        for quarter in range(4):
            lanes = pl.ds(quarter * LANES, LANES)
            for k in range(3):
                facets[(*own, me["z"] * 3 + k, pl.ds(quarter, 1), slice(None))] = (
                    facets_ref[k, pl.ds(leaf, 1), lanes].astype(jnp.float32)
                )
    lane = lax.broadcasted_iota(jnp.int32, (3, LANES), 1)
    my_lane = ((me["c"] * NY + me["y"]) * NZ + me["z"]) * 2
    for row, ref in ((0, points_ref), (3, shift_ref)):
        tile = jnp.zeros((3, LANES), jnp.float32)
        for leaf in range(2):
            mean = jnp.sum(ref[:, pl.ds(leaf * LEAF, LEAF)], axis=1, keepdims=True) * (1.0 / LEAF)
            tile = jnp.where(lane == my_lane + leaf, mean, tile)
        mom_own[pl.ds(row, 3), :] = tile
    mom_own[pl.ds(6, 2), :] = jnp.zeros((2, LANES), jnp.float32)
    pl.semaphore_wait(barrier, len(partners))

    sent = []

    def remote(src, dst, to, s_sem, r_sem):
        return pltpu.make_async_remote_copy(
            src_ref=src, dst_ref=dst, send_sem=s_sem, recv_sem=r_sem,
            device_id=mesh_id(to), device_id_type=MESH,
        )

    def start(copy):
        copy.start()
        sent.append(copy)

    tables = (nodes, facets)

    def sems(which, part, phase, k):
        slot = (part, phase, k)
        return send_sem.at[(which, *slot)], recv_sem.at[(which, *slot)]

    def issue(which, part, phase):
        axis = WAYS[part][phase]
        mine = span(tables[which], part, phase, me)
        if phase == 2:
            for turn in range(2):
                for k in (1, 3):
                    piece = half_span(tables[which], part, me, (k // 2) ^ turn)
                    start(remote(piece, piece, shifted(me, axis, k), *sems(which, part, 2, k + 4 * turn - 1)))
            return
        for k in NEAR_FIRST[SIZES[axis]]:
            start(remote(mine, mine, shifted(me, axis, k), *sems(which, part, phase, k)))

    def collect(which, part, phase):
        axis = WAYS[part][phase]
        for k in NEAR_FIRST[SIZES[axis]]:
            frm = shifted(me, axis, -k)
            theirs = span(tables[which], part, phase, frm)
            remote(theirs, theirs, frm, *sems(which, part, phase, k)).wait_recv()

    def collect_turn(which, part, k, turn):
        axis = WAYS[part][2]
        frm = shifted(me, axis, -k)
        piece = half_span(tables[which], part, frm, (k // 2) ^ turn)
        remote(piece, piece, frm, *sems(which, part, 2, k + 4 * turn - 1)).wait_recv()

    def forward(which, part, k):
        axis = WAYS[part][2]
        piece = half_span(tables[which], part, shifted(me, axis, -k), k // 2)
        start(remote(piece, piece, shifted(me, axis, k), *sems(which, part, 2, k)))

    def pass_on(which):
        for k in (1, 3):
            for part in range(2):
                collect_turn(which, part, k, 0)
                forward(which, part, k)

    def take_rest(which):
        for k in (1, 3):
            for part in range(2):
                collect_turn(which, part, k, 1)
                to_sibling(which, part, k)

    def collect_halves(which, part):
        axis = WAYS[part][2]
        for k in (1, 3):
            piece = half_span(tables[which], part, shifted(me, axis, 2), k // 2)
            remote(piece, piece, shifted(me, axis, -k), *sems(which, part, 2, k)).wait_recv()

    def to_sibling(which, part, k):
        mine = span(tables[which], part, 2, shifted(me, WAYS[part][2], -k))
        start(remote(mine, mine, sibling, core_send.at[which, part, k], core_recv.at[which, part, k]))

    def from_sibling(which, part, k):
        theirs = span(tables[which], part, 2, shifted(sibling, WAYS[part][2], -k))
        remote(theirs, theirs, sibling, core_send.at[which, part, k], core_recv.at[which, part, k]).wait_recv()

    def mom_copies(dst, others, slot0):
        return [
            remote(mom_own, dst.at[k], other, mom_send.at[slot0 + k], mom_recv.at[slot0 + k])
            for k, other in enumerate(others)
        ]

    def mom_sum(copies, arrived):
        total = mom_own[...]
        for k, copy in enumerate(copies):
            copy.wait()
            total = total + arrived[k]
        mom_own[...] = total

    issue(0, 0, 0)
    mom = mom_copies(mom_z, [shifted(me, "z", k) for k in range(1, NZ)], 0)
    for copy in mom:
        copy.start()
    collect(0, 0, 0)
    issue(0, 0, 1)
    issue(0, 1, 1)
    issue(1, 0, 0)
    mom_sum(mom, mom_z)
    mom = mom_copies(mom_y, [shifted(me, "y", k) for k in range(1, NY)], 7)
    for copy in mom:
        copy.start()
    for part in range(2):
        collect(0, part, 1)
        issue(0, part, 2)
    mom_sum(mom, mom_y)
    mom = mom_copies(mom_c, [sibling], 10)
    mom[0].start()
    for part in range(2):
        to_sibling(0, part, 0)

    def locate(n, carry):
        at = leaf_index(jnp.maximum(cand_ref[n % 16, surf * 4 + n // 16], 0))
        for i in range(4):
            where[i, n] = at[i]
        return carry

    lax.fori_loop(0, 64, locate, 0)
    mom_sum(mom, mom_c)
    moments[pl.ds(me["x"], 1)] = mom_own[...][None]
    for k in range(1, NX):
        start(remote(mom_own, moments.at[me["x"]], shifted(me, "x", k), mom_send.at[10 + k], mom_recv.at[10 + k]))
    collect(1, 0, 0)
    issue(1, 0, 1)
    issue(1, 1, 1)
    for block in range(4):
        for c in range(3):
            cols[block, c] = as_columns(vol_ref[pl.ds(c, 1), pl.ds(block * LANES, LANES)])
    pass_on(0)
    for k in range(1, NX):
        frm = shifted(me, "x", -k)
        remote(mom_own, moments.at[frm["x"]], frm, mom_send.at[10 + k], mom_recv.at[10 + k]).wait_recv()

    def far(block, carry):
        row = surf * 4 + block
        centers = []
        for x in range(NX):
            ids = leaf_ids(x)
            listed = ids == cand_ref[0, row]
            for j in range(1, 16):
                listed = listed | (ids == cand_ref[j, row])
            centers.append(jnp.where(listed, 0.0, float(LEAF)))
        for g in range(LANES // PG):
            part = pl.ds(g * PG, PG)
            p = [cols[block, c, part, :] for c in range(3)]
            sums = [None] * 4
            for x in range(NX):
                m = moments[x]
                w = weight([m[c:c + 1] - p[c] for c in range(3)]) * centers[x]
                terms = [w * m[3 + c:4 + c] for c in range(3)] + [w]
                sums = terms if x == 0 else [a + b for a, b in zip(sums, terms)]
            for c in range(4):
                acc[block, c, part, :] = sums[c]
        return carry

    lax.fori_loop(0, 4, far, 0)
    take_rest(0)
    for part in range(2):
        collect(1, part, 1)
        issue(1, part, 2)
    for part in range(2):
        collect_halves(0, part)
        to_sibling(0, part, 2)
    for part in range(2):
        to_sibling(1, part, 0)
        for k in range(4):
            from_sibling(0, part, k)

    def displace(block):
        def near(j, carry):
            n = block * 16 + j
            i0, i1, i2, quad = (where[i, n] for i in range(4))
            push_off = jnp.where(cand_ref[j, surf * 4 + block] >= 0, 0.0, 1e15)
            at = [
                [nodes[i0, i1, i2, quad + (2 * c) // 4, pl.ds((2 * c) % 4 + half, 1), :] for c in range(6)]
                for half in range(2)
            ]
            for half in range(2):
                at[half][0] = at[half][0] + push_off
            for g in range(LANES // PG):
                part = pl.ds(g * PG, PG)
                p = [cols[block, c, part, :] for c in range(3)]
                w = [weight([at[half][c] - p[c] for c in range(3)]) for half in range(2)]
                for c in range(3):
                    acc[block, c, part, :] += w[0] * at[0][3 + c] + w[1] * at[1][3 + c]
                acc[block, 3, part, :] += w[0] + w[1]
            for q in range(3):
                listed_ref[n, q] = nodes[i0, i1, i2, quad + q]
            return carry

        lax.fori_loop(0, 16, near, 0)
        out_lanes = pl.ds(block * LANES, LANES)
        total = [jnp.sum(jnp.transpose(acc[block, c]), axis=0, keepdims=True) for c in range(4)]
        inv = 1.0 / total[3]
        for c in range(3):
            disp = total[c] * inv
            disp_ref[pl.ds(c, 1), out_lanes] = disp
            target_ref[pl.ds(c, 1), out_lanes] = vol_ref[pl.ds(c, 1), out_lanes] + disp

    displace(0)
    pass_on(1)
    take_rest(1)
    displace(1)
    displace(2)
    for part in range(2):
        collect_halves(1, part)
        to_sibling(1, part, 2)
    displace(3)
    for part in range(2):
        for k in range(4):
            from_sibling(1, part, k)

    def hand_out(n, carry):
        i0, i1, i2, quad = (where[i, n] for i in range(4))
        for q in range(3):
            listed_ref[n, 3 + q] = facets[i0, i1, i2, quad + q]
        return carry

    lax.fori_loop(0, 64, hand_out, 0)
    for copy in sent:
        copy.wait_send()


def displace_and_list(candidates, points, shift, facets, vol):
    f32 = jnp.float32
    vmem = pl.BlockSpec(memory_space=pltpu.VMEM)
    table = pltpu.VMEM((2, 2 * NX, NY, NZ * 3, ROWS, LANES), f32)
    dma = pltpu.SemaphoreType.DMA
    return pl.pallas_call(
        gather_kernel,
        name="displace",
        out_shape=(
            jax.ShapeDtypeStruct((64, 6, ROWS, LANES), f32),
            jax.ShapeDtypeStruct((3, 4 * LANES), f32),
            jax.ShapeDtypeStruct((3, 4 * LANES), f32),
        ),
        in_specs=[pl.BlockSpec(memory_space=pltpu.HBM)] * 5,
        out_specs=(vmem, vmem, vmem),
        scratch_shapes=[
            table,
            table,
            pltpu.VMEM((8, LANES), f32),
            pltpu.VMEM((7, 8, LANES), f32),
            pltpu.VMEM((3, 8, LANES), f32),
            pltpu.VMEM((1, 8, LANES), f32),
            pltpu.VMEM((NX, 8, LANES), f32),
            pltpu.VMEM((4, 3, LANES, LANES), f32),
            pltpu.VMEM((4, 4, LANES, LANES), f32),
            pltpu.SMEM((4, 64), jnp.int32),
            pltpu.SMEM((16, 64), jnp.int32),
            pltpu.VMEM((3, 4 * LANES), f32),
            pltpu.VMEM((3, 4 * LANES), f32),
            pltpu.VMEM((3, 2, 4 * LANES), jnp.int32),
            pltpu.VMEM((3, 4 * LANES), f32),
            dma((5,)),
            dma((2, 2, 3, 8)),
            dma((2, 2, 3, 8)),
            dma((2, 2, 4)),
            dma((2, 2, 4)),
            dma((14,)),
            dma((14,)),
        ],
        compiler_params=pltpu.CompilerParams(
            collective_id=0, has_side_effects=True, vmem_limit_bytes=60 * 2**20
        ),
    )(candidates, points, shift, facets, vol)


def dot3(a, b):
    return a[0] * b[0] + a[1] * b[1] + a[2] * b[2]


def minus3(a, b):
    return [a[0] - b[0], a[1] - b[1], a[2] - b[2]]


def cross3(a, b):
    return [a[1] * b[2] - a[2] * b[1], a[2] * b[0] - a[0] * b[2], a[0] * b[1] - a[1] * b[0]]


def leaf_ids(x):
    lane = lax.broadcasted_iota(jnp.int32, (1, LANES), 1)
    z = (lane // 2) % NZ
    y = (lane // (2 * NZ)) % NY
    core = lane // (2 * NZ * NY)
    vol = ((y // 2) * NX + x) * 2 + core
    return (vol * 16 + z * 2 + y % 2) * 2 + lane % 2


margin = 1e-4
PG = 32


def facet_constants(a, b, c):
    sides = [dot3(d, d) for d in (minus3(b, a), minus3(c, b), minus3(a, c))]
    bc_long = (sides[1] > sides[0]) & (sides[1] >= sides[2])
    ca_long = (sides[2] > sides[0]) & (sides[2] > sides[1])

    def pick(p, q, r):
        return [jnp.where(bc_long, q[i], jnp.where(ca_long, r[i], p[i])) for i in range(3)]

    a, b, c = pick(a, b, c), pick(b, c, a), pick(c, a, b)
    ab, ac = minus3(b, a), minus3(c, a)
    normal = cross3(ab, ac)
    ab_len = jnp.sqrt(dot3(ab, ab))
    inv_ab = 1.0 / ab_len
    inv_n = lax.rsqrt(dot3(normal, normal))
    e1 = [q * inv_ab for q in ab]
    n = [q * inv_n for q in normal]
    e2 = cross3(n, e1)
    top = dot3(ac, e2)
    left = dot3(ac, e1)
    out = [*e1, -dot3(e1, a) - left, *e2, -dot3(e2, a), *n, -dot3(n, a)]
    for foot in (left, ab_len - left):
        leg = jnp.sqrt(foot * foot + top * top)
        inv_leg = 1.0 / leg
        out += [foot, top * inv_leg, foot * inv_leg, leg]
    return out


def facet_square(p, k):
    px, py, pz = p
    u = px * k[0] + py * k[1] + (pz * k[2] + k[3])
    v = px * k[4] + py * k[5] + (pz * k[6] + k[7])
    h = px * k[8] + py * k[9] + (pz * k[10] + k[11])
    on_left = u < 0.0
    foot, rise, run, leg = (jnp.where(on_left, k[12 + i], k[16 + i]) for i in range(4))
    past = jnp.abs(u) - foot
    s = past * rise + v * run
    t = v * rise - past * run
    below = v < 0.0
    across = jnp.where(below, past, s)
    across = jnp.maximum(across, 0.0)
    along = jnp.where(below, v, t - jnp.clip(t, 0.0, leg))
    return h * h + (across * across + along * along)


def weight(d):
    q = dot3(d, d) + smoothing
    inv = pl.reciprocal(q, approx=True)
    inv = inv * (2.0 - q * inv)
    return inv * inv


def as_columns(row):
    return jnp.transpose(jnp.broadcast_to(row, (LANES, LANES)))


def wall_kernel(cand_hbm, listed_hbm, target_hbm, flag_hbm, disp_hbm, disp_out, wall_ref,
                cols, moved, index, const, best, cand_ref, listed_ref, target_ref, flag_ref, in_sem):
    surf = lax.axis_index("surf")
    inputs = [
        pltpu.make_async_copy(cand_hbm, cand_ref, in_sem.at[0]),
        pltpu.make_async_copy(listed_hbm, listed_ref, in_sem.at[1]),
        pltpu.make_async_copy(target_hbm, target_ref, in_sem.at[2]),
        pltpu.make_async_copy(flag_hbm, flag_ref, in_sem.at[3]),
    ]
    hand_over = pltpu.make_async_copy(disp_hbm, disp_out, in_sem.at[4])
    for copy in inputs:
        copy.start()
    hand_over.start()
    for copy in inputs:
        copy.wait()

    def one_block(block, carry):
        row = surf * 4 + block
        lanes = pl.ds(pl.multiple_of(block * LANES, LANES), LANES)
        count = jnp.int32(0)
        for j in range(16):
            count += (cand_ref[j, row] >= 0).astype(jnp.int32)
        flags = flag_ref[pl.ds(row, 1), :]
        flagged = jnp.max(flags) > 0
        wall_ref[pl.ds(block, 1), :] = jnp.zeros((1, LANES), jnp.float32)

        @pl.when(flagged)
        def _():
            targets = [target_ref[pl.ds(c, 1), lanes] for c in range(3)]
            for c in range(3):
                cols[c] = as_columns(targets[c])

            def fetch(j, carry):
                here = pl.ds(j, 1)
                rows = block * 16 + j
                for half in range(2):
                    at = [listed_ref[rows, (2 * c) // 4, pl.ds((2 * c) % 4 + half, 1), :] for c in range(6)]
                    for c in range(3):
                        moved[c, half, here, :] = at[c] + at[3 + c]
                for k in range(3):
                    for quarter in range(4):
                        index[k, quarter, here, :] = listed_ref[rows, 3 + k, pl.ds(quarter, 1), :].astype(jnp.int32)
                return carry

            lax.fori_loop(0, 16, fetch, 0)
            for quarter in range(4):
                corners = []
                for k in range(3):
                    where = index[k, quarter]
                    low = where % LANES
                    corner = []
                    for c in range(3):
                        lo = jnp.take_along_axis(moved[c, 0], low, axis=1, mode="promise_in_bounds")
                        hi = jnp.take_along_axis(moved[c, 1], low, axis=1, mode="promise_in_bounds")
                        corner.append(jnp.where(where < LANES, lo, hi))
                    corners.append(corner)
                for i, value in enumerate(facet_constants(*corners)):
                    const[i, quarter] = value
            best[...] = jnp.full((LANES, LANES), big_value, jnp.float32)

            def one_leaf(j):
                for quarter in range(4):
                    k = [jnp.broadcast_to(const[i, quarter, pl.ds(j, 1), :], (8, LANES)) for i in range(20)]
                    for g in range(16):
                        part = pl.ds(g * 8, 8)
                        p = [cols[c, part, :] for c in range(3)]
                        best[part, :] = jnp.minimum(best[part, :], facet_square(p, k))

            slot = lax.broadcasted_iota(jnp.int32, (16, 1), 0)
            middle = [
                jnp.sum(moved[c, 0] + moved[c, 1], axis=1, keepdims=True) * (1.0 / LEAF) for c in range(3)
            ]
            spread = [
                sum((moved[c, half] - middle[c]) * (moved[c, half] - middle[c]) for c in range(3))
                for half in range(2)
            ]
            radius = jnp.sqrt(jnp.max(jnp.maximum(*spread), axis=1, keepdims=True)) + margin
            away = [middle[c] - targets[c] for c in range(3)]
            away = jnp.sqrt(dot3(away, away))
            valid = slot < count
            lower = jnp.maximum(away - radius, 0.0)
            lower = jnp.where(valid & (flags == 1), lower * lower, big_value)
            upper = jnp.where(valid, away + radius, 1e15)
            upper = jnp.min(upper * upper, axis=0, keepdims=True)
            rank = jnp.sum(jnp.where(flags == 1, away, 0.0), axis=1, keepdims=True)
            rank = jnp.where(valid, rank, big_value)

            def nearest_slot(rank):
                low = jnp.min(rank, axis=0, keepdims=True)
                return jnp.min(jnp.where(rank == low, slot, 15))

            def so_far():
                return jnp.min(jnp.transpose(best[...]), axis=0, keepdims=True)

            def wanted(open_):
                below = lower < jnp.minimum(so_far(), upper)
                hit = jnp.max(jnp.where(below, 1.0, 0.0), axis=1, keepdims=True)
                return jnp.where(open_, hit, 0.0)

            first = nearest_slot(rank)
            one_leaf(first)
            open_ = slot != first
            hit = wanted(open_)

            @pl.when(jnp.max(hit) > 0.0)
            def _():
                second = nearest_slot(jnp.where(hit > 0.0, rank, big_value))
                one_leaf(second)
                rest = wanted(open_ & (slot != second))
                bits = jnp.sum(jnp.where(rest > 0.0, lax.shift_left(jnp.ones_like(slot), slot), 0))

                def perhaps(j, carry):
                    @pl.when(lax.shift_right_logical(bits, j) % 2 == 1)
                    def _():
                        one_leaf(j)

                    return carry

                lax.fori_loop(0, count, perhaps, 0)

            wall_ref[pl.ds(block, 1), :] = jnp.where(flags == 1, jnp.sqrt(so_far()), 0.0)

        return carry

    lax.fori_loop(0, 4, one_block, 0)
    hand_over.wait()


def wall(candidates, listed, target, flags, displacement):
    f32 = jnp.float32
    hbm = pl.BlockSpec(memory_space=pltpu.HBM)
    return pl.pallas_call(
        wall_kernel,
        name="wall",
        out_shape=(
            jax.ShapeDtypeStruct((3, 4 * LANES), f32),
            jax.ShapeDtypeStruct((4, LANES), f32),
        ),
        in_specs=[hbm] * 5,
        out_specs=(hbm, pl.BlockSpec(memory_space=pltpu.VMEM)),
        scratch_shapes=[
            pltpu.VMEM((3, LANES, LANES), f32),
            pltpu.VMEM((3, 2, 16, LANES), f32),
            pltpu.VMEM((3, 4, 16, LANES), jnp.int32),
            pltpu.VMEM((20, 4, 16, LANES), f32),
            pltpu.VMEM((LANES, LANES), f32),
            pltpu.SMEM((16, 64), jnp.int32),
            pltpu.VMEM((64, 6, ROWS, LANES), f32),
            pltpu.VMEM((3, 4 * LANES), f32),
            pltpu.VMEM((64, LANES), jnp.int32),
            pltpu.SemaphoreType.DMA((5,)),
        ],
        compiler_params=pltpu.CompilerParams(vmem_limit_bytes=60 * 2**20),
    )(candidates, listed, target, flags, displacement)


def body(surface_points, surface_shift, facet_nodes, volume_points, near_wall, candidates):
    candidates = candidates.T
    listed, displacement, target = displace_and_list(
        candidates, surface_points, surface_shift, jnp.transpose(facet_nodes, (1, 0, 2)), volume_points
    )
    displacement, distance = wall(candidates, listed, target, near_wall.reshape(-1, LANES), displacement)
    return displacement, distance.reshape(-1)


def solution(mesh):
    placed = (
        P(None, ("vol", "surf")),
        P(None, ("vol", "surf")),
        P(("vol", "surf"), None, None),
        P(None, "vol"),
        P("vol"),
        P("vol", None),
    )
    return jax.shard_map(
        body,
        mesh=mesh,
        in_specs=placed,
        out_specs=(P(None, ("vol", "surf")), P(("vol", "surf"))),
        check_vma=False,
    )
```

```python
import jax
import jax.numpy as jnp
from jax import lax
from jax.experimental import pallas as pl
from jax.experimental.pallas import tpu as pltpu
from jax.sharding import PartitionSpec as P

MESH = pl.DeviceIdType.MESH
smoothing = 0.01
big_value = 1e30

NX, NY, NZ = 4, 4, 8
SIZES = {"x": NX, "y": NY, "z": NZ}
LEAF = 256
CHIPS = NX * NY * NZ
LANES = 128
ROWS = 4


def coords_of(vol, surf):
    return {
        "x": (vol // 2) % NX,
        "y": (vol // (2 * NX)) * 2 + surf % 2,
        "z": surf // 2,
        "c": vol % 2,
    }


def mesh_id(c):
    return ((c["y"] // 2) * NX + c["x"]) * 2 + c["c"], c["z"] * 2 + c["y"] % 2


def shifted(c, axis, k):
    n = SIZES[axis]
    return {**c, axis: lax.rem(c[axis] + (k % n), n)}


WAYS = (("z", "y", "x"), ("z", "x", "y"))
NEAR_FIRST = {4: (1, 3, 2), 8: (1, 7, 2, 6, 3, 5, 4)}


def span(table, part, phase, c):
    if phase == 0:
        return table.at[:, c["c"] * NX + c["x"], c["y"], pl.ds(c["z"] * 3, 3)]
    if phase == 1:
        return table.at[part, c["c"] * NX + c["x"], c["y"]]
    if part == 0:
        return table.at[0, c["c"] * NX + c["x"]]
    return table.at[1, pl.ds(c["c"] * NX, NX), c["y"]]


def half_span(table, part, c, half):
    if part == 0:
        return table.at[0, c["c"] * NX + c["x"], pl.ds(half * 2, 2)]
    return table.at[1, pl.ds(c["c"] * NX + half * 2, 2), c["y"]]


def leaf_index(leaf):
    right = lax.shift_right_logical
    surf, vol = right(leaf, 1) & 15, right(leaf, 5)
    y = (right(vol, 3) << 1) | (surf & 1)
    return leaf & 1, ((vol & 1) << 2) | (right(vol, 1) & 3), y, right(surf, 1) * 3


def gather_kernel(cand_hbm, points_hbm, shift_hbm, facets_hbm, vol_hbm, listed_ref, disp_ref, target_ref,
                  nodes, facets, mom_own, mom_z, mom_y, mom_c, moments, cols, acc, where,
                  cand_ref, points_ref, shift_ref, facets_ref, vol_ref,
                  in_sem, send_sem, recv_sem, core_send, core_recv, mom_send, mom_recv):
    surf = lax.axis_index("surf")
    me = coords_of(lax.axis_index("vol"), surf)
    sibling = {**me, "c": 1 - me["c"]}
    partners = [sibling]
    for axis, n in SIZES.items():
        partners += [shifted(me, axis, k) for k in range(1, n)]
    barrier = pltpu.get_barrier_semaphore()
    for other in partners:
        pl.semaphore_signal(barrier, inc=1, device_id=mesh_id(other), device_id_type=MESH)
    share = pl.ds(pl.multiple_of(surf * 4 * LANES, 4 * LANES), 4 * LANES)
    inputs = [
        pltpu.make_async_copy(points_hbm, points_ref, in_sem.at[0]),
        pltpu.make_async_copy(shift_hbm, shift_ref, in_sem.at[1]),
        pltpu.make_async_copy(facets_hbm, facets_ref, in_sem.at[2]),
        pltpu.make_async_copy(vol_hbm.at[:, share], vol_ref, in_sem.at[3]),
        pltpu.make_async_copy(cand_hbm, cand_ref, in_sem.at[4]),
    ]
    for copy in inputs:
        copy.start()
    for copy in inputs:
        copy.wait()

    for leaf in range(2):
        own = (leaf, me["c"] * NX + me["x"], me["y"])
        for half in range(2):
            lanes = pl.ds(leaf * LEAF + half * LANES, LANES)
            for c in range(3):
                nodes[(*own, me["z"] * 3 + (2 * c) // 4, pl.ds((2 * c) % 4 + half, 1), slice(None))] = (
                    points_ref[pl.ds(c, 1), lanes]
                )
                nodes[(*own, me["z"] * 3 + (6 + 2 * c) // 4, pl.ds((6 + 2 * c) % 4 + half, 1), slice(None))] = (
                    shift_ref[pl.ds(c, 1), lanes]
                )
        for quarter in range(4):
            lanes = pl.ds(quarter * LANES, LANES)
            for k in range(3):
                facets[(*own, me["z"] * 3 + k, pl.ds(quarter, 1), slice(None))] = (
                    facets_ref[k, pl.ds(leaf, 1), lanes].astype(jnp.float32)
                )
    lane = lax.broadcasted_iota(jnp.int32, (3, LANES), 1)
    my_lane = ((me["c"] * NY + me["y"]) * NZ + me["z"]) * 2
    for row, ref in ((0, points_ref), (3, shift_ref)):
        tile = jnp.zeros((3, LANES), jnp.float32)
        for leaf in range(2):
            mean = jnp.sum(ref[:, pl.ds(leaf * LEAF, LEAF)], axis=1, keepdims=True) * (1.0 / LEAF)
            tile = jnp.where(lane == my_lane + leaf, mean, tile)
        mom_own[pl.ds(row, 3), :] = tile
    mom_own[pl.ds(6, 2), :] = jnp.zeros((2, LANES), jnp.float32)
    pl.semaphore_wait(barrier, len(partners))

    sent = []

    def remote(src, dst, to, s_sem, r_sem):
        return pltpu.make_async_remote_copy(
            src_ref=src, dst_ref=dst, send_sem=s_sem, recv_sem=r_sem,
            device_id=mesh_id(to), device_id_type=MESH,
        )

    def start(copy):
        copy.start()
        sent.append(copy)

    tables = (nodes, facets)

    def sems(which, part, phase, k):
        slot = (part, phase, k)
        return send_sem.at[(which, *slot)], recv_sem.at[(which, *slot)]

    def issue(which, part, phase):
        axis = WAYS[part][phase]
        mine = span(tables[which], part, phase, me)
        if phase == 2:
            for turn in range(2):
                for k in (1, 3):
                    piece = half_span(tables[which], part, me, (k // 2) ^ turn)
                    start(remote(piece, piece, shifted(me, axis, k), *sems(which, part, 2, k + 4 * turn - 1)))
            return
        for k in NEAR_FIRST[SIZES[axis]]:
            start(remote(mine, mine, shifted(me, axis, k), *sems(which, part, phase, k)))

    def collect(which, part, phase):
        axis = WAYS[part][phase]
        for k in NEAR_FIRST[SIZES[axis]]:
            frm = shifted(me, axis, -k)
            theirs = span(tables[which], part, phase, frm)
            remote(theirs, theirs, frm, *sems(which, part, phase, k)).wait_recv()

    def collect_turn(which, part, k, turn):
        axis = WAYS[part][2]
        frm = shifted(me, axis, -k)
        piece = half_span(tables[which], part, frm, (k // 2) ^ turn)
        remote(piece, piece, frm, *sems(which, part, 2, k + 4 * turn - 1)).wait_recv()

    def forward(which, part, k):
        axis = WAYS[part][2]
        piece = half_span(tables[which], part, shifted(me, axis, -k), k // 2)
        start(remote(piece, piece, shifted(me, axis, k), *sems(which, part, 2, k)))

    def pass_on(which):
        for k in (1, 3):
            for part in range(2):
                collect_turn(which, part, k, 0)
                forward(which, part, k)

    def take_rest(which):
        for k in (1, 3):
            for part in range(2):
                collect_turn(which, part, k, 1)
                to_sibling(which, part, k)

    def collect_halves(which, part):
        axis = WAYS[part][2]
        for k in (1, 3):
            piece = half_span(tables[which], part, shifted(me, axis, 2), k // 2)
            remote(piece, piece, shifted(me, axis, -k), *sems(which, part, 2, k)).wait_recv()

    def to_sibling(which, part, k):
        mine = span(tables[which], part, 2, shifted(me, WAYS[part][2], -k))
        start(remote(mine, mine, sibling, core_send.at[which, part, k], core_recv.at[which, part, k]))

    def from_sibling(which, part, k):
        theirs = span(tables[which], part, 2, shifted(sibling, WAYS[part][2], -k))
        remote(theirs, theirs, sibling, core_send.at[which, part, k], core_recv.at[which, part, k]).wait_recv()

    def mom_copies(dst, others, slot0):
        return [
            remote(mom_own, dst.at[k], other, mom_send.at[slot0 + k], mom_recv.at[slot0 + k])
            for k, other in enumerate(others)
        ]

    def mom_sum(copies, arrived):
        total = mom_own[...]
        for k, copy in enumerate(copies):
            copy.wait()
            total = total + arrived[k]
        mom_own[...] = total

    issue(0, 0, 0)
    mom = mom_copies(mom_z, [shifted(me, "z", k) for k in range(1, NZ)], 0)
    for copy in mom:
        copy.start()
    collect(0, 0, 0)
    issue(0, 0, 1)
    issue(0, 1, 1)
    issue(1, 0, 0)
    mom_sum(mom, mom_z)
    mom = mom_copies(mom_y, [shifted(me, "y", k) for k in range(1, NY)], 7)
    for copy in mom:
        copy.start()
    for part in range(2):
        collect(0, part, 1)
        issue(0, part, 2)
    mom_sum(mom, mom_y)
    mom = mom_copies(mom_c, [sibling], 10)
    mom[0].start()
    for part in range(2):
        to_sibling(0, part, 0)

    def locate(n, carry):
        at = leaf_index(jnp.maximum(cand_ref[n % 16, surf * 4 + n // 16], 0))
        for i in range(4):
            where[i, n] = at[i]
        return carry

    lax.fori_loop(0, 64, locate, 0)
    mom_sum(mom, mom_c)
    moments[pl.ds(me["x"], 1)] = mom_own[...][None]
    for k in range(1, NX):
        start(remote(mom_own, moments.at[me["x"]], shifted(me, "x", k), mom_send.at[10 + k], mom_recv.at[10 + k]))
    collect(1, 0, 0)
    issue(1, 0, 1)
    issue(1, 1, 1)
    for block in range(4):
        for c in range(3):
            cols[block, c] = as_columns(vol_ref[pl.ds(c, 1), pl.ds(block * LANES, LANES)])
    pass_on(0)
    for k in range(1, NX):
        frm = shifted(me, "x", -k)
        remote(mom_own, moments.at[frm["x"]], frm, mom_send.at[10 + k], mom_recv.at[10 + k]).wait_recv()

    def far(block, carry):
        row = surf * 4 + block
        centers = []
        for x in range(NX):
            ids = leaf_ids(x)
            listed = ids == cand_ref[0, row]
            for j in range(1, 16):
                listed = listed | (ids == cand_ref[j, row])
            centers.append(jnp.where(listed, 0.0, float(LEAF)))
        for g in range(LANES // PG):
            part = pl.ds(g * PG, PG)
            p = [cols[block, c, part, :] for c in range(3)]
            sums = [None] * 4
            for x in range(NX):
                m = moments[x]
                w = weight([m[c:c + 1] - p[c] for c in range(3)]) * centers[x]
                terms = [w * m[3 + c:4 + c] for c in range(3)] + [w]
                sums = terms if x == 0 else [a + b for a, b in zip(sums, terms)]
            for c in range(4):
                acc[block, c, part, :] = sums[c]
        return carry

    lax.fori_loop(0, 4, far, 0)
    take_rest(0)
    for part in range(2):
        collect(1, part, 1)
        issue(1, part, 2)
    for part in range(2):
        collect_halves(0, part)
        to_sibling(0, part, 2)
    for part in range(2):
        to_sibling(1, part, 0)
        for k in range(4):
            from_sibling(0, part, k)

    def displace(block):
        def near(j, carry):
            n = block * 16 + j
            i0, i1, i2, quad = (where[i, n] for i in range(4))
            push_off = jnp.where(cand_ref[j, surf * 4 + block] >= 0, 0.0, 1e15)
            at = [
                [nodes[i0, i1, i2, quad + (2 * c) // 4, pl.ds((2 * c) % 4 + half, 1), :] for c in range(6)]
                for half in range(2)
            ]
            for half in range(2):
                at[half][0] = at[half][0] + push_off
            for g in range(LANES // PG):
                part = pl.ds(g * PG, PG)
                p = [cols[block, c, part, :] for c in range(3)]
                w = [weight([at[half][c] - p[c] for c in range(3)]) for half in range(2)]
                for c in range(3):
                    acc[block, c, part, :] += w[0] * at[0][3 + c] + w[1] * at[1][3 + c]
                acc[block, 3, part, :] += w[0] + w[1]
            for q in range(3):
                listed_ref[n, q] = nodes[i0, i1, i2, quad + q]
            return carry

        lax.fori_loop(0, 16, near, 0)
        out_lanes = pl.ds(block * LANES, LANES)
        total = [jnp.sum(jnp.transpose(acc[block, c]), axis=0, keepdims=True) for c in range(4)]
        inv = 1.0 / total[3]
        for c in range(3):
            disp = total[c] * inv
            disp_ref[pl.ds(c, 1), out_lanes] = disp
            target_ref[pl.ds(c, 1), out_lanes] = vol_ref[pl.ds(c, 1), out_lanes] + disp

    displace(0)
    pass_on(1)
    take_rest(1)
    displace(1)
    displace(2)
    for part in range(2):
        collect_halves(1, part)
        to_sibling(1, part, 2)
    displace(3)
    for part in range(2):
        for k in range(4):
            from_sibling(1, part, k)

    def hand_out(n, carry):
        i0, i1, i2, quad = (where[i, n] for i in range(4))
        for q in range(3):
            listed_ref[n, 3 + q] = facets[i0, i1, i2, quad + q]
        return carry

    lax.fori_loop(0, 64, hand_out, 0)
    for copy in sent:
        copy.wait_send()


def displace_and_list(candidates, points, shift, facets, vol):
    f32 = jnp.float32
    vmem = pl.BlockSpec(memory_space=pltpu.VMEM)
    table = pltpu.VMEM((2, 2 * NX, NY, NZ * 3, ROWS, LANES), f32)
    dma = pltpu.SemaphoreType.DMA
    return pl.pallas_call(
        gather_kernel,
        name="displace",
        out_shape=(
            jax.ShapeDtypeStruct((64, 6, ROWS, LANES), f32),
            jax.ShapeDtypeStruct((3, 4 * LANES), f32),
            jax.ShapeDtypeStruct((3, 4 * LANES), f32),
        ),
        in_specs=[pl.BlockSpec(memory_space=pltpu.HBM)] * 5,
        out_specs=(vmem, vmem, vmem),
        scratch_shapes=[
            table,
            table,
            pltpu.VMEM((8, LANES), f32),
            pltpu.VMEM((7, 8, LANES), f32),
            pltpu.VMEM((3, 8, LANES), f32),
            pltpu.VMEM((1, 8, LANES), f32),
            pltpu.VMEM((NX, 8, LANES), f32),
            pltpu.VMEM((4, 3, LANES, LANES), f32),
            pltpu.VMEM((4, 4, LANES, LANES), f32),
            pltpu.SMEM((4, 64), jnp.int32),
            pltpu.SMEM((16, 64), jnp.int32),
            pltpu.VMEM((3, 4 * LANES), f32),
            pltpu.VMEM((3, 4 * LANES), f32),
            pltpu.VMEM((3, 2, 4 * LANES), jnp.int32),
            pltpu.VMEM((3, 4 * LANES), f32),
            dma((5,)),
            dma((2, 2, 3, 8)),
            dma((2, 2, 3, 8)),
            dma((2, 2, 4)),
            dma((2, 2, 4)),
            dma((14,)),
            dma((14,)),
        ],
        compiler_params=pltpu.CompilerParams(
            collective_id=0, has_side_effects=True, vmem_limit_bytes=60 * 2**20
        ),
    )(candidates, points, shift, facets, vol)


def dot3(a, b):
    return a[0] * b[0] + a[1] * b[1] + a[2] * b[2]


def minus3(a, b):
    return [a[0] - b[0], a[1] - b[1], a[2] - b[2]]


def cross3(a, b):
    return [a[1] * b[2] - a[2] * b[1], a[2] * b[0] - a[0] * b[2], a[0] * b[1] - a[1] * b[0]]


def leaf_ids(x):
    lane = lax.broadcasted_iota(jnp.int32, (1, LANES), 1)
    z = (lane // 2) % NZ
    y = (lane // (2 * NZ)) % NY
    core = lane // (2 * NZ * NY)
    vol = ((y // 2) * NX + x) * 2 + core
    return (vol * 16 + z * 2 + y % 2) * 2 + lane % 2


margin = 1e-4
PG = 32


def facet_constants(a, b, c):
    sides = [dot3(d, d) for d in (minus3(b, a), minus3(c, b), minus3(a, c))]
    bc_long = (sides[1] > sides[0]) & (sides[1] >= sides[2])
    ca_long = (sides[2] > sides[0]) & (sides[2] > sides[1])

    def pick(p, q, r):
        return [jnp.where(bc_long, q[i], jnp.where(ca_long, r[i], p[i])) for i in range(3)]

    a, b, c = pick(a, b, c), pick(b, c, a), pick(c, a, b)
    ab, ac = minus3(b, a), minus3(c, a)
    normal = cross3(ab, ac)
    ab_len = jnp.sqrt(dot3(ab, ab))
    inv_ab = 1.0 / ab_len
    inv_n = lax.rsqrt(dot3(normal, normal))
    e1 = [q * inv_ab for q in ab]
    n = [q * inv_n for q in normal]
    e2 = cross3(n, e1)
    top = dot3(ac, e2)
    left = dot3(ac, e1)
    out = [*e1, -dot3(e1, a) - left, *e2, -dot3(e2, a), *n, -dot3(n, a)]
    for foot in (left, ab_len - left):
        leg = jnp.sqrt(foot * foot + top * top)
        inv_leg = 1.0 / leg
        out += [foot, top * inv_leg, foot * inv_leg, leg]
    return out


def facet_square(p, k):
    px, py, pz = p
    u = px * k[0] + py * k[1] + (pz * k[2] + k[3])
    v = px * k[4] + py * k[5] + (pz * k[6] + k[7])
    h = px * k[8] + py * k[9] + (pz * k[10] + k[11])
    on_left = u < 0.0
    foot, rise, run, leg = (jnp.where(on_left, k[12 + i], k[16 + i]) for i in range(4))
    past = jnp.abs(u) - foot
    s = past * rise + v * run
    t = v * rise - past * run
    below = v < 0.0
    across = jnp.where(below, past, s)
    across = jnp.maximum(across, 0.0)
    along = jnp.where(below, v, t - jnp.clip(t, 0.0, leg))
    return h * h + (across * across + along * along)


def weight(d):
    q = dot3(d, d) + smoothing
    inv = pl.reciprocal(q, approx=True)
    inv = inv * (2.0 - q * inv)
    return inv * inv


def as_columns(row):
    return jnp.transpose(jnp.broadcast_to(row, (LANES, LANES)))


def wall_kernel(cand_hbm, listed_hbm, target_hbm, flag_hbm, disp_hbm, disp_out, wall_ref,
                cols, moved, index, const, best, cand_ref, listed_ref, target_ref, flag_ref, in_sem):
    surf = lax.axis_index("surf")
    inputs = [
        pltpu.make_async_copy(cand_hbm, cand_ref, in_sem.at[0]),
        pltpu.make_async_copy(listed_hbm, listed_ref, in_sem.at[1]),
        pltpu.make_async_copy(target_hbm, target_ref, in_sem.at[2]),
        pltpu.make_async_copy(flag_hbm, flag_ref, in_sem.at[3]),
    ]
    hand_over = pltpu.make_async_copy(disp_hbm, disp_out, in_sem.at[4])
    for copy in inputs:
        copy.start()
    hand_over.start()
    for copy in inputs:
        copy.wait()

    def one_block(block, carry):
        row = surf * 4 + block
        lanes = pl.ds(pl.multiple_of(block * LANES, LANES), LANES)
        count = jnp.int32(0)
        for j in range(16):
            count += (cand_ref[j, row] >= 0).astype(jnp.int32)
        flags = flag_ref[pl.ds(row, 1), :]
        flagged = jnp.max(flags) > 0
        wall_ref[pl.ds(block, 1), :] = jnp.zeros((1, LANES), jnp.float32)

        @pl.when(flagged)
        def _():
            targets = [target_ref[pl.ds(c, 1), lanes] for c in range(3)]
            for c in range(3):
                cols[c] = as_columns(targets[c])

            def fetch(j, carry):
                here = pl.ds(j, 1)
                rows = block * 16 + j
                for half in range(2):
                    at = [listed_ref[rows, (2 * c) // 4, pl.ds((2 * c) % 4 + half, 1), :] for c in range(6)]
                    for c in range(3):
                        moved[c, half, here, :] = at[c] + at[3 + c]
                for k in range(3):
                    for quarter in range(4):
                        index[k, quarter, here, :] = listed_ref[rows, 3 + k, pl.ds(quarter, 1), :].astype(jnp.int32)
                return carry

            lax.fori_loop(0, 16, fetch, 0)
            axis = [jnp.zeros((16, LANES), jnp.float32)] * 3
            for quarter in range(4):
                corners = []
                for k in range(3):
                    where = index[k, quarter]
                    low = where % LANES
                    corner = []
                    for c in range(3):
                        lo = jnp.take_along_axis(moved[c, 0], low, axis=1, mode="promise_in_bounds")
                        hi = jnp.take_along_axis(moved[c, 1], low, axis=1, mode="promise_in_bounds")
                        corner.append(jnp.where(where < LANES, lo, hi))
                    corners.append(corner)
                values = facet_constants(*corners)
                for i, value in enumerate(values):
                    const[i, quarter] = value
                axis = [axis[c] + values[8 + c] for c in range(3)]
            best[...] = jnp.full((LANES, LANES), big_value, jnp.float32)

            def one_leaf(j):
                for quarter in range(4):
                    k = [jnp.broadcast_to(const[i, quarter, pl.ds(j, 1), :], (8, LANES)) for i in range(20)]
                    for g in range(16):
                        part = pl.ds(g * 8, 8)
                        p = [cols[c, part, :] for c in range(3)]
                        best[part, :] = jnp.minimum(best[part, :], facet_square(p, k))

            slot = lax.broadcasted_iota(jnp.int32, (16, 1), 0)
            middle = [
                jnp.sum(moved[c, 0] + moved[c, 1], axis=1, keepdims=True) * (1.0 / LEAF) for c in range(3)
            ]
            axis = [jnp.sum(q, axis=1, keepdims=True) for q in axis]
            unit = lax.rsqrt(jnp.maximum(dot3(axis, axis), 1e-12))
            axis = [q * unit for q in axis]

            def along_and_across(d):
                along = dot3(d, axis)
                across = [d[c] - along * axis[c] for c in range(3)]
                return jnp.abs(along), dot3(across, across)

            own = [[moved[c, half] - middle[c] for c in range(3)] for half in range(2)]
            spread = [dot3(d, d) for d in own]
            radius = jnp.sqrt(jnp.max(jnp.maximum(*spread), axis=1, keepdims=True)) + margin
            tall, wide = zip(*[along_and_across(d) for d in own])
            tall = jnp.max(jnp.maximum(*tall), axis=1, keepdims=True) + margin
            wide = jnp.sqrt(jnp.max(jnp.maximum(*wide), axis=1, keepdims=True)) + margin
            way = [targets[c] - middle[c] for c in range(3)]
            along, across = along_and_across(way)
            along = jnp.maximum(along - tall, 0.0)
            across = jnp.maximum(jnp.sqrt(across) - wide, 0.0)
            cylinder = along * along + across * across
            away = jnp.sqrt(dot3(way, way))
            valid = slot < count
            lower = jnp.maximum(away - radius, 0.0)
            lower = lower * lower
            lower = jnp.where(cylinder > lower, cylinder, lower)
            lower = jnp.where(valid & (flags == 1), lower, big_value)
            upper = jnp.where(valid, away + radius, 1e15)
            upper = jnp.min(upper * upper, axis=0, keepdims=True)
            rank = jnp.sum(jnp.where(flags == 1, away, 0.0), axis=1, keepdims=True)
            rank = jnp.where(valid, rank, big_value)

            def nearest_slot(rank):
                low = jnp.min(rank, axis=0, keepdims=True)
                return jnp.min(jnp.where(rank == low, slot, 15))

            def so_far():
                return jnp.min(jnp.transpose(best[...]), axis=0, keepdims=True)

            def wanted(open_):
                below = lower < jnp.minimum(so_far(), upper)
                hit = jnp.max(jnp.where(below, 1.0, 0.0), axis=1, keepdims=True)
                return jnp.where(open_, hit, 0.0)

            first = nearest_slot(rank)
            one_leaf(first)
            open_ = slot != first
            hit = wanted(open_)

            @pl.when(jnp.max(hit) > 0.0)
            def _():
                second = nearest_slot(jnp.where(hit > 0.0, rank, big_value))
                one_leaf(second)
                rest = wanted(open_ & (slot != second))
                bits = jnp.sum(jnp.where(rest > 0.0, lax.shift_left(jnp.ones_like(slot), slot), 0))

                def perhaps(j, carry):
                    @pl.when(lax.shift_right_logical(bits, j) % 2 == 1)
                    def _():
                        one_leaf(j)

                    return carry

                lax.fori_loop(0, count, perhaps, 0)

            wall_ref[pl.ds(block, 1), :] = jnp.where(flags == 1, jnp.sqrt(so_far()), 0.0)

        return carry

    lax.fori_loop(0, 4, one_block, 0)
    hand_over.wait()


def wall(candidates, listed, target, flags, displacement):
    f32 = jnp.float32
    hbm = pl.BlockSpec(memory_space=pltpu.HBM)
    return pl.pallas_call(
        wall_kernel,
        name="wall",
        out_shape=(
            jax.ShapeDtypeStruct((3, 4 * LANES), f32),
            jax.ShapeDtypeStruct((4, LANES), f32),
        ),
        in_specs=[hbm] * 5,
        out_specs=(hbm, pl.BlockSpec(memory_space=pltpu.VMEM)),
        scratch_shapes=[
            pltpu.VMEM((3, LANES, LANES), f32),
            pltpu.VMEM((3, 2, 16, LANES), f32),
            pltpu.VMEM((3, 4, 16, LANES), jnp.int32),
            pltpu.VMEM((20, 4, 16, LANES), f32),
            pltpu.VMEM((LANES, LANES), f32),
            pltpu.SMEM((16, 64), jnp.int32),
            pltpu.VMEM((64, 6, ROWS, LANES), f32),
            pltpu.VMEM((3, 4 * LANES), f32),
            pltpu.VMEM((64, LANES), jnp.int32),
            pltpu.SemaphoreType.DMA((5,)),
        ],
        compiler_params=pltpu.CompilerParams(vmem_limit_bytes=60 * 2**20),
    )(candidates, listed, target, flags, displacement)


def body(surface_points, surface_shift, facet_nodes, volume_points, near_wall, candidates):
    candidates = candidates.T
    listed, displacement, target = displace_and_list(
        candidates, surface_points, surface_shift, jnp.transpose(facet_nodes, (1, 0, 2)), volume_points
    )
    displacement, distance = wall(candidates, listed, target, near_wall.reshape(-1, LANES), displacement)
    return displacement, distance.reshape(-1)


def solution(mesh):
    placed = (
        P(None, ("vol", "surf")),
        P(None, ("vol", "surf")),
        P(("vol", "surf"), None, None),
        P(None, "vol"),
        P("vol"),
        P("vol", None),
    )
    return jax.shard_map(
        body,
        mesh=mesh,
        in_specs=placed,
        out_specs=(P(None, ("vol", "surf")), P(("vol", "surf"))),
        check_vma=False,
    )
```

```python
import jax
import jax.numpy as jnp
from jax import lax
from jax.experimental import pallas as pl
from jax.experimental.pallas import tpu as pltpu
from jax.sharding import PartitionSpec as P

MESH = pl.DeviceIdType.MESH
smoothing = 0.01
big_value = 1e30

NX, NY, NZ = 4, 4, 8
SIZES = {"x": NX, "y": NY, "z": NZ}
LEAF = 256
CHIPS = NX * NY * NZ
LANES = 128
ROWS = 4


def coords_of(vol, surf):
    return {
        "x": (vol // 2) % NX,
        "y": (vol // (2 * NX)) * 2 + surf % 2,
        "z": surf // 2,
        "c": vol % 2,
    }


def mesh_id(c):
    return ((c["y"] // 2) * NX + c["x"]) * 2 + c["c"], c["z"] * 2 + c["y"] % 2


def shifted(c, axis, k):
    n = SIZES[axis]
    return {**c, axis: lax.rem(c[axis] + (k % n), n)}


WAYS = (("z", "y", "x"), ("z", "x", "y"))
NEAR_FIRST = {4: (1, 3, 2), 8: (1, 7, 2, 6, 3, 5, 4)}


def span(table, part, phase, c):
    if phase == 0:
        return table.at[:, c["c"] * NX + c["x"], c["y"], pl.ds(c["z"] * 3, 3)]
    if phase == 1:
        return table.at[part, c["c"] * NX + c["x"], c["y"]]
    if part == 0:
        return table.at[0, c["c"] * NX + c["x"]]
    return table.at[1, pl.ds(c["c"] * NX, NX), c["y"]]


def half_span(table, part, c, half):
    if part == 0:
        return table.at[0, c["c"] * NX + c["x"], pl.ds(half * 2, 2)]
    return table.at[1, pl.ds(c["c"] * NX + half * 2, 2), c["y"]]


def leaf_index(leaf):
    right = lax.shift_right_logical
    surf, vol = right(leaf, 1) & 15, right(leaf, 5)
    y = (right(vol, 3) << 1) | (surf & 1)
    return leaf & 1, ((vol & 1) << 2) | (right(vol, 1) & 3), y, right(surf, 1) * 3


def gather_kernel(cand_hbm, points_hbm, shift_hbm, facets_hbm, vol_hbm, listed_ref, disp_ref, target_ref,
                  nodes, facets, mom_own, mom_z, mom_y, mom_c, moments, cols, acc, where,
                  cand_ref, points_ref, shift_ref, facets_ref, vol_ref,
                  in_sem, send_sem, recv_sem, core_send, core_recv, mom_send, mom_recv):
    surf = lax.axis_index("surf")
    me = coords_of(lax.axis_index("vol"), surf)
    sibling = {**me, "c": 1 - me["c"]}
    partners = [sibling]
    for axis, n in SIZES.items():
        partners += [shifted(me, axis, k) for k in range(1, n)]
    barrier = pltpu.get_barrier_semaphore()
    for other in partners:
        pl.semaphore_signal(barrier, inc=1, device_id=mesh_id(other), device_id_type=MESH)
    share = pl.ds(pl.multiple_of(surf * 4 * LANES, 4 * LANES), 4 * LANES)
    inputs = [
        pltpu.make_async_copy(points_hbm, points_ref, in_sem.at[0]),
        pltpu.make_async_copy(shift_hbm, shift_ref, in_sem.at[1]),
        pltpu.make_async_copy(facets_hbm, facets_ref, in_sem.at[2]),
        pltpu.make_async_copy(vol_hbm.at[:, share], vol_ref, in_sem.at[3]),
        pltpu.make_async_copy(cand_hbm, cand_ref, in_sem.at[4]),
    ]
    for copy in inputs:
        copy.start()
    for copy in inputs:
        copy.wait()

    for leaf in range(2):
        own = (leaf, me["c"] * NX + me["x"], me["y"])
        for half in range(2):
            lanes = pl.ds(leaf * LEAF + half * LANES, LANES)
            for c in range(3):
                nodes[(*own, me["z"] * 3 + (2 * c) // 4, pl.ds((2 * c) % 4 + half, 1), slice(None))] = (
                    points_ref[pl.ds(c, 1), lanes]
                )
                nodes[(*own, me["z"] * 3 + (6 + 2 * c) // 4, pl.ds((6 + 2 * c) % 4 + half, 1), slice(None))] = (
                    shift_ref[pl.ds(c, 1), lanes]
                )
        for quarter in range(4):
            lanes = pl.ds(quarter * LANES, LANES)
            for k in range(3):
                facets[(*own, me["z"] * 3 + k, pl.ds(quarter, 1), slice(None))] = (
                    facets_ref[k, pl.ds(leaf, 1), lanes].astype(jnp.float32)
                )
    lane = lax.broadcasted_iota(jnp.int32, (3, LANES), 1)
    my_lane = ((me["c"] * NY + me["y"]) * NZ + me["z"]) * 2
    for row, ref in ((0, points_ref), (3, shift_ref)):
        tile = jnp.zeros((3, LANES), jnp.float32)
        for leaf in range(2):
            mean = jnp.sum(ref[:, pl.ds(leaf * LEAF, LEAF)], axis=1, keepdims=True) * (1.0 / LEAF)
            tile = jnp.where(lane == my_lane + leaf, mean, tile)
        mom_own[pl.ds(row, 3), :] = tile
    mom_own[pl.ds(6, 2), :] = jnp.zeros((2, LANES), jnp.float32)
    pl.semaphore_wait(barrier, len(partners))

    sent = []

    def remote(src, dst, to, s_sem, r_sem):
        return pltpu.make_async_remote_copy(
            src_ref=src, dst_ref=dst, send_sem=s_sem, recv_sem=r_sem,
            device_id=mesh_id(to), device_id_type=MESH,
        )

    def start(copy):
        copy.start()
        sent.append(copy)

    tables = (nodes, facets)

    def sems(which, part, phase, k):
        slot = (part, phase, k)
        return send_sem.at[(which, *slot)], recv_sem.at[(which, *slot)]

    def issue(which, part, phase):
        axis = WAYS[part][phase]
        mine = span(tables[which], part, phase, me)
        if phase == 2:
            for turn in range(2):
                for k in (1, 3):
                    piece = half_span(tables[which], part, me, (k // 2) ^ turn)
                    start(remote(piece, piece, shifted(me, axis, k), *sems(which, part, 2, k + 4 * turn - 1)))
            return
        for k in NEAR_FIRST[SIZES[axis]]:
            start(remote(mine, mine, shifted(me, axis, k), *sems(which, part, phase, k)))

    def collect(which, part, phase):
        axis = WAYS[part][phase]
        for k in NEAR_FIRST[SIZES[axis]]:
            frm = shifted(me, axis, -k)
            theirs = span(tables[which], part, phase, frm)
            remote(theirs, theirs, frm, *sems(which, part, phase, k)).wait_recv()

    def collect_turn(which, part, k, turn):
        axis = WAYS[part][2]
        frm = shifted(me, axis, -k)
        piece = half_span(tables[which], part, frm, (k // 2) ^ turn)
        remote(piece, piece, frm, *sems(which, part, 2, k + 4 * turn - 1)).wait_recv()

    def forward(which, part, k):
        axis = WAYS[part][2]
        piece = half_span(tables[which], part, shifted(me, axis, -k), k // 2)
        start(remote(piece, piece, shifted(me, axis, k), *sems(which, part, 2, k)))

    def pass_on(which):
        for k in (1, 3):
            for part in range(2):
                collect_turn(which, part, k, 0)
                forward(which, part, k)

    def take_rest(which):
        for k in (1, 3):
            for part in range(2):
                collect_turn(which, part, k, 1)
                to_sibling(which, part, k)

    def collect_halves(which, part):
        axis = WAYS[part][2]
        for k in (1, 3):
            piece = half_span(tables[which], part, shifted(me, axis, 2), k // 2)
            remote(piece, piece, shifted(me, axis, -k), *sems(which, part, 2, k)).wait_recv()

    def to_sibling(which, part, k):
        mine = span(tables[which], part, 2, shifted(me, WAYS[part][2], -k))
        start(remote(mine, mine, sibling, core_send.at[which, part, k], core_recv.at[which, part, k]))

    def from_sibling(which, part, k):
        theirs = span(tables[which], part, 2, shifted(sibling, WAYS[part][2], -k))
        remote(theirs, theirs, sibling, core_send.at[which, part, k], core_recv.at[which, part, k]).wait_recv()

    def mom_copies(dst, others, slot0):
        return [
            remote(mom_own, dst.at[k], other, mom_send.at[slot0 + k], mom_recv.at[slot0 + k])
            for k, other in enumerate(others)
        ]

    def mom_sum(copies, arrived):
        total = mom_own[...]
        for k, copy in enumerate(copies):
            copy.wait()
            total = total + arrived[k]
        mom_own[...] = total

    issue(0, 0, 0)
    mom = mom_copies(mom_z, [shifted(me, "z", k) for k in range(1, NZ)], 0)
    for copy in mom:
        copy.start()
    collect(0, 0, 0)
    issue(0, 0, 1)
    issue(0, 1, 1)
    issue(1, 0, 0)
    mom_sum(mom, mom_z)
    mom = mom_copies(mom_y, [shifted(me, "y", k) for k in range(1, NY)], 7)
    for copy in mom:
        copy.start()
    for part in range(2):
        collect(0, part, 1)
        issue(0, part, 2)
    mom_sum(mom, mom_y)
    mom = mom_copies(mom_c, [sibling], 10)
    mom[0].start()
    for part in range(2):
        to_sibling(0, part, 0)

    def locate(n, carry):
        at = leaf_index(jnp.maximum(cand_ref[n % 16, surf * 4 + n // 16], 0))
        for i in range(4):
            where[i, n] = at[i]
        return carry

    lax.fori_loop(0, 64, locate, 0)
    mom_sum(mom, mom_c)
    moments[pl.ds(me["x"], 1)] = mom_own[...][None]
    for k in range(1, NX):
        start(remote(mom_own, moments.at[me["x"]], shifted(me, "x", k), mom_send.at[10 + k], mom_recv.at[10 + k]))
    collect(1, 0, 0)
    issue(1, 0, 1)
    issue(1, 1, 1)
    for block in range(4):
        for c in range(3):
            cols[block, c] = as_columns(vol_ref[pl.ds(c, 1), pl.ds(block * LANES, LANES)])
    pass_on(0)
    for k in range(1, NX):
        frm = shifted(me, "x", -k)
        remote(mom_own, moments.at[frm["x"]], frm, mom_send.at[10 + k], mom_recv.at[10 + k]).wait_recv()

    def far(block, carry):
        row = surf * 4 + block
        centers = []
        for x in range(NX):
            ids = leaf_ids(x)
            listed = ids == cand_ref[0, row]
            for j in range(1, 16):
                listed = listed | (ids == cand_ref[j, row])
            centers.append(jnp.where(listed, 0.0, float(LEAF)))
        for g in range(LANES // PG):
            part = pl.ds(g * PG, PG)
            p = [cols[block, c, part, :] for c in range(3)]
            sums = [None] * 4
            for x in range(NX):
                m = moments[x]
                w = weight([m[c:c + 1] - p[c] for c in range(3)]) * centers[x]
                terms = [w * m[3 + c:4 + c] for c in range(3)] + [w]
                sums = terms if x == 0 else [a + b for a, b in zip(sums, terms)]
            for c in range(4):
                acc[block, c, part, :] = sums[c]
        return carry

    lax.fori_loop(0, 4, far, 0)
    take_rest(0)
    for part in range(2):
        collect(1, part, 1)
        issue(1, part, 2)
    for part in range(2):
        collect_halves(0, part)
        to_sibling(0, part, 2)
    for part in range(2):
        to_sibling(1, part, 0)
        for k in range(4):
            from_sibling(0, part, k)

    def displace(block):
        def near(j, carry):
            n = block * 16 + j
            i0, i1, i2, quad = (where[i, n] for i in range(4))
            push_off = jnp.where(cand_ref[j, surf * 4 + block] >= 0, 0.0, 1e15)
            at = [
                [nodes[i0, i1, i2, quad + (2 * c) // 4, pl.ds((2 * c) % 4 + half, 1), :] for c in range(6)]
                for half in range(2)
            ]
            for half in range(2):
                at[half][0] = at[half][0] + push_off
            for g in range(LANES // PG):
                part = pl.ds(g * PG, PG)
                p = [cols[block, c, part, :] for c in range(3)]
                w = [weight([at[half][c] - p[c] for c in range(3)]) for half in range(2)]
                for c in range(3):
                    acc[block, c, part, :] += w[0] * at[0][3 + c] + w[1] * at[1][3 + c]
                acc[block, 3, part, :] += w[0] + w[1]
            for q in range(3):
                listed_ref[n, q] = nodes[i0, i1, i2, quad + q]
            return carry

        lax.fori_loop(0, 16, near, 0)
        out_lanes = pl.ds(block * LANES, LANES)
        total = [jnp.sum(jnp.transpose(acc[block, c]), axis=0, keepdims=True) for c in range(4)]
        inv = 1.0 / total[3]
        for c in range(3):
            disp = total[c] * inv
            disp_ref[pl.ds(c, 1), out_lanes] = disp
            target_ref[pl.ds(c, 1), out_lanes] = vol_ref[pl.ds(c, 1), out_lanes] + disp

    displace(0)
    pass_on(1)
    take_rest(1)
    displace(1)
    displace(2)
    for part in range(2):
        collect_halves(1, part)
        to_sibling(1, part, 2)
    displace(3)
    for part in range(2):
        for k in range(4):
            from_sibling(1, part, k)

    def hand_out(n, carry):
        i0, i1, i2, quad = (where[i, n] for i in range(4))
        for q in range(3):
            listed_ref[n, 3 + q] = facets[i0, i1, i2, quad + q]
        return carry

    lax.fori_loop(0, 64, hand_out, 0)
    for copy in sent:
        copy.wait_send()


def displace_and_list(candidates, points, shift, facets, vol):
    f32 = jnp.float32
    vmem = pl.BlockSpec(memory_space=pltpu.VMEM)
    table = pltpu.VMEM((2, 2 * NX, NY, NZ * 3, ROWS, LANES), f32)
    dma = pltpu.SemaphoreType.DMA
    return pl.pallas_call(
        gather_kernel,
        name="displace",
        out_shape=(
            jax.ShapeDtypeStruct((64, 6, ROWS, LANES), f32),
            jax.ShapeDtypeStruct((3, 4 * LANES), f32),
            jax.ShapeDtypeStruct((3, 4 * LANES), f32),
        ),
        in_specs=[pl.BlockSpec(memory_space=pltpu.HBM)] * 5,
        out_specs=(vmem, vmem, vmem),
        scratch_shapes=[
            table,
            table,
            pltpu.VMEM((8, LANES), f32),
            pltpu.VMEM((7, 8, LANES), f32),
            pltpu.VMEM((3, 8, LANES), f32),
            pltpu.VMEM((1, 8, LANES), f32),
            pltpu.VMEM((NX, 8, LANES), f32),
            pltpu.VMEM((4, 3, LANES, LANES), f32),
            pltpu.VMEM((4, 4, LANES, LANES), f32),
            pltpu.SMEM((4, 64), jnp.int32),
            pltpu.SMEM((16, 64), jnp.int32),
            pltpu.VMEM((3, 4 * LANES), f32),
            pltpu.VMEM((3, 4 * LANES), f32),
            pltpu.VMEM((3, 2, 4 * LANES), jnp.int32),
            pltpu.VMEM((3, 4 * LANES), f32),
            dma((5,)),
            dma((2, 2, 3, 8)),
            dma((2, 2, 3, 8)),
            dma((2, 2, 4)),
            dma((2, 2, 4)),
            dma((14,)),
            dma((14,)),
        ],
        compiler_params=pltpu.CompilerParams(
            collective_id=0, has_side_effects=True, vmem_limit_bytes=60 * 2**20
        ),
    )(candidates, points, shift, facets, vol)


def dot3(a, b):
    return a[0] * b[0] + a[1] * b[1] + a[2] * b[2]


def minus3(a, b):
    return [a[0] - b[0], a[1] - b[1], a[2] - b[2]]


def cross3(a, b):
    return [a[1] * b[2] - a[2] * b[1], a[2] * b[0] - a[0] * b[2], a[0] * b[1] - a[1] * b[0]]


def leaf_ids(x):
    lane = lax.broadcasted_iota(jnp.int32, (1, LANES), 1)
    z = (lane // 2) % NZ
    y = (lane // (2 * NZ)) % NY
    core = lane // (2 * NZ * NY)
    vol = ((y // 2) * NX + x) * 2 + core
    return (vol * 16 + z * 2 + y % 2) * 2 + lane % 2


margin = 1e-4
PG = 32


def facet_constants(a, b, c):
    sides = [dot3(d, d) for d in (minus3(b, a), minus3(c, b), minus3(a, c))]
    bc_long = (sides[1] > sides[0]) & (sides[1] >= sides[2])
    ca_long = (sides[2] > sides[0]) & (sides[2] > sides[1])

    def pick(p, q, r):
        return [jnp.where(bc_long, q[i], jnp.where(ca_long, r[i], p[i])) for i in range(3)]

    a, b, c = pick(a, b, c), pick(b, c, a), pick(c, a, b)
    ab, ac = minus3(b, a), minus3(c, a)
    normal = cross3(ab, ac)
    ab_len = jnp.sqrt(dot3(ab, ab))
    inv_ab = 1.0 / ab_len
    inv_n = lax.rsqrt(dot3(normal, normal))
    e1 = [q * inv_ab for q in ab]
    n = [q * inv_n for q in normal]
    e2 = cross3(n, e1)
    top = dot3(ac, e2)
    left = dot3(ac, e1)
    out = [*e1, -dot3(e1, a) - left, *e2, -dot3(e2, a), *n, -dot3(n, a)]
    for foot in (left, ab_len - left):
        leg = jnp.sqrt(foot * foot + top * top)
        inv_leg = 1.0 / leg
        out += [foot, top * inv_leg, foot * inv_leg, leg]
    return out


def facet_square(p, k):
    px, py, pz = p
    u = px * k[0] + py * k[1] + (pz * k[2] + k[3])
    v = px * k[4] + py * k[5] + (pz * k[6] + k[7])
    h = px * k[8] + py * k[9] + (pz * k[10] + k[11])
    on_left = u < 0.0
    foot, rise, run, leg = (jnp.where(on_left, k[12 + i], k[16 + i]) for i in range(4))
    past = jnp.abs(u) - foot
    s = past * rise + v * run
    t = v * rise - past * run
    below = v < 0.0
    across = jnp.where(below, past, s)
    across = jnp.maximum(across, 0.0)
    along = jnp.where(below, v, t - jnp.clip(t, 0.0, leg))
    return h * h + (across * across + along * along)


def weight(d):
    q = dot3(d, d) + smoothing
    inv = pl.reciprocal(q, approx=True)
    inv = inv * (2.0 - q * inv)
    return inv * inv


def as_columns(row):
    return jnp.transpose(jnp.broadcast_to(row, (LANES, LANES)))


def wall_kernel(cand_hbm, listed_hbm, target_hbm, flag_hbm, disp_hbm, disp_out, wall_ref,
                cols, moved, index, const, best, cand_ref, listed_ref, target_ref, flag_ref, in_sem):
    surf = lax.axis_index("surf")
    inputs = [
        pltpu.make_async_copy(cand_hbm, cand_ref, in_sem.at[0]),
        pltpu.make_async_copy(listed_hbm, listed_ref, in_sem.at[1]),
        pltpu.make_async_copy(target_hbm, target_ref, in_sem.at[2]),
        pltpu.make_async_copy(flag_hbm, flag_ref, in_sem.at[3]),
    ]
    hand_over = pltpu.make_async_copy(disp_hbm, disp_out, in_sem.at[4])
    for copy in inputs:
        copy.start()
    hand_over.start()
    for copy in inputs:
        copy.wait()

    def one_block(block, carry):
        row = surf * 4 + block
        lanes = pl.ds(pl.multiple_of(block * LANES, LANES), LANES)
        count = jnp.int32(0)
        for j in range(16):
            count += (cand_ref[j, row] >= 0).astype(jnp.int32)
        flags = flag_ref[pl.ds(row, 1), :]
        flagged = jnp.max(flags) > 0
        wall_ref[pl.ds(block, 1), :] = jnp.zeros((1, LANES), jnp.float32)

        @pl.when(flagged)
        def _():
            targets = [target_ref[pl.ds(c, 1), lanes] for c in range(3)]
            for c in range(3):
                cols[c] = as_columns(targets[c])

            def fetch(j, carry):
                here = pl.ds(j, 1)
                rows = block * 16 + j
                for half in range(2):
                    at = [listed_ref[rows, (2 * c) // 4, pl.ds((2 * c) % 4 + half, 1), :] for c in range(6)]
                    for c in range(3):
                        moved[c, half, here, :] = at[c] + at[3 + c]
                for k in range(3):
                    for quarter in range(4):
                        index[k, quarter, here, :] = listed_ref[rows, 3 + k, pl.ds(quarter, 1), :].astype(jnp.int32)
                return carry

            lax.fori_loop(0, 16, fetch, 0)
            axis = [jnp.zeros((16, LANES), jnp.float32)] * 3
            for quarter in range(4):
                corners = []
                for k in range(3):
                    where = index[k, quarter]
                    low = where % LANES
                    corner = []
                    for c in range(3):
                        lo = jnp.take_along_axis(moved[c, 0], low, axis=1, mode="promise_in_bounds")
                        hi = jnp.take_along_axis(moved[c, 1], low, axis=1, mode="promise_in_bounds")
                        corner.append(jnp.where(where < LANES, lo, hi))
                    corners.append(corner)
                values = facet_constants(*corners)
                for i, value in enumerate(values):
                    const[i, quarter] = value
                axis = [axis[c] + values[8 + c] for c in range(3)]
            best[...] = jnp.full((LANES, LANES), big_value, jnp.float32)

            def one_leaf(j, groups=range(16)):
                for quarter in range(4):
                    k = [jnp.broadcast_to(const[i, quarter, pl.ds(j, 1), :], (8, LANES)) for i in range(20)]
                    for g in groups:
                        part = pl.ds(g * 8, 8)
                        p = [cols[c, part, :] for c in range(3)]
                        best[part, :] = jnp.minimum(best[part, :], facet_square(p, k))

            slot = lax.broadcasted_iota(jnp.int32, (16, 1), 0)
            middle = [
                jnp.sum(moved[c, 0] + moved[c, 1], axis=1, keepdims=True) * (1.0 / LEAF) for c in range(3)
            ]
            axis = [jnp.sum(q, axis=1, keepdims=True) for q in axis]
            unit = lax.rsqrt(jnp.maximum(dot3(axis, axis), 1e-12))
            axis = [q * unit for q in axis]

            def along_and_across(d):
                along = dot3(d, axis)
                across = [d[c] - along * axis[c] for c in range(3)]
                return jnp.abs(along), dot3(across, across)

            own = [[moved[c, half] - middle[c] for c in range(3)] for half in range(2)]
            spread = [dot3(d, d) for d in own]
            radius = jnp.sqrt(jnp.max(jnp.maximum(*spread), axis=1, keepdims=True)) + margin
            tall, wide = zip(*[along_and_across(d) for d in own])
            tall = jnp.max(jnp.maximum(*tall), axis=1, keepdims=True) + margin
            wide = jnp.sqrt(jnp.max(jnp.maximum(*wide), axis=1, keepdims=True)) + margin
            way = [targets[c] - middle[c] for c in range(3)]
            along, across = along_and_across(way)
            along = jnp.maximum(along - tall, 0.0)
            across = jnp.maximum(jnp.sqrt(across) - wide, 0.0)
            cylinder = along * along + across * across
            away = jnp.sqrt(dot3(way, way))
            valid = slot < count
            lower = jnp.maximum(away - radius, 0.0)
            lower = lower * lower
            lower = jnp.where(cylinder > lower, cylinder, lower)
            lower = jnp.where(valid & (flags == 1), lower, big_value)
            upper = jnp.where(valid, away + radius, 1e15)
            upper = jnp.min(upper * upper, axis=0, keepdims=True)
            rank = jnp.sum(jnp.where(flags == 1, away, 0.0), axis=1, keepdims=True)
            rank = jnp.where(valid, rank, big_value)

            def nearest_slot(rank):
                low = jnp.min(rank, axis=0, keepdims=True)
                return jnp.min(jnp.where(rank == low, slot, 15))

            def so_far():
                return jnp.min(jnp.transpose(best[...]), axis=0, keepdims=True)

            def below():
                return jnp.where(lower < jnp.minimum(so_far(), upper), 1.0, 0.0)

            def wanted(open_, found):
                return jnp.where(open_, jnp.max(found, axis=1, keepdims=True), 0.0)

            first = nearest_slot(rank)
            one_leaf(first)
            open_ = slot != first
            hit = wanted(open_, below())

            @pl.when(jnp.max(hit) > 0.0)
            def _():
                second = nearest_slot(jnp.where(hit > 0.0, rank, big_value))
                one_leaf(second)
                found = below()
                lane_group = lax.broadcasted_iota(jnp.int32, (1, LANES), 1) // 32
                bits = []
                for quad in range(4):
                    rest = wanted(open_ & (slot != second), jnp.where(lane_group == quad, found, 0.0))
                    bits.append(jnp.sum(jnp.where(rest > 0.0, lax.shift_left(jnp.ones_like(slot), slot), 0)))

                def perhaps(j, carry):
                    for quad in range(4):
                        @pl.when(lax.shift_right_logical(bits[quad], j) % 2 == 1)
                        def _():
                            one_leaf(j, range(4 * quad, 4 * quad + 4))

                    return carry

                lax.fori_loop(0, count, perhaps, 0)

            wall_ref[pl.ds(block, 1), :] = jnp.where(flags == 1, jnp.sqrt(so_far()), 0.0)

        return carry

    lax.fori_loop(0, 4, one_block, 0)
    hand_over.wait()


def wall(candidates, listed, target, flags, displacement):
    f32 = jnp.float32
    hbm = pl.BlockSpec(memory_space=pltpu.HBM)
    return pl.pallas_call(
        wall_kernel,
        name="wall",
        out_shape=(
            jax.ShapeDtypeStruct((3, 4 * LANES), f32),
            jax.ShapeDtypeStruct((4, LANES), f32),
        ),
        in_specs=[hbm] * 5,
        out_specs=(hbm, pl.BlockSpec(memory_space=pltpu.VMEM)),
        scratch_shapes=[
            pltpu.VMEM((3, LANES, LANES), f32),
            pltpu.VMEM((3, 2, 16, LANES), f32),
            pltpu.VMEM((3, 4, 16, LANES), jnp.int32),
            pltpu.VMEM((20, 4, 16, LANES), f32),
            pltpu.VMEM((LANES, LANES), f32),
            pltpu.SMEM((16, 64), jnp.int32),
            pltpu.VMEM((64, 6, ROWS, LANES), f32),
            pltpu.VMEM((3, 4 * LANES), f32),
            pltpu.VMEM((64, LANES), jnp.int32),
            pltpu.SemaphoreType.DMA((5,)),
        ],
        compiler_params=pltpu.CompilerParams(vmem_limit_bytes=60 * 2**20),
    )(candidates, listed, target, flags, displacement)


def body(surface_points, surface_shift, facet_nodes, volume_points, near_wall, candidates):
    candidates = candidates.T
    listed, displacement, target = displace_and_list(
        candidates, surface_points, surface_shift, jnp.transpose(facet_nodes, (1, 0, 2)), volume_points
    )
    displacement, distance = wall(candidates, listed, target, near_wall.reshape(-1, LANES), displacement)
    return displacement, distance.reshape(-1)


def solution(mesh):
    placed = (
        P(None, ("vol", "surf")),
        P(None, ("vol", "surf")),
        P(("vol", "surf"), None, None),
        P(None, "vol"),
        P("vol"),
        P("vol", None),
    )
    return jax.shard_map(
        body,
        mesh=mesh,
        in_specs=placed,
        out_specs=(P(None, ("vol", "surf")), P(("vol", "surf"))),
        check_vma=False,
    )
```
